32 devices in a mesh: groups: 2 (over y), tensor: 4 (over x, core), store: 4 (over z).
Axes of the slice: x: 2, y: 2, z: 4, core: 2. Of those that a mesh axis runs over, the one named last changes fastest.
Arguments:
- normed_input: bfloat16 [8192, 8192], P(('groups', 'store')), parts along dimension 0, may hold values from -6 to 6
- query_weight: bfloat16 [8192, 1024], P(None, 'tensor'), may hold values from -0.0625 to 0.0625
- down_factors: bfloat16 [64, 8192, 64], P('store', 'tensor'), may hold values from -0.0625 to 0.0625
- up_factors: bfloat16 [64, 64, 1024], P('store', None, 'tensor'), may hold values from -0.75 to 0.75
- adapter_per_block: int32 [64], P(('groups', 'store')), parts along dimension 0, may hold values from 0 to 63
- key_value_cache: bfloat16 [8192, 1, 256], P(('groups', 'store')), parts along dimension 0, may hold values from -70 to 70
- token_segment: int32 [8192], P(('groups', 'store')), parts along dimension 0, may hold values from 0 to 3, never falling along the last dimension, each value on 1 to 2048 neighbouring positions
Outputs:
- attended: bfloat16 [8192, 1024], P(('groups', 'store'), 'tensor'), parts along dimension 0
The draws below stay inside these ranges and needn't reach their ends.
There are 2 independent parts, one for each index of `groups`. The reference program is written for one: setup_inputs(seed, part) draws one part's arguments, and reference() takes and returns one part's arrays. A program takes and returns all parts, laid end to end along the dimension named above; an argument that names none is the same for every part. Nothing has to cross between parts.
Inputs may be any that keep to these rules, and one draw needn't show every extreme that they name: `token_segment`: segment numbers never fall along the tokens; a segment holds at most 2048 tokens.
All inputs are finite; a program needn't handle non-finite values.
Results may differ from the reference program's by a relative error of at most 0.005.
The reference program's roundings to bfloat16 on the way count: a program that leaves them out, or rounds other values in their place, can miss the bound.
Values may be sent and summed in bfloat16 or wider, within the bound.
No kernel may reach another device: no remote copies, remote signals or barrier semaphores. Data moves between devices by JAX's collectives and lax.ppermute only.
A program may use at most 256 MiB of HBM per device.

```python
import math
import jax
import jax.numpy as jnp
import numpy as np
from jax import lax

MODEL_WIDTH = 8192
HEAD_SIZE = 128
GROUP = 8
ADAPTER_RANK = 64
ADAPTER_COUNT = 64
BLOCK = 128
SEGMENTS = 4
QUERY_HEADS = 8
KVH = 1
TOKENS = 4096
BLOCKS = 32
SEG_MOST = 2048


def draw_key_value_cache(key, part):
    key = jax.random.fold_in(key, 7)
    noise_key = jax.random.fold_in(key, 0)
    values_drawn = jnp.clip(jax.random.normal(noise_key, (TOKENS, KVH, 2 * HEAD_SIZE), jnp.float32), -6.0, 6.0)
    return values_drawn.astype(jnp.bfloat16)


def with_ends(result, rng, smallest, largest):
    longest = result.shape.index(max(result.shape))
    spots = []
    for shift in (0, 1):
        where = [jax.random.randint(jax.random.fold_in(rng, axis), (), 0, length) for axis, length in enumerate(result.shape)]
        where[longest] = (where[longest] + shift) % result.shape[longest]
        spots.append(tuple(where))
    return result.at[spots[0]].set(smallest).at[spots[1]].set(largest)


def levels(rng, extent, pieces, least, top_value):
    factor_of, own = 1.0, jax.random.fold_in(rng, 6)
    for position, shards_of in pieces:
        heights = jnp.exp(jax.random.uniform(jax.random.fold_in(own, position), (shards_of,), jnp.float32, least / len(pieces), top_value / len(pieces)))
        factor_of = factor_of * jnp.repeat(heights, extent[position] // shards_of).reshape([-1 if axis == position else 1 for axis in range(len(extent))])
    return factor_of


def cumulative_ranks(count, lean):
    portions = [(1 << 20) // math.isqrt(grade ** lean) + 1 for grade in range(1, count + 1)]
    spread = 1 + sum(portions) // (1 << 30)
    return np.cumsum(np.array([max(1, weight // spread) for weight in portions]))


def ranked(key, dims, number_of, skew):
    grid = cumulative_ranks(number_of, skew)
    lot = jax.random.randint(jax.random.fold_in(key, 1), dims, 0, int(grid[number_of - 1]))
    standing = jnp.searchsorted(jnp.asarray(grid, jnp.int32), lot, side="right")
    return jax.random.permutation(jax.random.fold_in(key, 2), number_of)[standing].astype(jnp.int32)


def length_profile(count, total, most, skew):
    portions = [(1 << 20) // math.isqrt(grade ** skew) + 1 for grade in range(2, count + 1)]
    spare, counts = total - most - (count - 1), [1] * (count - 1)
    while spare > 0:
        movable = [i for i in range(count - 1) if counts[i] < most]
        mass, left = sum([portions[i] for i in movable]), spare
        for i in movable:
            extra = min(most - counts[i], max(1, left * portions[i] // mass), spare)
            counts[i] = counts[i] + extra
            spare = spare - extra
    return np.array([most] + counts)


def uneven_parts(rng, number_of, total, bound, skew):
    if number_of == 2:
        one = jax.random.randint(rng, (), max(1, total - bound), min(bound, total - 1) + 1)
        return jnp.stack([one, total - one])
    sizes = jnp.asarray(length_profile(number_of, total, bound, skew), jnp.int32)
    twos = (number_of - 1) // 2
    donor, taker = sizes[1:1 + 2 * twos:2], sizes[2:2 + 2 * twos:2]
    room = jnp.minimum(donor - 1, bound - taker)
    moved = jax.random.randint(jax.random.fold_in(rng, 1), (twos,), 0, 1 << 20) % (room + 1)
    sizes = sizes.at[1:1 + 2 * twos:2].set(donor - moved).at[2:2 + 2 * twos:2].set(taker + moved)
    return sizes[jax.random.permutation(jax.random.fold_in(rng, 2), number_of)]


def gaussian(rng, extent, scale, reach, cuts=(), kind=jnp.bfloat16):
    result = jax.random.normal(rng, extent, jnp.float32) * scale
    if len(cuts) > 0:
        result = levels(rng, extent, cuts, -0.22, 0.18) * result
    return jnp.clip(result, min=-reach, max=reach).astype(kind)


def setup_inputs(seed: int = 0, part: int = 0) -> dict:
    key_list = jax.random.split(jax.random.key(seed), 8)
    part_keys = jax.random.split(jax.random.fold_in(key_list[7], part), 8)
    return {
        "normed_input": gaussian(part_keys[0], (TOKENS, MODEL_WIDTH), 1.0, 6.0, ((0, 4),)),
        "query_weight": gaussian(key_list[1], (MODEL_WIDTH, QUERY_HEADS * HEAD_SIZE), MODEL_WIDTH ** -0.5, 0.0625, ((1, 4),)),
        "down_factors": gaussian(key_list[2], (ADAPTER_COUNT, MODEL_WIDTH, ADAPTER_RANK), MODEL_WIDTH ** -0.5, 0.0625, ((0, 4), (1, 4))),
        "up_factors": gaussian(key_list[3], (ADAPTER_COUNT, ADAPTER_RANK, QUERY_HEADS * HEAD_SIZE), ADAPTER_RANK ** -0.5, 0.75, ((0, 4), (2, 4))),
        "adapter_per_block": with_ends(ranked(part_keys[4], (BLOCKS,), ADAPTER_COUNT, 2), jax.random.fold_in(part_keys[4], 3), 0, ADAPTER_COUNT - 1).astype(jnp.int32),
        "key_value_cache": draw_key_value_cache(jax.random.fold_in(jax.random.fold_in(key_list[7], part), 71), part),
        "token_segment": jnp.searchsorted(jnp.cumsum(uneven_parts(part_keys[6], SEGMENTS, TOKENS, SEG_MOST, 2)), jnp.arange(TOKENS), side="right").astype(jnp.int32),
    }


def reference(normed_input, query_weight, down_factors, up_factors, adapter_per_block, key_value_cache, token_segment):
    tokens = normed_input.shape[0]
    base_query = jnp.dot(normed_input, query_weight, preferred_element_type=jnp.float32)
    selected_down = jnp.take(down_factors, adapter_per_block, axis=0).astype(jnp.float32)
    selected_up = jnp.take(up_factors, adapter_per_block, axis=0).astype(jnp.float32)
    blocks = normed_input.reshape(BLOCKS, BLOCK, MODEL_WIDTH).astype(jnp.float32)
    low_rank = jnp.einsum("jbd,jdr->jbr", blocks, selected_down).astype(jnp.bfloat16)
    adapter_term = jnp.einsum("jbr,jrc->jbc", low_rank.astype(jnp.float32), selected_up).reshape(tokens, QUERY_HEADS * HEAD_SIZE)
    queries = (base_query + adapter_term).astype(jnp.bfloat16).reshape(tokens, QUERY_HEADS, HEAD_SIZE)
    positions = jnp.arange(tokens, dtype=jnp.int32)
    allowed = (token_segment[:, None] == token_segment[None, :]) & (positions[None, :] <= positions[:, None])
    inv_root = HEAD_SIZE ** -0.5

    def one_head(head_index):
        query_rows = lax.dynamic_index_in_dim(queries, head_index, 1, keepdims=False)
        kv_rows = lax.dynamic_index_in_dim(key_value_cache, head_index // GROUP, 1, keepdims=False)
        key_rows = kv_rows[:, :HEAD_SIZE]
        value_rows = kv_rows[:, HEAD_SIZE:]
        scores = jnp.dot(query_rows, key_rows.T, preferred_element_type=jnp.float32) * inv_root
        masked = jnp.where(allowed, scores, jnp.float32(-1e30))
        row_max = jnp.max(masked, axis=1, keepdims=True)
        weights = jnp.where(allowed, jnp.exp(masked - row_max), jnp.float32(0.0))
        numerator = jnp.dot(weights.astype(jnp.bfloat16), value_rows, preferred_element_type=jnp.float32)
        return numerator / jnp.sum(weights, axis=1, keepdims=True)

    heads_out = lax.map(one_head, jnp.arange(QUERY_HEADS, dtype=jnp.int32))
    return jnp.transpose(heads_out, (1, 0, 2)).reshape(tokens, QUERY_HEADS * HEAD_SIZE).astype(jnp.bfloat16)
```

```python
import functools
import math

import jax
import jax.numpy as jnp
from jax import lax
from jax.experimental import pallas as pl
from jax.experimental.pallas import tpu as pltpu
from jax.sharding import PartitionSpec as P

HEAD_SIZE = 128
GROUP = 8
BLOCK = 128
ADAPTERS = 64
SEGMENTS = 4
LAG = 2
CHUNK = 512
MIB = 1 << 20
ANY = pl.BlockSpec(memory_space=pl.ANY)
SMEM = pl.BlockSpec(memory_space=pltpu.SMEM)
VMEM = pl.BlockSpec(memory_space=pltpu.VMEM)


def slot_bound(stores, per_store, blocks):
    load = max(
        min(per_store * (link + 1), blocks * (stores - 1 - link)) for link in range(stores - 1)
    )
    return load + (stores - 2) * LAG


def plan_kernel(groups, stores, blocks, per_store, slots, *refs):
    ranks = groups * stores
    index_refs = refs[:ranks]
    plan = refs[ranks]
    names, place, listed, bases, counts = refs[ranks + 1 :]
    capacity = per_store + 1
    my_group = lax.axis_index("groups")
    my_store = lax.axis_index("store")
    me = my_group * stores + my_store
    zero = jnp.int32(0)
    for shift in range(ranks):
        origin = lax.rem(me + ranks - shift, ranks)
        for b in range(blocks):
            names[origin * blocks + b] = index_refs[shift][b]

    def clear(i, _):
        place[i] = jnp.int32(-1)
        return 0

    lax.fori_loop(0, groups * 2 * ADAPTERS, clear, 0)
    most = zero
    for group in range(groups):
        for way in range(2):
            part = group * 2 + way
            count = [zero] * stores
            crossing = [[zero] * stores for _ in range(stores)]
            for dest in range(stores - 1, 0, -1):
                real = dest if way == 0 else stores - 1 - dest
                for b in range(blocks):
                    name = names[(group * stores + real) * blocks + b]
                    owner = lax.div(name, jnp.int32(per_store))
                    if way == 1:
                        owner = stores - 1 - owner
                    held = place[part * ADAPTERS + name]
                    new = (owner < dest) & (held < 0)
                    at = zero
                    for o in range(stores):
                        at = jnp.where(owner == o, count[o], at)
                    listed[(part * stores + owner) * capacity + at] = name
                    place[part * ADAPTERS + name] = jnp.where(new, at, held)
                    step = new.astype(jnp.int32)
                    for o in range(dest):
                        count[o] = count[o] + jnp.where(owner == o, step, 0)
                for o in range(dest):
                    crossing[o][dest - 1] = count[o]
            base = [[zero] * stores for _ in range(stores)]
            for link in range(stores):
                cursor = zero
                for o in range(stores):
                    spot = (part * stores + link) * stores + o
                    bases[spot] = zero
                    counts[spot] = zero
                if link == stores - 1:
                    continue
                for o in range(link, -1, -1):
                    start = cursor if o == link else jnp.maximum(cursor, base[link - 1][o] + LAG)
                    base[link][o] = start
                    number = crossing[o][link]
                    spot = (part * stores + link) * stores + o
                    bases[spot] = start
                    counts[spot] = number
                    cursor = jnp.where(number > 0, start + number, cursor)
                most = jnp.maximum(most, cursor)
    plan[0] = most

    def idle(i, _):
        plan[1 + i] = zero
        return 0

    lax.fori_loop(0, 2 * slots, idle, 0)
    for way in range(2):
        part = my_group * 2 + way
        mine = my_store if way == 0 else stores - 1 - my_store
        for o in range(stores - 1):
            spot = (part * stores + mine) * stores + o
            before = (part * stores + jnp.maximum(mine - 1, 0)) * stores + o
            start = bases[spot]
            earlier = bases[before]
            row = (part * stores + o) * capacity

            def fill(r, _):
                own = listed[row + r] - my_store * per_store
                plan[1 + way * slots + start + r] = jnp.where(
                    mine == o, own, per_store + way * slots + earlier + r
                )
                return 0

            lax.fori_loop(0, counts[spot], fill, 0)
    for b in range(blocks):
        name = names[me * blocks + b]
        owner = lax.div(name, jnp.int32(per_store))
        source = name - my_store * per_store
        for way in range(2):
            part = my_group * 2 + way
            mine = my_store if way == 0 else stores - 1 - my_store
            far = owner if way == 0 else stores - 1 - owner
            spot = (part * stores + jnp.maximum(mine - 1, 0)) * stores + far
            arrives = (
                per_store + way * slots + bases[spot] + place[part * ADAPTERS + name]
            )
            source = jnp.where(far < mine, arrives, source)
        plan[1 + 2 * slots + b] = source


def make_plan(shifted, groups, stores, blocks, per_store, slots):
    return pl.pallas_call(
        functools.partial(plan_kernel, groups, stores, blocks, per_store, slots),
        out_shape=jax.ShapeDtypeStruct((1 + 2 * slots + blocks,), jnp.int32),
        in_specs=[SMEM] * len(shifted),
        out_specs=SMEM,
        scratch_shapes=[
            pltpu.SMEM((groups * stores * blocks,), jnp.int32),
            pltpu.SMEM((groups * 2 * ADAPTERS,), jnp.int32),
            pltpu.SMEM((groups * 2 * stores * (per_store + 1),), jnp.int32),
            pltpu.SMEM((groups * 2 * stores * stores,), jnp.int32),
            pltpu.SMEM((groups * 2 * stores * stores,), jnp.int32),
        ],
        name="plan",
    )(*shifted)


def pack_kernel(slots, per_store, which, received, plan, down, up, *refs):
    got = [refs[:received], refs[received : 2 * received]]
    out = refs[2 * received : 2 * received + 2 * len(which)]
    sems = refs[-1]
    width = down.shape[2]

    def copies(way, i):
        source = plan[1 + way * slots + which[i]]
        dst = out[way * len(which) + i]
        sem = sems.at[way * len(which) + i]
        own = jnp.minimum(source, per_store - 1)
        pairs = [
            (
                source < per_store,
                [
                    pltpu.make_async_copy(down.at[own], dst.at[:, pl.ds(0, width)], sem),
                    pltpu.make_async_copy(
                        up.at[own], dst.at[:, pl.ds(width, up.shape[2])], sem
                    ),
                ],
            )
        ]
        for j in range(received):
            pairs.append(
                (
                    source == per_store + way * slots + j,
                    [pltpu.make_async_copy(got[way][j], dst, sem)],
                )
            )
        return pairs

    for act in ("start", "wait"):
        for way in range(2):
            for i in range(len(which)):
                for chosen, moves in copies(way, i):

                    @pl.when(chosen)
                    def _():
                        for move in moves:
                            getattr(move, act)()


def pack(plan, down, up, ups, downs, which, slots):
    per_store, rank, width = down.shape
    item = jax.ShapeDtypeStruct((rank, width + up.shape[2]), down.dtype)
    made = 2 * len(which)
    out = pl.pallas_call(
        functools.partial(pack_kernel, slots, per_store, tuple(which), len(ups)),
        out_shape=[item] * made,
        in_specs=[SMEM] + [ANY] * (2 + 2 * len(ups)),
        out_specs=[ANY] * made,
        scratch_shapes=[pltpu.SemaphoreType.DMA((made,))],
        cost_estimate=pl.CostEstimate(
            flops=0, bytes_accessed=made * 2 * 2 * item.shape[0] * item.shape[1], transcendentals=0
        ),
        name="pack",
    )(plan, down, up, *ups, *downs)
    return out[: len(which)], out[len(which) :]


def low_rank_kernel(slots, per_store, received, tensor, plan, x, down, up, *refs):
    got = refs[: 2 * received]
    outs = refs[2 * received : 2 * received + tensor]
    selected, x_rows, factors, sems = refs[2 * received + tensor :]
    blocks, rank, width = factors.shape
    share = blocks // tensor
    member = lax.axis_index("tensor")
    columns = pl.ds(pl.multiple_of(member * width, 128), width)
    if tensor == 1:
        member = 0

    def copies(b):
        source = plan[1 + 2 * slots + b]
        own = jnp.minimum(source, per_store - 1)
        pairs = [
            (
                source < per_store,
                [
                    pltpu.make_async_copy(down.at[own], factors.at[b], sems.at[b]),
                    pltpu.make_async_copy(up.at[own], selected.at[b], sems.at[b]),
                ],
            )
        ]
        for j in range(2 * received):
            spot = j if j < received else slots + j - received
            pairs.append(
                (
                    source == per_store + spot,
                    [
                        pltpu.make_async_copy(
                            got[j].at[:, pl.ds(0, width)], factors.at[b], sems.at[b]
                        ),
                        pltpu.make_async_copy(
                            got[j].at[:, pl.ds(width, up.shape[2])], selected.at[b], sems.at[b]
                        ),
                    ],
                )
            )
        return pairs

    def rows_of(b):
        rows = pl.ds(pl.multiple_of(b * BLOCK, BLOCK), BLOCK)
        return pltpu.make_async_copy(x.at[rows, columns], x_rows.at[b], sems.at[blocks + b])

    def start(b, _):
        rows_of(b).start()
        for chosen, moves in copies(b):

            @pl.when(chosen)
            def _():
                for move in moves:
                    move.start()

        return 0

    lax.fori_loop(0, blocks, start, 0)

    def finish(b):
        own = pltpu.make_async_copy(down.at[0], factors.at[b], sems.at[b])
        own_up = pltpu.make_async_copy(up.at[0], selected.at[b], sems.at[b])
        own.wait()
        own_up.wait()
        rows_of(b).wait()

    for m in range(tensor):
        for i in range(share):
            b = (member ^ m) * share + i
            finish(b)
            outs[m][i] = lax.dot_general(
                factors[b], x_rows[b], (((1,), (1,)), ((), ())), preferred_element_type=jnp.float32
            )


def low_rank_parts(plan, x, down, up, ups, downs, slots, tensor, blocks):
    per_store, rank, width = down.shape
    share = blocks // tensor
    out = pl.pallas_call(
        functools.partial(low_rank_kernel, slots, per_store, len(ups), tensor),
        out_shape=[jax.ShapeDtypeStruct((share, rank, BLOCK), jnp.float32)] * tensor
        + [jax.ShapeDtypeStruct((blocks, rank, up.shape[2]), up.dtype)],
        in_specs=[SMEM] + [ANY] * (3 + 2 * len(ups)),
        out_specs=[VMEM] * (tensor + 1),
        scratch_shapes=[
            pltpu.VMEM((blocks, BLOCK, width), x.dtype),
            pltpu.VMEM((blocks, rank, width), down.dtype),
            pltpu.SemaphoreType.DMA((2 * blocks,)),
        ],
        compiler_params=pltpu.CompilerParams(vmem_limit_bytes=24 * MIB),
        cost_estimate=pl.CostEstimate(
            flops=2 * blocks * BLOCK * rank * width,
            bytes_accessed=2 * blocks * width * (BLOCK + rank),
            transcendentals=0,
        ),
        name="low_rank",
    )(plan, x, down, up, *ups, *downs)
    return out[:tensor], out[tensor]


def window_kernel(hops, share, pad, *refs):
    pieces = refs[: hops * share]
    own = refs[hops * share]
    segments = refs[hops * share + 1]
    keys, values, starts, firsts, buffer, sems = refs[hops * share + 2 :]
    rows = own.shape[0]
    part = rows // share
    member = lax.rem(lax.axis_index("tensor"), share)
    moves = [
        pltpu.make_async_copy(own, buffer.at[pl.ds(hops * rows, rows)], sems.at[hops * share])
    ]
    for hop in range(hops):
        for m in range(share):
            at = pl.multiple_of((hops - 1 - hop) * rows + (member ^ m) * part, part)
            moves.append(
                pltpu.make_async_copy(
                    pieces[hop * share + m], buffer.at[pl.ds(at, part)], sems.at[hop * share + m]
                )
            )
    for move in moves:
        move.start()
    store = lax.axis_index("store")
    names = segments[...]
    mine = names[hops * (rows // BLOCK) :]
    empty = jnp.maximum(hops - store, 0) * rows
    start = jnp.zeros(mine.shape, jnp.int32) + empty
    for value in range(1, SEGMENTS):
        number = jnp.sum((names < value).astype(jnp.float32)).astype(jnp.int32)
        start = jnp.where(mine == value, jnp.maximum(number, empty), start)
    starts[...] = start.reshape(starts.shape)
    for j in range(mine.shape[0]):
        firsts[j] = jnp.min(start[j : j + 1].astype(jnp.float32)).astype(jnp.int32)
    for move in moves:
        move.wait()
    keys[pl.ds(0, pad), :] = jnp.zeros((pad, HEAD_SIZE), keys.dtype)
    values[:, pl.ds(0, pad)] = jnp.zeros((HEAD_SIZE, pad), values.dtype)

    def turn(c, _):
        at = pl.ds(pl.multiple_of(c * 256, 256), 256)
        to = pl.ds(pl.multiple_of(pad + c * 256, 256), 256)
        keys[to, :] = buffer[at, pl.ds(0, HEAD_SIZE)]
        values[:, to] = buffer[at, pl.ds(HEAD_SIZE, HEAD_SIZE)].astype(jnp.float32).T.astype(
            values.dtype
        )
        return 0

    lax.fori_loop(0, (hops + 1) * rows // 256, turn, 0)


def window(pieces, own, segments, hops, share, pad):
    rows = own.shape[0]
    length = pad + (hops + 1) * rows
    return pl.pallas_call(
        functools.partial(window_kernel, hops, share, pad),
        out_shape=[
            jax.ShapeDtypeStruct((length, HEAD_SIZE), own.dtype),
            jax.ShapeDtypeStruct((HEAD_SIZE, length), own.dtype),
            jax.ShapeDtypeStruct((rows // BLOCK, 1, BLOCK), jnp.int32),
            jax.ShapeDtypeStruct((rows // BLOCK,), jnp.int32),
        ],
        in_specs=[ANY] * (hops * share + 1) + [VMEM],
        out_specs=[VMEM, VMEM, VMEM, SMEM],
        scratch_shapes=[
            pltpu.VMEM(((hops + 1) * rows, 2 * HEAD_SIZE), own.dtype),
            pltpu.SemaphoreType.DMA((hops * share + 1,)),
        ],
        compiler_params=pltpu.CompilerParams(vmem_limit_bytes=24 * MIB),
        cost_estimate=pl.CostEstimate(
            flops=0, bytes_accessed=8 * length * HEAD_SIZE, transcendentals=0
        ),
        name="window",
    )(*pieces, own, segments)


def attention_kernel(
    hops, tensor, pad, heads, firsts, base, starts, keys, values, selected, *refs
):
    ranks = refs[:tensor]
    out, scores, queries = refs[tensor:]
    j = pl.program_id(0)
    share = ranks[0].shape[0]
    member = lax.axis_index("tensor") if tensor > 1 else 0
    rows = (keys.shape[0] - pad) // (hops + 1)
    low = jnp.zeros(ranks[0].shape[1:], jnp.bfloat16)
    for m in range(tensor):
        for i in range(share):
            low = jnp.where(j == (member ^ m) * share + i, ranks[m][i], low)
    term = lax.dot_general(
        selected[0], low, (((0,), (0,)), ((), ())), preferred_element_type=jnp.float32
    )
    turned = (base[...] + term).astype(jnp.bfloat16)
    for h in range(heads):
        queries[:, h * BLOCK : (h + 1) * BLOCK] = turned[h * HEAD_SIZE : (h + 1) * HEAD_SIZE]
    q = queries[...]
    columns = heads * BLOCK
    start = jnp.concatenate([starts[0]] * heads, axis=1)
    token = hops * rows + j * BLOCK + lax.rem(
        lax.broadcasted_iota(jnp.int32, (1, columns), 1), BLOCK
    )
    end = pad + hops * rows + (j + 1) * BLOCK
    steps = lax.div(end - pad - firsts[j] + CHUNK - 1, jnp.int32(CHUNK))
    scale = HEAD_SIZE**-0.5 * math.log2(math.e)

    def score(c, largest):
        at = pl.multiple_of(end - (c + 1) * CHUNK, BLOCK)
        s = jnp.dot(keys[pl.ds(at, CHUNK), :], q, preferred_element_type=jnp.float32)
        position = at - pad + lax.broadcasted_iota(jnp.int32, (CHUNK, columns), 0)
        s = jnp.where((position >= start) & (position <= token), s, jnp.float32(-1e30))
        scores[pl.ds(pl.multiple_of(c * CHUNK, CHUNK), CHUNK), :] = s
        return jnp.maximum(largest, jnp.max(s.reshape(CHUNK // 8, 8, columns), axis=0))

    largest = lax.fori_loop(0, steps, score, jnp.full((8, columns), -1e30, jnp.float32))
    top = jnp.max(largest, axis=0, keepdims=True)

    def weigh(c, carry):
        total, summed = carry
        at = pl.multiple_of(end - (c + 1) * CHUNK, BLOCK)
        s = scores[pl.ds(pl.multiple_of(c * CHUNK, CHUNK), CHUNK), :]
        w = jnp.exp2((s - top) * scale)
        total = total + jnp.sum(w.reshape(CHUNK // 8, 8, columns), axis=0)
        summed = summed + jnp.dot(
            values[:, pl.ds(at, CHUNK)], w.astype(jnp.bfloat16), preferred_element_type=jnp.float32
        )
        return total, summed

    total, summed = lax.fori_loop(
        0,
        steps,
        weigh,
        (jnp.zeros((8, columns), jnp.float32), jnp.zeros((HEAD_SIZE, columns), jnp.float32)),
    )
    attended = summed / jnp.sum(total, axis=0, keepdims=True)
    for h in range(heads):
        out[:, h * HEAD_SIZE : (h + 1) * HEAD_SIZE] = (
            attended[:, h * BLOCK : (h + 1) * BLOCK].T.astype(out.dtype)
        )


def attention(firsts, base, starts, keys, values, selected, ranks, hops, pad, heads):
    columns, rows = base.shape
    blocks = rows // BLOCK
    length = keys.shape[0]
    whole = lambda shape: pl.BlockSpec(shape, lambda j, *_: (0,) * len(shape))
    return pl.pallas_call(
        functools.partial(attention_kernel, hops, len(ranks), pad, heads),
        out_shape=jax.ShapeDtypeStruct((rows, columns), jnp.bfloat16),
        grid_spec=pltpu.PrefetchScalarGridSpec(
            num_scalar_prefetch=1,
            grid=(blocks,),
            in_specs=[
                pl.BlockSpec((columns, BLOCK), lambda j, *_: (0, j)),
                pl.BlockSpec((1, 1, BLOCK), lambda j, *_: (j, 0, 0)),
                whole(keys.shape),
                whole(values.shape),
                pl.BlockSpec((1,) + selected.shape[1:], lambda j, *_: (j, 0, 0)),
            ]
            + [whole(r.shape) for r in ranks],
            out_specs=pl.BlockSpec((BLOCK, columns), lambda j, *_: (j, 0)),
            scratch_shapes=[
                pltpu.VMEM((length, heads * BLOCK), jnp.float32),
                pltpu.VMEM((HEAD_SIZE, heads * BLOCK), jnp.bfloat16),
            ],
        ),
        compiler_params=pltpu.CompilerParams(vmem_limit_bytes=40 * MIB),
        cost_estimate=pl.CostEstimate(
            flops=2 * rows * columns * length,
            bytes_accessed=8 * length * HEAD_SIZE,
            transcendentals=rows * heads * length,
        ),
        name="attention",
    )(firsts, base, starts, keys, values, selected, *ranks)


def per_device(
    mesh_shape,
    normed_input,
    query_weight,
    down_factors,
    up_factors,
    adapter_per_block,
    key_value_cache,
    token_segment,
):
    groups, tensor, stores = (mesh_shape[a] for a in ("groups", "tensor", "store"))
    rows = normed_input.shape[0]
    blocks = adapter_per_block.shape[0]
    heads = query_weight.shape[1] // HEAD_SIZE
    per_store = down_factors.shape[0]
    member = lax.axis_index("tensor")
    slots = slot_bound(stores, per_store, blocks)
    hops = min(stores - 1, -(-(stores * rows // 2 - 1) // rows))
    share = min(tensor, max(1, GROUP // heads))
    quarter = rows // share
    both = ("groups", "store")
    ranks = groups * stores

    shifted = [adapter_per_block] + [
        lax.ppermute(adapter_per_block, both, [(i, (i + m) % ranks) for i in range(ranks)])
        for m in range(1, ranks)
    ]
    cache = jnp.swapaxes(key_value_cache, 0, 1)
    cache = lax.dynamic_index_in_dim(cache, member * heads // GROUP, 0, keepdims=False)
    my_quarter = lax.dynamic_slice_in_dim(cache, lax.rem(member, share) * quarter, quarter, 0)
    later = lambda v, hop: lax.ppermute(v, "store", [(i, i + hop) for i in range(stores - hop)])
    quarters = [later(my_quarter, hop) for hop in range(1, hops + 1)]
    earlier = [later(token_segment, hop) for hop in range(1, hops + 1)]

    down = jnp.swapaxes(down_factors, 1, 2)
    plan = make_plan(shifted, groups, stores, blocks, per_store, slots)

    def fetch(count, plan, x, weight, down, up, cache, segments, quarters, earlier):
        raise_up = [(i, i + 1) for i in range(stores - 1)]
        raise_down = [(i + 1, i) for i in range(stores - 1)]
        ups, downs, sent = [], [], []
        first = min(LAG, count)
        s_up, s_down = pack(plan, down, up, [], [], range(first), slots)
        for k in range(count):
            if k >= first:
                u, d = pack(plan, down, up, ups[: k - LAG + 1], downs[: k - LAG + 1], [k], slots)
                s_up, s_down = list(s_up) + list(u), list(s_down) + list(d)
            ups.append(lax.ppermute(s_up[k], "store", raise_up))
            downs.append(lax.ppermute(s_down[k], "store", raise_down))
        pieces = []
        for piece in quarters:
            pieces.append(piece)
            for m in range(1, share):
                pieces.append(lax.ppermute(piece, "tensor", [(t, t ^ m) for t in range(tensor)]))
        names = jnp.concatenate([s.reshape(-1, BLOCK) for s in earlier[::-1]] + [segments.reshape(-1, BLOCK)])
        keys, values, starts, firsts = window(pieces, cache, names, hops, share, CHUNK)
        base = lax.dot_general(
            weight, x, (((0,), (1,)), ((), ())), preferred_element_type=jnp.float32
        )
        exchange = tensor if blocks % tensor == 0 else 1
        parts, selected = low_rank_parts(
            plan, x, down, up, ups, downs, slots, exchange, blocks
        )
        return base, keys, values, starts, firsts, tuple(parts), selected

    sizes = [n for n in (5, 6, 7, 8, 9, 10, 12) if n < slots] if slots <= 24 else [slots // 2]
    sizes.append(slots)
    which = sum((plan[0] > n).astype(jnp.int32) for n in sizes[:-1])
    base, keys, values, starts, firsts, parts, selected = lax.switch(
        which,
        [functools.partial(fetch, n) for n in sizes],
        plan,
        normed_input,
        query_weight,
        down,
        up_factors,
        cache,
        token_segment,
        tuple(quarters),
        tuple(earlier),
    )
    if len(parts) == tensor:
        pairs = lambda m: [(t, t ^ m) for t in range(tensor)]
        total = parts[0]
        for m in range(1, tensor):
            total = total + lax.ppermute(parts[m], "tensor", pairs(m))
        total = total.astype(jnp.bfloat16)
        low = [total] + [lax.ppermute(total, "tensor", pairs(m)) for m in range(1, tensor)]
    else:
        low = [lax.psum(parts[0], "tensor").astype(jnp.bfloat16)]
    return attention(firsts, base, starts, keys, values, selected, low, hops, CHUNK, heads)


def solution(mesh):
    return jax.shard_map(
        functools.partial(per_device, dict(mesh.shape)),
        mesh=mesh,
        in_specs=(
            P(("groups", "store"), None),
            P(None, "tensor"),
            P("store", "tensor", None),
            P("store", None, "tensor"),
            P(("groups", "store")),
            P(("groups", "store"), None, None),
            P(("groups", "store")),
        ),
        out_specs=P(("groups", "store"), "tensor"),
        check_vma=False,
    )
```

```python
import functools
import math

import jax
import jax.numpy as jnp
from jax import lax
from jax.experimental import pallas as pl
from jax.experimental.pallas import tpu as pltpu
from jax.sharding import PartitionSpec as P

HEAD_SIZE = 128
GROUP = 8
BLOCK = 128
ADAPTERS = 64
SEGMENTS = 4
LAG = 2
USUAL_SLOTS = 10
CHUNK = 512
MIB = 1 << 20
ANY = pl.BlockSpec(memory_space=pl.ANY)
SMEM = pl.BlockSpec(memory_space=pltpu.SMEM)
VMEM = pl.BlockSpec(memory_space=pltpu.VMEM)


def slot_bound(stores, per_store, blocks):
    load = max(
        min(per_store * (link + 1), blocks * (stores - 1 - link)) for link in range(stores - 1)
    )
    return load + (stores - 2) * LAG


def plan_kernel(stores, blocks, per_store, slots, *refs):
    index_refs = refs[:stores]
    plan, most_ref = refs[stores : stores + 2]
    names, place, listed, bases, counts = refs[stores + 2 :]
    capacity = per_store + 1
    my_store = lax.axis_index("store")
    zero = jnp.int32(0)
    for shift in range(stores):
        origin = lax.rem(my_store + stores - shift, stores)
        for b in range(blocks):
            names[origin * blocks + b] = index_refs[shift][b]
    for i in range(2 * ADAPTERS):
        place[i] = jnp.int32(-1)
    for i in range(2 * slots):
        plan[1 + i] = zero
    most = zero
    for way in range(2):
        count = [zero] * stores
        crossing = [[zero] * stores for _ in range(stores)]
        for dest in range(stores - 1, 0, -1):
            real = dest if way == 0 else stores - 1 - dest
            for b in range(blocks):
                name = names[real * blocks + b]
                owner = lax.div(name, jnp.int32(per_store))
                if way == 1:
                    owner = stores - 1 - owner
                held = place[way * ADAPTERS + name]
                new = (owner < dest) & (held < 0)
                at = zero
                for o in range(stores):
                    at = jnp.where(owner == o, count[o], at)
                listed[(way * stores + owner) * capacity + at] = name
                place[way * ADAPTERS + name] = jnp.where(new, at, held)
                step = new.astype(jnp.int32)
                for o in range(dest):
                    count[o] = count[o] + jnp.where(owner == o, step, 0)
            for o in range(dest):
                crossing[o][dest - 1] = count[o]
        base = [[zero] * stores for _ in range(stores)]
        for link in range(stores):
            cursor = zero
            for o in range(stores):
                spot = (way * stores + link) * stores + o
                bases[spot] = zero
                counts[spot] = zero
            if link == stores - 1:
                continue
            for o in range(link, -1, -1):
                start = cursor if o == link else jnp.maximum(cursor, base[link - 1][o] + LAG)
                base[link][o] = start
                number = crossing[o][link]
                spot = (way * stores + link) * stores + o
                bases[spot] = start
                counts[spot] = number
                cursor = jnp.where(number > 0, start + number, cursor)
            most = jnp.maximum(most, cursor)
    plan[0] = most
    for i in range(8):
        most_ref[i] = most
    for way in range(2):
        mine = my_store if way == 0 else stores - 1 - my_store
        for o in range(stores - 1):
            spot = (way * stores + mine) * stores + o
            before = (way * stores + jnp.maximum(mine - 1, 0)) * stores + o
            start = bases[spot]
            earlier = bases[before]
            row = (way * stores + o) * capacity

            def fill(r, _):
                own = listed[row + r] - my_store * per_store
                plan[1 + way * slots + start + r] = jnp.where(
                    mine == o, own, per_store + way * slots + earlier + r
                )
                return 0

            lax.fori_loop(0, counts[spot], fill, 0)
    for b in range(blocks):
        name = names[my_store * blocks + b]
        owner = lax.div(name, jnp.int32(per_store))
        source = name - my_store * per_store
        for way in range(2):
            mine = my_store if way == 0 else stores - 1 - my_store
            far = owner if way == 0 else stores - 1 - owner
            spot = (way * stores + jnp.maximum(mine - 1, 0)) * stores + far
            arrives = per_store + way * slots + bases[spot] + place[way * ADAPTERS + name]
            source = jnp.where(far < mine, arrives, source)
        plan[1 + 2 * slots + b] = source


def make_plan(shifted, stores, blocks, per_store, slots):
    return pl.pallas_call(
        functools.partial(plan_kernel, stores, blocks, per_store, slots),
        out_shape=[
            jax.ShapeDtypeStruct((1 + 2 * slots + blocks,), jnp.int32),
            jax.ShapeDtypeStruct((8,), jnp.int32),
        ],
        in_specs=[SMEM] * len(shifted),
        out_specs=[SMEM, SMEM],
        scratch_shapes=[
            pltpu.SMEM((stores * blocks,), jnp.int32),
            pltpu.SMEM((2 * ADAPTERS,), jnp.int32),
            pltpu.SMEM((2 * stores * (per_store + 1),), jnp.int32),
            pltpu.SMEM((2 * stores * stores,), jnp.int32),
            pltpu.SMEM((2 * stores * stores,), jnp.int32),
        ],
        name="plan",
    )(*shifted)


def pack_kernel(slots, per_store, which, received, plan, down, up, *refs):
    got = [refs[:received], refs[received : 2 * received]]
    out = refs[2 * received : 2 * received + 2 * len(which)]
    sems = refs[-1]
    width = down.shape[2]

    def copies(way, i):
        source = plan[1 + way * slots + which[i]]
        dst = out[way * len(which) + i]
        sem = sems.at[way * len(which) + i]
        own = jnp.minimum(source, per_store - 1)
        pairs = [
            (
                source < per_store,
                [
                    pltpu.make_async_copy(down.at[own], dst.at[:, pl.ds(0, width)], sem),
                    pltpu.make_async_copy(
                        up.at[own], dst.at[:, pl.ds(width, up.shape[2])], sem
                    ),
                ],
            )
        ]
        for j in range(received):
            pairs.append(
                (
                    source == per_store + way * slots + j,
                    [pltpu.make_async_copy(got[way][j], dst, sem)],
                )
            )
        return pairs

    for act in ("start", "wait"):
        for way in range(2):
            for i in range(len(which)):
                for chosen, moves in copies(way, i):

                    @pl.when(chosen)
                    def _():
                        for move in moves:
                            getattr(move, act)()


def pack(plan, down, up, ups, downs, which, slots):
    per_store, rank, width = down.shape
    item = jax.ShapeDtypeStruct((rank, width + up.shape[2]), down.dtype)
    made = 2 * len(which)
    out = pl.pallas_call(
        functools.partial(pack_kernel, slots, per_store, tuple(which), len(ups)),
        out_shape=[item] * made,
        in_specs=[SMEM] + [ANY] * (2 + 2 * len(ups)),
        out_specs=[VMEM] * made,
        scratch_shapes=[pltpu.SemaphoreType.DMA((made,))],
        compiler_params=pltpu.CompilerParams(vmem_limit_bytes=16 * MIB),
        cost_estimate=pl.CostEstimate(
            flops=0, bytes_accessed=made * 2 * 2 * item.shape[0] * item.shape[1], transcendentals=0
        ),
        name="pack",
    )(plan, down, up, *ups, *downs)
    return out[: len(which)], out[len(which) :]


def low_rank_kernel(slots, per_store, received, tensor, plan, x, down, up, *refs):
    got = refs[: 2 * received]
    outs = refs[2 * received : 2 * received + tensor]
    selected, x_rows, factors, sems = refs[2 * received + tensor :]
    blocks, rank, width = factors.shape
    share = blocks // tensor
    member = lax.axis_index("tensor")
    columns = pl.ds(pl.multiple_of(member * width, 128), width)
    if tensor == 1:
        member = 0

    def copies(b):
        source = plan[1 + 2 * slots + b]
        known = (source < per_store + received) | (
            (source >= per_store + slots) & (source < per_store + slots + received)
        )
        source = jnp.where(known, source, 0)
        own = jnp.minimum(source, per_store - 1)
        pairs = [
            (
                source < per_store,
                [
                    pltpu.make_async_copy(down.at[own], factors.at[b], sems.at[b]),
                    pltpu.make_async_copy(up.at[own], selected.at[b], sems.at[b]),
                ],
            )
        ]
        for j in range(2 * received):
            spot = j if j < received else slots + j - received
            pairs.append(
                (
                    source == per_store + spot,
                    [
                        pltpu.make_async_copy(
                            got[j].at[:, pl.ds(0, width)], factors.at[b], sems.at[b]
                        ),
                        pltpu.make_async_copy(
                            got[j].at[:, pl.ds(width, up.shape[2])], selected.at[b], sems.at[b]
                        ),
                    ],
                )
            )
        return pairs

    def rows_of(b):
        rows = pl.ds(pl.multiple_of(b * BLOCK, BLOCK), BLOCK)
        return pltpu.make_async_copy(x.at[rows, columns], x_rows.at[b], sems.at[blocks + b])

    def start(b, _):
        rows_of(b).start()
        for chosen, moves in copies(b):

            @pl.when(chosen)
            def _():
                for move in moves:
                    move.start()

        return 0

    lax.fori_loop(0, blocks, start, 0)

    def finish(b):
        own = pltpu.make_async_copy(down.at[0], factors.at[b], sems.at[b])
        own_up = pltpu.make_async_copy(up.at[0], selected.at[b], sems.at[b])
        own.wait()
        own_up.wait()
        rows_of(b).wait()

    for m in range(tensor):
        for i in range(share):
            b = (member ^ m) * share + i
            finish(b)
            outs[m][i] = lax.dot_general(
                x_rows[b], factors[b], (((1,), (1,)), ((), ())), preferred_element_type=jnp.float32
            ).T


def low_rank_parts(plan, x, down, up, ups, downs, slots, tensor, blocks):
    per_store, rank, width = down.shape
    share = blocks // tensor
    out = pl.pallas_call(
        functools.partial(low_rank_kernel, slots, per_store, len(ups), tensor),
        out_shape=[jax.ShapeDtypeStruct((share, rank, BLOCK), jnp.float32)] * tensor
        + [jax.ShapeDtypeStruct((blocks, rank, up.shape[2]), up.dtype)],
        in_specs=[SMEM] + [ANY] * (3 + 2 * len(ups)),
        out_specs=[VMEM] * (tensor + 1),
        scratch_shapes=[
            pltpu.VMEM((blocks, BLOCK, width), x.dtype),
            pltpu.VMEM((blocks, rank, width), down.dtype),
            pltpu.SemaphoreType.DMA((2 * blocks,)),
        ],
        compiler_params=pltpu.CompilerParams(vmem_limit_bytes=24 * MIB),
        cost_estimate=pl.CostEstimate(
            flops=2 * blocks * BLOCK * rank * width,
            bytes_accessed=2 * blocks * width * (BLOCK + rank),
            transcendentals=0,
        ),
        name="low_rank",
    )(plan, x, down, up, *ups, *downs)
    return out[:tensor], out[tensor]


def window_kernel(hops, share, pad, *refs):
    pieces = refs[:share]
    own, segments, keys, values, starts, firsts, buffer, sems = refs[share:]
    rows = own.shape[0]
    part = rows // share
    member = lax.rem(lax.axis_index("tensor"), share)
    moves = [
        pltpu.make_async_copy(own, buffer.at[pl.ds(hops * rows, rows)], sems.at[hops * share])
    ]
    for hop in range(hops):
        for m in range(share):
            at = pl.multiple_of((hops - 1 - hop) * rows + (member ^ m) * part, part)
            moves.append(
                pltpu.make_async_copy(
                    pieces[m].at[hop], buffer.at[pl.ds(at, part)], sems.at[hop * share + m]
                )
            )
    for move in moves:
        move.start()
    store = lax.axis_index("store")
    names = segments[...]
    mine = names[hops * (rows // BLOCK) :]
    empty = jnp.maximum(hops - store, 0) * rows
    start = jnp.zeros(mine.shape, jnp.int32) + empty
    for value in range(1, SEGMENTS):
        number = jnp.sum((names < value).astype(jnp.float32)).astype(jnp.int32)
        start = jnp.where(mine == value, jnp.maximum(number, empty), start)
    starts[...] = start.reshape(starts.shape)
    for j in range(mine.shape[0]):
        firsts[j] = jnp.min(start[j : j + 1].astype(jnp.float32)).astype(jnp.int32)
    for move in moves:
        move.wait()
    keys[pl.ds(0, pad), :] = jnp.zeros((pad, HEAD_SIZE), keys.dtype)
    values[:, pl.ds(0, pad)] = jnp.zeros((HEAD_SIZE, pad), values.dtype)

    def turn(c, _):
        at = pl.ds(pl.multiple_of(c * 256, 256), 256)
        to = pl.ds(pl.multiple_of(pad + c * 256, 256), 256)
        keys[to, :] = buffer[at, pl.ds(0, HEAD_SIZE)]
        values[:, to] = buffer[at, pl.ds(HEAD_SIZE, HEAD_SIZE)].astype(jnp.float32).T.astype(
            values.dtype
        )
        return 0

    lax.fori_loop(0, (hops + 1) * rows // 256, turn, 0)


def window(pieces, own, segments, hops, share, pad):
    rows = own.shape[0]
    length = pad + (hops + 1) * rows
    return pl.pallas_call(
        functools.partial(window_kernel, hops, share, pad),
        out_shape=[
            jax.ShapeDtypeStruct((length, HEAD_SIZE), own.dtype),
            jax.ShapeDtypeStruct((HEAD_SIZE, length), own.dtype),
            jax.ShapeDtypeStruct((rows // BLOCK, 1, BLOCK), jnp.int32),
            jax.ShapeDtypeStruct((rows // BLOCK,), jnp.int32),
        ],
        in_specs=[ANY] * (share + 1) + [VMEM],
        out_specs=[VMEM, VMEM, VMEM, SMEM],
        scratch_shapes=[
            pltpu.VMEM(((hops + 1) * rows, 2 * HEAD_SIZE), own.dtype),
            pltpu.SemaphoreType.DMA((hops * share + 1,)),
        ],
        compiler_params=pltpu.CompilerParams(vmem_limit_bytes=24 * MIB),
        cost_estimate=pl.CostEstimate(
            flops=0, bytes_accessed=8 * length * HEAD_SIZE, transcendentals=0
        ),
        name="window",
    )(*pieces, own, segments)


def attention_kernel(
    hops, tensor, pad, heads, firsts, base, starts, keys, values, selected, *refs
):
    ranks = refs[:tensor]
    out, scores, queries = refs[tensor:]
    j = pl.program_id(0)
    share = ranks[0].shape[0]
    member = lax.axis_index("tensor") if tensor > 1 else 0
    rows = (keys.shape[0] - pad) // (hops + 1)
    low = jnp.zeros(ranks[0].shape[1:], jnp.bfloat16)
    for m in range(tensor):
        for i in range(share):
            low = jnp.where(j == (member ^ m) * share + i, ranks[m][i], low)
    term = lax.dot_general(
        selected[0], low, (((0,), (0,)), ((), ())), preferred_element_type=jnp.float32
    )
    turned = (base[...] + term).astype(jnp.bfloat16)
    for h in range(heads):
        queries[:, h * BLOCK : (h + 1) * BLOCK] = turned[h * HEAD_SIZE : (h + 1) * HEAD_SIZE]
    q = queries[...]
    columns = heads * BLOCK
    start = jnp.concatenate([starts[0]] * heads, axis=1)
    token = hops * rows + j * BLOCK + lax.rem(
        lax.broadcasted_iota(jnp.int32, (1, columns), 1), BLOCK
    )
    end = pad + hops * rows + (j + 1) * BLOCK
    steps = lax.div(end - pad - firsts[j] + CHUNK - 1, jnp.int32(CHUNK))
    scale = HEAD_SIZE**-0.5 * math.log2(math.e)

    def score(c, largest):
        at = pl.multiple_of(end - (c + 1) * CHUNK, BLOCK)
        s = jnp.dot(keys[pl.ds(at, CHUNK), :], q, preferred_element_type=jnp.float32)
        position = at - pad + lax.broadcasted_iota(jnp.int32, (CHUNK, columns), 0)
        s = jnp.where((position >= start) & (position <= token), s, jnp.float32(-1e30))
        scores[pl.ds(pl.multiple_of(c * CHUNK, CHUNK), CHUNK), :] = s
        return jnp.maximum(largest, jnp.max(s.reshape(CHUNK // 8, 8, columns), axis=0))

    largest = lax.fori_loop(0, steps, score, jnp.full((8, columns), -1e30, jnp.float32))
    top = jnp.max(largest, axis=0, keepdims=True)

    def weigh(c, carry):
        total, summed = carry
        at = pl.multiple_of(end - (c + 1) * CHUNK, BLOCK)
        s = scores[pl.ds(pl.multiple_of(c * CHUNK, CHUNK), CHUNK), :]
        w = jnp.exp2((s - top) * scale)
        total = total + jnp.sum(w.reshape(CHUNK // 8, 8, columns), axis=0)
        summed = summed + jnp.dot(
            values[:, pl.ds(at, CHUNK)], w.astype(jnp.bfloat16), preferred_element_type=jnp.float32
        )
        return total, summed

    total, summed = lax.fori_loop(
        0,
        steps,
        weigh,
        (jnp.zeros((8, columns), jnp.float32), jnp.zeros((HEAD_SIZE, columns), jnp.float32)),
    )
    attended = summed / jnp.sum(total, axis=0, keepdims=True)
    for h in range(heads):
        out[:, h * HEAD_SIZE : (h + 1) * HEAD_SIZE] = (
            attended[:, h * BLOCK : (h + 1) * BLOCK].T.astype(out.dtype)
        )


def attention(firsts, base, starts, keys, values, selected, ranks, hops, pad, heads):
    columns, rows = base.shape
    blocks = rows // BLOCK
    length = keys.shape[0]
    whole = lambda shape: pl.BlockSpec(shape, lambda j, *_: (0,) * len(shape))
    return pl.pallas_call(
        functools.partial(attention_kernel, hops, len(ranks), pad, heads),
        out_shape=jax.ShapeDtypeStruct((rows, columns), jnp.bfloat16),
        grid_spec=pltpu.PrefetchScalarGridSpec(
            num_scalar_prefetch=1,
            grid=(blocks,),
            in_specs=[
                pl.BlockSpec((columns, BLOCK), lambda j, *_: (0, j)),
                pl.BlockSpec((1, 1, BLOCK), lambda j, *_: (j, 0, 0)),
                whole(keys.shape),
                whole(values.shape),
                pl.BlockSpec((1,) + selected.shape[1:], lambda j, *_: (j, 0, 0)),
            ]
            + [whole(r.shape) for r in ranks],
            out_specs=pl.BlockSpec((BLOCK, columns), lambda j, *_: (j, 0)),
            scratch_shapes=[
                pltpu.VMEM((length, heads * BLOCK), jnp.float32),
                pltpu.VMEM((HEAD_SIZE, heads * BLOCK), jnp.bfloat16),
            ],
        ),
        compiler_params=pltpu.CompilerParams(vmem_limit_bytes=40 * MIB),
        cost_estimate=pl.CostEstimate(
            flops=2 * rows * columns * length,
            bytes_accessed=8 * length * HEAD_SIZE,
            transcendentals=rows * heads * length,
        ),
        name="attention",
    )(firsts, base, starts, keys, values, selected, *ranks)


def per_device(
    mesh_shape,
    normed_input,
    query_weight,
    down_factors,
    up_factors,
    adapter_per_block,
    key_value_cache,
    token_segment,
):
    groups, tensor, stores = (mesh_shape[a] for a in ("groups", "tensor", "store"))
    rows = normed_input.shape[0]
    blocks = adapter_per_block.shape[0]
    heads = query_weight.shape[1] // HEAD_SIZE
    per_store = down_factors.shape[0]
    member = lax.axis_index("tensor")
    slots = slot_bound(stores, per_store, blocks)
    usual = min(slots, USUAL_SLOTS)
    hops = min(stores - 1, -(-(stores * rows // 2 - 1) // rows))
    share = min(tensor, max(1, GROUP // heads))
    quarter = rows // share
    exchange = tensor if blocks % tensor == 0 else 1
    raise_up = [(i, i + 1) for i in range(stores - 1)]
    raise_down = [(i + 1, i) for i in range(stores - 1)]
    pairs = lambda m: [(t, t ^ m) for t in range(tensor)]

    shifted = [adapter_per_block] + [
        lax.ppermute(adapter_per_block, "store", [(i, (i + m) % stores) for i in range(stores)])
        for m in range(1, stores)
    ]
    down = jnp.swapaxes(down_factors, 1, 2)
    plan, most = make_plan(shifted, stores, blocks, per_store, slots)

    cache = jnp.swapaxes(key_value_cache, 0, 1)
    cache = lax.dynamic_index_in_dim(cache, member * heads // GROUP, 0, keepdims=False)
    my_quarter = lax.dynamic_slice_in_dim(cache, lax.rem(member, share) * quarter, quarter, 0)
    my_quarter, token_segment, *_ = lax.optimization_barrier(
        (my_quarter, token_segment, *shifted)
    )
    later = lambda v, hop: lax.ppermute(v, "store", [(i, i + hop) for i in range(stores - hop)])
    quarters = jnp.stack([later(my_quarter, hop) for hop in range(1, hops + 1)])
    earlier = [later(token_segment, hop) for hop in range(1, hops + 1)]

    def fetch(first, last, ups, downs, plan):
        sent_up, sent_down = [], []
        head = max(0, min(LAG, last) - first)
        if head:
            sent_up, sent_down = pack(plan, down, up_factors, [], [], range(head), slots)
            sent_up, sent_down = list(sent_up), list(sent_down)
        ups, downs = list(ups), list(downs)
        for k in range(first, last):
            if k >= LAG:
                got = k - LAG + 1
                u, d = pack(plan, down, up_factors, ups[:got], downs[:got], [k], slots)
                sent_up += u
                sent_down += d
            ups.append(lax.ppermute(sent_up[k - first], "store", raise_up))
            downs.append(lax.ppermute(sent_down[k - first], "store", raise_down))
        return ups, downs

    ups, downs = fetch(0, usual, [], [], plan)
    base = lax.dot_general(
        query_weight, normed_input, (((0,), (1,)), ((), ())), preferred_element_type=jnp.float32
    )
    pieces = [quarters] + [lax.ppermute(quarters, "tensor", pairs(m)) for m in range(1, share)]
    names = jnp.concatenate([s.reshape(-1, BLOCK) for s in earlier[::-1] + [token_segment]])
    keys, values, starts, firsts = window(pieces, cache, names, hops, share, CHUNK)

    def finish(ups, downs, plan):
        parts, selected = low_rank_parts(
            plan, normed_input, down, up_factors, ups, downs, slots, exchange, blocks
        )
        if exchange > 1:
            total = parts[0]
            for m in range(1, tensor):
                total = total + lax.ppermute(parts[m], "tensor", pairs(m))
            total = total.astype(jnp.bfloat16)
            low = [total] + [lax.ppermute(total, "tensor", pairs(m)) for m in range(1, tensor)]
        else:
            low = [lax.psum(parts[0], "tensor").astype(jnp.bfloat16)]
        return attention(firsts, base, starts, keys, values, selected, low, hops, CHUNK, heads)

    usually = finish(ups, downs, plan)
    if usual == slots:
        return usually
    count = most[0]
    for m in range(1, groups):
        other = lax.ppermute(most, "groups", [(g, (g + m) % groups) for g in range(groups)])
        count = jnp.maximum(count, other[0])

    def with_all(plan, ups, downs, usually):
        return finish(*fetch(usual, slots, ups, downs, plan), plan)

    return lax.cond(
        count > usual, with_all, lambda plan, ups, downs, usually: usually, plan, ups, downs, usually
    )


def solution(mesh):
    return jax.shard_map(
        functools.partial(per_device, dict(mesh.shape)),
        mesh=mesh,
        in_specs=(
            P(("groups", "store"), None),
            P(None, "tensor"),
            P("store", "tensor", None),
            P("store", None, "tensor"),
            P(("groups", "store")),
            P(("groups", "store"), None, None),
            P(("groups", "store")),
        ),
        out_specs=P(("groups", "store"), "tensor"),
        check_vma=False,
    )
```

```python
import functools
import math

import jax
import jax.numpy as jnp
from jax import lax
from jax.experimental import pallas as pl
from jax.experimental.pallas import tpu as pltpu
from jax.sharding import PartitionSpec as P

HEAD_SIZE = 128
GROUP = 8
BLOCK = 128
ADAPTERS = 64
SEGMENTS = 4
LAG = 2
USUAL_SLOTS = 10
CHUNK = 512
MIB = 1 << 20
ANY = pl.BlockSpec(memory_space=pl.ANY)
SMEM = pl.BlockSpec(memory_space=pltpu.SMEM)
VMEM = pl.BlockSpec(memory_space=pltpu.VMEM)


def slot_bound(stores, per_store, blocks):
    load = max(
        min(per_store * (link + 1), blocks * (stores - 1 - link)) for link in range(stores - 1)
    )
    return load + (stores - 2) * LAG


def plan_kernel(stores, blocks, per_store, slots, *refs):
    index_refs = refs[:stores]
    plan, most_ref = refs[stores : stores + 2]
    names, place, listed, bases, counts = refs[stores + 2 :]
    capacity = per_store + 1
    my_store = lax.axis_index("store")
    zero = jnp.int32(0)
    for shift in range(stores):
        origin = lax.rem(my_store + stores - shift, stores)
        for b in range(blocks):
            names[origin * blocks + b] = index_refs[shift][b]
    for i in range(2 * ADAPTERS):
        place[i] = jnp.int32(-1)
    for i in range(2 * slots):
        plan[1 + i] = zero
    most = zero
    for way in range(2):
        count = [zero] * stores
        crossing = [[zero] * stores for _ in range(stores)]
        for dest in range(stores - 1, 0, -1):
            real = dest if way == 0 else stores - 1 - dest
            for b in range(blocks):
                name = names[real * blocks + b]
                owner = lax.div(name, jnp.int32(per_store))
                if way == 1:
                    owner = stores - 1 - owner
                held = place[way * ADAPTERS + name]
                new = (owner < dest) & (held < 0)
                at = zero
                for o in range(stores):
                    at = jnp.where(owner == o, count[o], at)
                listed[(way * stores + owner) * capacity + at] = name
                place[way * ADAPTERS + name] = jnp.where(new, at, held)
                step = new.astype(jnp.int32)
                for o in range(dest):
                    count[o] = count[o] + jnp.where(owner == o, step, 0)
            for o in range(dest):
                crossing[o][dest - 1] = count[o]
        base = [[zero] * stores for _ in range(stores)]
        for link in range(stores):
            cursor = zero
            for o in range(stores):
                spot = (way * stores + link) * stores + o
                bases[spot] = zero
                counts[spot] = zero
            if link == stores - 1:
                continue
            for o in range(link, -1, -1):
                start = cursor if o == link else jnp.maximum(cursor, base[link - 1][o] + LAG)
                base[link][o] = start
                number = crossing[o][link]
                spot = (way * stores + link) * stores + o
                bases[spot] = start
                counts[spot] = number
                cursor = jnp.where(number > 0, start + number, cursor)
            most = jnp.maximum(most, cursor)
    plan[0] = most
    for i in range(8):
        most_ref[i] = most
    for way in range(2):
        mine = my_store if way == 0 else stores - 1 - my_store
        for o in range(stores - 1):
            spot = (way * stores + mine) * stores + o
            before = (way * stores + jnp.maximum(mine - 1, 0)) * stores + o
            start = bases[spot]
            earlier = bases[before]
            row = (way * stores + o) * capacity

            def fill(r, _):
                own = listed[row + r] - my_store * per_store
                plan[1 + way * slots + start + r] = jnp.where(
                    mine == o, own, per_store + way * slots + earlier + r
                )
                return 0

            lax.fori_loop(0, counts[spot], fill, 0)
    for b in range(blocks):
        name = names[my_store * blocks + b]
        owner = lax.div(name, jnp.int32(per_store))
        source = name - my_store * per_store
        for way in range(2):
            mine = my_store if way == 0 else stores - 1 - my_store
            far = owner if way == 0 else stores - 1 - owner
            spot = (way * stores + jnp.maximum(mine - 1, 0)) * stores + far
            arrives = per_store + way * slots + bases[spot] + place[way * ADAPTERS + name]
            source = jnp.where(far < mine, arrives, source)
        plan[1 + 2 * slots + b] = source


def make_plan(shifted, stores, blocks, per_store, slots):
    return pl.pallas_call(
        functools.partial(plan_kernel, stores, blocks, per_store, slots),
        out_shape=[
            jax.ShapeDtypeStruct((1 + 2 * slots + blocks,), jnp.int32),
            jax.ShapeDtypeStruct((8,), jnp.int32),
        ],
        in_specs=[SMEM] * len(shifted),
        out_specs=[SMEM, SMEM],
        scratch_shapes=[
            pltpu.SMEM((stores * blocks,), jnp.int32),
            pltpu.SMEM((2 * ADAPTERS,), jnp.int32),
            pltpu.SMEM((2 * stores * (per_store + 1),), jnp.int32),
            pltpu.SMEM((2 * stores * stores,), jnp.int32),
            pltpu.SMEM((2 * stores * stores,), jnp.int32),
        ],
        name="plan",
    )(*shifted)


def pack_kernel(slots, per_store, which, received, plan, down, up, *refs):
    got = [refs[:received], refs[received : 2 * received]]
    out = refs[2 * received : 2 * received + 2 * len(which)]
    sems = refs[-1]
    width = down.shape[2]

    def copies(way, i):
        source = plan[1 + way * slots + which[i]]
        dst = out[way * len(which) + i]
        sem = sems.at[way * len(which) + i]
        own = jnp.minimum(source, per_store - 1)
        pairs = [
            (
                source < per_store,
                [
                    pltpu.make_async_copy(down.at[own], dst.at[:, pl.ds(0, width)], sem),
                    pltpu.make_async_copy(
                        up.at[own], dst.at[:, pl.ds(width, up.shape[2])], sem
                    ),
                ],
            )
        ]
        for j in range(received):
            pairs.append(
                (
                    source == per_store + way * slots + j,
                    [pltpu.make_async_copy(got[way][j], dst, sem)],
                )
            )
        return pairs

    for act in ("start", "wait"):
        for way in range(2):
            for i in range(len(which)):
                for chosen, moves in copies(way, i):

                    @pl.when(chosen)
                    def _():
                        for move in moves:
                            getattr(move, act)()


def pack(plan, down, up, ups, downs, which, slots):
    per_store, rank, width = down.shape
    item = jax.ShapeDtypeStruct((rank, width + up.shape[2]), down.dtype)
    made = 2 * len(which)
    out = pl.pallas_call(
        functools.partial(pack_kernel, slots, per_store, tuple(which), len(ups)),
        out_shape=[item] * made,
        in_specs=[SMEM] + [ANY] * (2 + 2 * len(ups)),
        out_specs=[VMEM] * made,
        scratch_shapes=[pltpu.SemaphoreType.DMA((made,))],
        compiler_params=pltpu.CompilerParams(vmem_limit_bytes=16 * MIB),
        cost_estimate=pl.CostEstimate(
            flops=5 * 10**8, bytes_accessed=made * 4 * math.prod(item.shape), transcendentals=0
        ),
        name="pack",
    )(plan, down, up, *ups, *downs)
    return out[: len(which)], out[len(which) :]


def low_rank_kernel(slots, per_store, former, received, tensor, plan, x, down, up, *refs):
    earlier = refs[: tensor + 1] if former is not None else ()
    refs = refs[len(earlier) :]
    got = refs[: 2 * received]
    outs = refs[2 * received : 2 * received + tensor]
    selected, x_rows, factors, sems = refs[2 * received + tensor :]
    blocks, rank, width = factors.shape
    share = blocks // tensor
    member = lax.axis_index("tensor")
    columns = pl.ds(pl.multiple_of(member * width, 128), width)
    if tensor == 1:
        member = 0

    def within(source, number):
        return (source < per_store + number) | (
            (source >= per_store + slots) & (source < per_store + slots + number)
        )

    def due(b):
        source = plan[1 + 2 * slots + b]
        if former is None:
            return within(source, received)
        return jnp.logical_not(within(source, former))

    def copies(b):
        source = plan[1 + 2 * slots + b]
        source = jnp.where(within(source, received), source, 0)
        own = jnp.minimum(source, per_store - 1)
        pairs = [
            (
                source < per_store,
                [
                    pltpu.make_async_copy(down.at[own], factors.at[b], sems.at[b]),
                    pltpu.make_async_copy(up.at[own], selected.at[b], sems.at[b]),
                ],
            )
        ]
        for j in range(2 * received):
            spot = j if j < received else slots + j - received
            pairs.append(
                (
                    source == per_store + spot,
                    [
                        pltpu.make_async_copy(
                            got[j].at[:, pl.ds(0, width)], factors.at[b], sems.at[b]
                        ),
                        pltpu.make_async_copy(
                            got[j].at[:, pl.ds(width, up.shape[2])], selected.at[b], sems.at[b]
                        ),
                    ],
                )
            )
        return pairs

    def rows_of(b):
        rows = pl.ds(pl.multiple_of(b * BLOCK, BLOCK), BLOCK)
        return pltpu.make_async_copy(x.at[rows, columns], x_rows.at[b], sems.at[blocks + b])

    if former is not None:
        selected[...] = earlier[tensor][...]
    else:
        selected[...] = jnp.zeros_like(selected)

    def start(b, _):
        @pl.when(due(b))
        def _():
            rows_of(b).start()
            for chosen, moves in copies(b):

                @pl.when(chosen)
                def _():
                    for move in moves:
                        move.start()

        return 0

    lax.fori_loop(0, blocks, start, 0)
    for m in range(tensor):
        for i in range(share):
            b = (member ^ m) * share + i
            wanted = due(b)

            @pl.when(wanted)
            def _():
                pltpu.make_async_copy(down.at[0], factors.at[b], sems.at[b]).wait()
                pltpu.make_async_copy(up.at[0], selected.at[b], sems.at[b]).wait()
                rows_of(b).wait()
                outs[m][i] = lax.dot_general(
                    x_rows[b],
                    factors[b],
                    (((1,), (1,)), ((), ())),
                    preferred_element_type=jnp.float32,
                ).T

            @pl.when(jnp.logical_not(wanted))
            def _():
                if former is not None:
                    outs[m][i] = earlier[m][i]
                else:
                    outs[m][i] = jnp.zeros(outs[m].shape[1:], jnp.float32)


def low_rank_parts(plan, x, down, up, ups, downs, slots, tensor, blocks, former=None, earlier=()):
    per_store, rank, width = down.shape
    share = blocks // tensor
    return pl.pallas_call(
        functools.partial(low_rank_kernel, slots, per_store, former, len(ups), tensor),
        out_shape=[jax.ShapeDtypeStruct((share, rank, BLOCK), jnp.float32)] * tensor
        + [jax.ShapeDtypeStruct((blocks, rank, up.shape[2]), up.dtype)],
        in_specs=[SMEM] + [ANY] * 3 + [VMEM] * len(earlier) + [ANY] * (2 * len(ups)),
        out_specs=[VMEM] * (tensor + 1),
        scratch_shapes=[
            pltpu.VMEM((blocks, BLOCK, width), x.dtype),
            pltpu.VMEM((blocks, rank, width), down.dtype),
            pltpu.SemaphoreType.DMA((2 * blocks,)),
        ],
        compiler_params=pltpu.CompilerParams(vmem_limit_bytes=24 * MIB),
        cost_estimate=pl.CostEstimate(
            flops=2 * blocks * BLOCK * rank * width,
            bytes_accessed=2 * blocks * width * (BLOCK + rank),
            transcendentals=0,
        ),
        name="low_rank",
    )(plan, x, down, up, *earlier, *ups, *downs)


def window_kernel(hops, share, pad, *refs):
    pieces = refs[:share]
    own, segments, keys, values, starts, firsts, buffer, sems = refs[share:]
    rows = own.shape[0]
    part = rows // share
    member = lax.rem(lax.axis_index("tensor"), share)
    moves = [
        pltpu.make_async_copy(own, buffer.at[pl.ds(hops * rows, rows)], sems.at[hops * share])
    ]
    for hop in range(hops):
        for m in range(share):
            at = pl.multiple_of((hops - 1 - hop) * rows + (member ^ m) * part, part)
            moves.append(
                pltpu.make_async_copy(
                    pieces[m].at[hop], buffer.at[pl.ds(at, part)], sems.at[hop * share + m]
                )
            )
    for move in moves:
        move.start()
    store = lax.axis_index("store")
    names = segments[...]
    mine = names[hops * (rows // BLOCK) :]
    empty = jnp.maximum(hops - store, 0) * rows
    start = jnp.zeros(mine.shape, jnp.int32) + empty
    for value in range(1, SEGMENTS):
        number = jnp.sum((names < value).astype(jnp.float32)).astype(jnp.int32)
        start = jnp.where(mine == value, jnp.maximum(number, empty), start)
    starts[...] = start.reshape(starts.shape)
    for j in range(mine.shape[0]):
        firsts[j] = jnp.min(start[j : j + 1].astype(jnp.float32)).astype(jnp.int32)
    for move in moves:
        move.wait()
    keys[pl.ds(0, pad), :] = jnp.zeros((pad, HEAD_SIZE), keys.dtype)
    values[:, pl.ds(0, pad)] = jnp.zeros((HEAD_SIZE, pad), values.dtype)

    def turn(c, _):
        at = pl.ds(pl.multiple_of(c * 256, 256), 256)
        to = pl.ds(pl.multiple_of(pad + c * 256, 256), 256)
        keys[to, :] = buffer[at, pl.ds(0, HEAD_SIZE)]
        values[:, to] = buffer[at, pl.ds(HEAD_SIZE, HEAD_SIZE)].astype(jnp.float32).T.astype(
            values.dtype
        )
        return 0

    lax.fori_loop(0, (hops + 1) * rows // 256, turn, 0)


def window(pieces, own, segments, hops, share, pad):
    rows = own.shape[0]
    length = pad + (hops + 1) * rows
    return pl.pallas_call(
        functools.partial(window_kernel, hops, share, pad),
        out_shape=[
            jax.ShapeDtypeStruct((length, HEAD_SIZE), own.dtype),
            jax.ShapeDtypeStruct((HEAD_SIZE, length), own.dtype),
            jax.ShapeDtypeStruct((rows // BLOCK, 1, BLOCK), jnp.int32),
            jax.ShapeDtypeStruct((rows // BLOCK,), jnp.int32),
        ],
        in_specs=[ANY] * (share + 1) + [VMEM],
        out_specs=[VMEM, VMEM, VMEM, SMEM],
        scratch_shapes=[
            pltpu.VMEM(((hops + 1) * rows, 2 * HEAD_SIZE), own.dtype),
            pltpu.SemaphoreType.DMA((hops * share + 1,)),
        ],
        compiler_params=pltpu.CompilerParams(vmem_limit_bytes=24 * MIB),
        cost_estimate=pl.CostEstimate(
            flops=0, bytes_accessed=8 * length * HEAD_SIZE, transcendentals=0
        ),
        name="window",
    )(*pieces, own, segments)


def attention_kernel(
    hops, tensor, pad, heads, firsts, base, starts, keys, values, selected, *refs
):
    ranks = refs[:tensor]
    out, even, odd, even_largest, odd_largest, top, total, summed, queries = refs[tensor:]
    j = pl.program_id(0)
    share = ranks[0].shape[0]
    member = lax.axis_index("tensor") if tensor > 1 else 0
    rows = (keys.shape[0] - pad) // (hops + 1)
    low = jnp.zeros(ranks[0].shape[1:], jnp.bfloat16)
    for m in range(tensor):
        for i in range(share):
            low = jnp.where(j == (member ^ m) * share + i, ranks[m][i], low)
    term = lax.dot_general(
        selected[0], low, (((0,), (0,)), ((), ())), preferred_element_type=jnp.float32
    )
    turned = (base[...] + term).astype(jnp.bfloat16)
    for h in range(heads):
        queries[:, h * BLOCK : (h + 1) * BLOCK] = turned[h * HEAD_SIZE : (h + 1) * HEAD_SIZE]
    q = queries[...]
    columns = heads * BLOCK
    start = jnp.concatenate([starts[0]] * heads, axis=1) + pad
    end = pad + hops * rows + (j + 1) * BLOCK
    steps = lax.div(end - pad - firsts[j] + CHUNK - 1, jnp.int32(CHUNK))
    scale = HEAD_SIZE**-0.5 * math.log2(math.e)
    key = lax.broadcasted_iota(jnp.int32, (CHUNK, columns), 0)

    def place_of(c):
        return pl.multiple_of(jnp.maximum(end - (c + 1) * CHUNK, 0), BLOCK)

    def score(c, buffer, largest, diagonal):
        at = place_of(c)
        s = jnp.dot(keys[pl.ds(at, CHUNK), :], q, preferred_element_type=jnp.float32)
        allowed = key >= start - at
        if diagonal:
            token = lax.rem(lax.broadcasted_iota(jnp.int32, (1, columns), 1), BLOCK)
            allowed = allowed & (key <= token + (CHUNK - BLOCK))
        s = jnp.where(allowed, s, jnp.float32(-1e30))
        buffer[...] = s
        largest[...] = jnp.max(s.reshape(CHUNK // 8, 8, columns), axis=0)

    def weigh(c, buffer, largest):
        before = top[...]
        now = jnp.maximum(before, jnp.max(largest[...], axis=0, keepdims=True))
        top[...] = now
        fade = jnp.exp2((before - now) * scale)
        w = jnp.exp2((buffer[...] - now) * scale)
        total[...] = total[...] * fade + jnp.sum(w.reshape(CHUNK // 8, 8, columns), axis=0)
        summed[...] = summed[...] * fade + jnp.dot(
            values[:, pl.ds(place_of(c), CHUNK)],
            w.astype(jnp.bfloat16),
            preferred_element_type=jnp.float32,
        )

    top[...] = jnp.full(top.shape, -1e30, jnp.float32)
    total[...] = jnp.zeros(total.shape, jnp.float32)
    summed[...] = jnp.zeros(summed.shape, jnp.float32)
    score(0, even, even_largest, True)

    def two(i, _):
        score(2 * i + 1, odd, odd_largest, False)
        weigh(2 * i, even, even_largest)

        @pl.when(2 * i + 1 < steps)
        def _():
            score(2 * i + 2, even, even_largest, False)
            weigh(2 * i + 1, odd, odd_largest)

        return 0

    lax.fori_loop(0, lax.div(steps + 1, jnp.int32(2)), two, 0)
    attended = summed[...] / jnp.sum(total[...], axis=0, keepdims=True)
    for h in range(heads):
        out[:, h * HEAD_SIZE : (h + 1) * HEAD_SIZE] = (
            attended[:, h * BLOCK : (h + 1) * BLOCK].T.astype(out.dtype)
        )


def attention(firsts, base, starts, keys, values, selected, ranks, hops, pad, heads):
    columns, rows = base.shape
    blocks = rows // BLOCK
    length = keys.shape[0]
    whole = lambda shape: pl.BlockSpec(shape, lambda j, *_: (0,) * len(shape))
    return pl.pallas_call(
        functools.partial(attention_kernel, hops, len(ranks), pad, heads),
        out_shape=jax.ShapeDtypeStruct((rows, columns), jnp.bfloat16),
        grid_spec=pltpu.PrefetchScalarGridSpec(
            num_scalar_prefetch=1,
            grid=(blocks,),
            in_specs=[
                pl.BlockSpec((columns, BLOCK), lambda j, *_: (0, j)),
                pl.BlockSpec((1, 1, BLOCK), lambda j, *_: (j, 0, 0)),
                whole(keys.shape),
                whole(values.shape),
                pl.BlockSpec((1,) + selected.shape[1:], lambda j, *_: (j, 0, 0)),
            ]
            + [whole(r.shape) for r in ranks],
            out_specs=pl.BlockSpec((BLOCK, columns), lambda j, *_: (j, 0)),
            scratch_shapes=[
                pltpu.VMEM((CHUNK, heads * BLOCK), jnp.float32),
                pltpu.VMEM((CHUNK, heads * BLOCK), jnp.float32),
                pltpu.VMEM((8, heads * BLOCK), jnp.float32),
                pltpu.VMEM((8, heads * BLOCK), jnp.float32),
                pltpu.VMEM((1, heads * BLOCK), jnp.float32),
                pltpu.VMEM((8, heads * BLOCK), jnp.float32),
                pltpu.VMEM((HEAD_SIZE, heads * BLOCK), jnp.float32),
                pltpu.VMEM((HEAD_SIZE, heads * BLOCK), jnp.bfloat16),
            ],
        ),
        compiler_params=pltpu.CompilerParams(vmem_limit_bytes=40 * MIB),
        cost_estimate=pl.CostEstimate(
            flops=2 * rows * columns * length,
            bytes_accessed=8 * length * HEAD_SIZE,
            transcendentals=rows * heads * length,
        ),
        name="attention",
    )(firsts, base, starts, keys, values, selected, *ranks)


def per_device(
    mesh_shape,
    normed_input,
    query_weight,
    down_factors,
    up_factors,
    adapter_per_block,
    key_value_cache,
    token_segment,
):
    groups, tensor, stores = (mesh_shape[a] for a in ("groups", "tensor", "store"))
    rows = normed_input.shape[0]
    blocks = adapter_per_block.shape[0]
    heads = query_weight.shape[1] // HEAD_SIZE
    per_store = down_factors.shape[0]
    member = lax.axis_index("tensor")
    slots = slot_bound(stores, per_store, blocks)
    usual = min(slots, USUAL_SLOTS)
    hops = min(stores - 1, -(-(stores * rows // 2 - 1) // rows))
    share = min(tensor, max(1, GROUP // heads))
    quarter = rows // share
    exchange = tensor if blocks % tensor == 0 else 1
    raise_up = [(i, i + 1) for i in range(stores - 1)]
    raise_down = [(i + 1, i) for i in range(stores - 1)]
    pairs = lambda m: [(t, t ^ m) for t in range(tensor)]

    shifted = [adapter_per_block] + [
        lax.ppermute(adapter_per_block, "store", [(i, (i + m) % stores) for i in range(stores)])
        for m in range(1, stores)
    ]
    down = jnp.swapaxes(down_factors, 1, 2)
    plan, most = make_plan(shifted, stores, blocks, per_store, slots)

    cache = jnp.swapaxes(key_value_cache, 0, 1)
    cache = lax.dynamic_index_in_dim(cache, member * heads // GROUP, 0, keepdims=False)
    my_quarter = lax.dynamic_slice_in_dim(cache, lax.rem(member, share) * quarter, quarter, 0)
    my_quarter, token_segment, *_ = lax.optimization_barrier(
        (my_quarter, token_segment, *shifted)
    )
    later = lambda v, hop: lax.ppermute(v, "store", [(i, i + hop) for i in range(stores - hop)])
    quarters = jnp.stack([later(my_quarter, hop) for hop in range(1, hops + 1)])
    earlier = [later(token_segment, hop) for hop in range(1, hops + 1)]

    def fetch(first, last, ups, downs, plan, beside):
        sent_up, sent_down = [], []
        head = max(0, min(LAG, last) - first)
        if head:
            sent_up, sent_down = pack(plan, down, up_factors, [], [], range(head), slots)
            sent_up, sent_down = list(sent_up), list(sent_down)
        ups, downs = list(ups), list(downs)
        for k in range(first, last):
            if k in beside:
                plan, *_ = lax.optimization_barrier((plan, *beside[k](plan, ups, downs)))
            if k >= LAG:
                got = k - LAG + 1
                u, d = pack(plan, down, up_factors, ups[:got], downs[:got], [k], slots)
                plan, *ud = lax.optimization_barrier((plan, *u, *d))
                sent_up += ud[:1]
                sent_down += ud[1:]
            ups.append(lax.ppermute(sent_up[k - first], "store", raise_up))
            downs.append(lax.ppermute(sent_down[k - first], "store", raise_down))
        return ups, downs

    base = lax.dot_general(
        query_weight, normed_input, (((0,), (1,)), ((), ())), preferred_element_type=jnp.float32
    )
    pieces = [quarters] + [lax.ppermute(quarters, "tensor", pairs(m)) for m in range(1, share)]
    names = jnp.concatenate([s.reshape(-1, BLOCK) for s in earlier[::-1] + [token_segment]])
    keys, values, starts, firsts = window(pieces, cache, names, hops, share, CHUNK)
    former = max(0, usual - 4)
    earlier_parts = []

    def early_parts(plan, ups, downs):
        earlier_parts[:] = low_rank_parts(
            plan,
            normed_input,
            down,
            up_factors,
            ups[:former],
            downs[:former],
            slots,
            exchange,
            blocks,
        )
        return earlier_parts

    beside = {
        3: lambda *_: (quarters, *earlier),
        7: lambda *_: (keys, values, starts, firsts),
        usual - 2: early_parts,
    }
    ups, downs = fetch(0, usual, [], [], plan, beside)
    plan, base, keys, values, starts, firsts = lax.optimization_barrier(
        (plan, base, keys, values, starts, firsts)
    )

    def finish(ups, downs, plan):
        *parts, selected = low_rank_parts(
            plan,
            normed_input,
            down,
            up_factors,
            ups,
            downs,
            slots,
            exchange,
            blocks,
            former,
            earlier_parts,
        )
        if exchange > 1:
            total = parts[0]
            for m in range(1, tensor):
                total = total + lax.ppermute(parts[m], "tensor", pairs(m))
            total = total.astype(jnp.bfloat16)
            low = [total] + [lax.ppermute(total, "tensor", pairs(m)) for m in range(1, tensor)]
        else:
            low = [lax.psum(parts[0], "tensor").astype(jnp.bfloat16)]
        return attention(firsts, base, starts, keys, values, selected, low, hops, CHUNK, heads)

    usually = finish(ups, downs, plan)
    if usual == slots:
        return usually
    count = most[0]
    for m in range(1, groups):
        other = lax.ppermute(most, "groups", [(g, (g + m) % groups) for g in range(groups)])
        count = jnp.maximum(count, other[0])

    def with_all(plan, ups, downs, usually):
        return finish(*fetch(usual, slots, ups, downs, plan, {}), plan)

    return lax.cond(
        count > usual, with_all, lambda plan, ups, downs, usually: usually, plan, ups, downs, usually
    )


def solution(mesh):
    return jax.shard_map(
        functools.partial(per_device, dict(mesh.shape)),
        mesh=mesh,
        in_specs=(
            P(("groups", "store"), None),
            P(None, "tensor"),
            P("store", "tensor", None),
            P("store", None, "tensor"),
            P(("groups", "store")),
            P(("groups", "store"), None, None),
            P(("groups", "store")),
        ),
        out_specs=P(("groups", "store"), "tensor"),
        check_vma=False,
    )
```

```python
import functools
import math

import jax
import jax.numpy as jnp
from jax import lax
from jax.experimental import pallas as pl
from jax.experimental.pallas import tpu as pltpu
from jax.sharding import PartitionSpec as P

HEAD_SIZE = 128
GROUP = 8
BLOCK = 128
ADAPTERS = 64
SEGMENTS = 4
LAG = 2
USUAL_SLOTS = 10
CHUNK = 512
MIB = 1 << 20
ANY = pl.BlockSpec(memory_space=pl.ANY)
SMEM = pl.BlockSpec(memory_space=pltpu.SMEM)
VMEM = pl.BlockSpec(memory_space=pltpu.VMEM)


def slot_bound(stores, per_store, blocks):
    load = max(
        min(per_store * (link + 1), blocks * (stores - 1 - link)) for link in range(stores - 1)
    )
    return load + (stores - 2) * LAG


def plan_kernel(stores, blocks, per_store, slots, *refs):
    index_refs = refs[:stores]
    plan, names, place, listed, bases, counts = refs[stores:]
    capacity = per_store + 1
    my_store = lax.axis_index("store")
    zero = jnp.int32(0)
    for shift in range(stores):
        origin = lax.rem(my_store + stores - shift, stores)
        for b in range(blocks):
            names[origin * blocks + b] = index_refs[shift][index_refs[shift].shape[0] - 1, b]
    for i in range(2 * ADAPTERS):
        place[i] = jnp.int32(-1)
    for i in range(2 * slots):
        plan[1 + i] = zero
    most = zero
    for way in range(2):
        count = [zero] * stores
        crossing = [[zero] * stores for _ in range(stores)]
        for dest in range(stores - 1, 0, -1):
            real = dest if way == 0 else stores - 1 - dest
            for b in range(blocks):
                name = names[real * blocks + b]
                owner = lax.div(name, jnp.int32(per_store))
                if way == 1:
                    owner = stores - 1 - owner
                held = place[way * ADAPTERS + name]
                new = (owner < dest) & (held < 0)
                at = zero
                for o in range(stores):
                    at = jnp.where(owner == o, count[o], at)
                listed[(way * stores + owner) * capacity + at] = name
                place[way * ADAPTERS + name] = jnp.where(new, at, held)
                step = new.astype(jnp.int32)
                for o in range(dest):
                    count[o] = count[o] + jnp.where(owner == o, step, 0)
            for o in range(dest):
                crossing[o][dest - 1] = count[o]
        base = [[zero] * stores for _ in range(stores)]
        for link in range(stores):
            cursor = zero
            for o in range(stores):
                spot = (way * stores + link) * stores + o
                bases[spot] = zero
                counts[spot] = zero
            if link == stores - 1:
                continue
            for o in range(link, -1, -1):
                start = cursor if o == link else jnp.maximum(cursor, base[link - 1][o] + LAG)
                base[link][o] = start
                number = crossing[o][link]
                spot = (way * stores + link) * stores + o
                bases[spot] = start
                counts[spot] = number
                cursor = jnp.where(number > 0, start + number, cursor)
            most = jnp.maximum(most, cursor)
    plan[0] = most
    for way in range(2):
        mine = my_store if way == 0 else stores - 1 - my_store
        for o in range(stores - 1):
            spot = (way * stores + mine) * stores + o
            before = (way * stores + jnp.maximum(mine - 1, 0)) * stores + o
            start = bases[spot]
            earlier = bases[before]
            row = (way * stores + o) * capacity

            def fill(r, _):
                own = listed[row + r] - my_store * per_store
                plan[1 + way * slots + start + r] = jnp.where(
                    mine == o, own, per_store + way * slots + earlier + r
                )
                return 0

            lax.fori_loop(0, counts[spot], fill, 0)
    for b in range(blocks):
        name = names[my_store * blocks + b]
        owner = lax.div(name, jnp.int32(per_store))
        source = name - my_store * per_store
        for way in range(2):
            mine = my_store if way == 0 else stores - 1 - my_store
            far = owner if way == 0 else stores - 1 - owner
            spot = (way * stores + jnp.maximum(mine - 1, 0)) * stores + far
            arrives = per_store + way * slots + bases[spot] + place[way * ADAPTERS + name]
            source = jnp.where(far < mine, arrives, source)
        plan[1 + 2 * slots + b] = source


def make_plan(shifted, stores, blocks, per_store, slots):
    return pl.pallas_call(
        functools.partial(plan_kernel, stores, blocks, per_store, slots),
        out_shape=jax.ShapeDtypeStruct((1 + 2 * slots + blocks,), jnp.int32),
        in_specs=[SMEM] * len(shifted),
        out_specs=SMEM,
        scratch_shapes=[
            pltpu.SMEM((stores * blocks,), jnp.int32),
            pltpu.SMEM((2 * ADAPTERS,), jnp.int32),
            pltpu.SMEM((2 * stores * (per_store + 1),), jnp.int32),
            pltpu.SMEM((2 * stores * stores,), jnp.int32),
            pltpu.SMEM((2 * stores * stores,), jnp.int32),
        ],
        name="plan",
    )(*shifted)


def pack_kernel(slots, per_store, which, received, plan, down, up, *refs):
    got = [refs[:received], refs[received : 2 * received]]
    out = refs[2 * received : 2 * received + 2 * len(which)]
    sems = refs[-1]
    width = down.shape[2]

    def copies(way, i):
        source = plan[1 + way * slots + which[i]]
        dst = out[way * len(which) + i]
        sem = sems.at[way * len(which) + i]
        own = jnp.minimum(source, per_store - 1)
        pairs = [
            (
                source < per_store,
                [
                    pltpu.make_async_copy(down.at[own], dst.at[:, pl.ds(0, width)], sem),
                    pltpu.make_async_copy(
                        up.at[own], dst.at[:, pl.ds(width, up.shape[2])], sem
                    ),
                ],
            )
        ]
        for j in range(received):
            pairs.append(
                (
                    source == per_store + way * slots + j,
                    [pltpu.make_async_copy(got[way][j], dst, sem)],
                )
            )
        return pairs

    for act in ("start", "wait"):
        for way in range(2):
            for i in range(len(which)):
                for chosen, moves in copies(way, i):

                    @pl.when(chosen)
                    def _():
                        for move in moves:
                            getattr(move, act)()


def pack(plan, down, up, ups, downs, which, slots):
    per_store, rank, width = down.shape
    item = jax.ShapeDtypeStruct((rank, width + up.shape[2]), down.dtype)
    made = 2 * len(which)
    out = pl.pallas_call(
        functools.partial(pack_kernel, slots, per_store, tuple(which), len(ups)),
        out_shape=[item] * made,
        in_specs=[SMEM] + [ANY] * (2 + 2 * len(ups)),
        out_specs=[VMEM] * made,
        scratch_shapes=[pltpu.SemaphoreType.DMA((made,))],
        compiler_params=pltpu.CompilerParams(vmem_limit_bytes=16 * MIB),
        cost_estimate=pl.CostEstimate(
            flops=5 * 10**8, bytes_accessed=made * 4 * math.prod(item.shape), transcendentals=0
        ),
        name="pack",
    )(plan, down, up, *ups, *downs)
    return out[: len(which)], out[len(which) :]


def low_rank_kernel(slots, per_store, former, received, tensor, plan, x, down, up, *refs):
    earlier = refs[: tensor + 1] if former is not None else ()
    refs = refs[len(earlier) :]
    got = refs[: 2 * received]
    outs = refs[2 * received : 2 * received + tensor]
    selected, x_rows, factors, sems = refs[2 * received + tensor :]
    blocks, rank, width = factors.shape
    share = blocks // tensor
    member = lax.axis_index("tensor")
    columns = pl.ds(pl.multiple_of(member * width, 128), width)
    if tensor == 1:
        member = 0

    def within(source, number):
        return (source < per_store + number) | (
            (source >= per_store + slots) & (source < per_store + slots + number)
        )

    def due(b):
        source = plan[1 + 2 * slots + b]
        if former is None:
            return within(source, received)
        return jnp.logical_not(within(source, former))

    def copies(b):
        source = plan[1 + 2 * slots + b]
        source = jnp.where(within(source, received), source, 0)
        own = jnp.minimum(source, per_store - 1)
        pairs = [
            (
                source < per_store,
                [
                    pltpu.make_async_copy(down.at[own], factors.at[b], sems.at[b]),
                    pltpu.make_async_copy(up.at[own], selected.at[b], sems.at[b]),
                ],
            )
        ]
        for j in range(2 * received):
            spot = j if j < received else slots + j - received
            pairs.append(
                (
                    source == per_store + spot,
                    [
                        pltpu.make_async_copy(
                            got[j].at[:, pl.ds(0, width)], factors.at[b], sems.at[b]
                        ),
                        pltpu.make_async_copy(
                            got[j].at[:, pl.ds(width, up.shape[2])], selected.at[b], sems.at[b]
                        ),
                    ],
                )
            )
        return pairs

    def rows_of(b):
        rows = pl.ds(pl.multiple_of(b * BLOCK, BLOCK), BLOCK)
        return pltpu.make_async_copy(x.at[rows, columns], x_rows.at[b], sems.at[blocks + b])

    if former is not None:
        selected[...] = earlier[tensor][...]
    else:
        selected[...] = jnp.zeros_like(selected)

    def start(b, _):
        @pl.when(due(b))
        def _():
            rows_of(b).start()
            for chosen, moves in copies(b):

                @pl.when(chosen)
                def _():
                    for move in moves:
                        move.start()

        return 0

    lax.fori_loop(0, blocks, start, 0)
    for m in range(tensor):
        for i in range(share):
            b = (member ^ m) * share + i
            wanted = due(b)

            @pl.when(wanted)
            def _():
                pltpu.make_async_copy(down.at[0], factors.at[b], sems.at[b]).wait()
                pltpu.make_async_copy(up.at[0], selected.at[b], sems.at[b]).wait()
                rows_of(b).wait()
                outs[m][i] = lax.dot_general(
                    x_rows[b],
                    factors[b],
                    (((1,), (1,)), ((), ())),
                    preferred_element_type=jnp.float32,
                ).T

            @pl.when(jnp.logical_not(wanted))
            def _():
                if former is not None:
                    outs[m][i] = earlier[m][i]
                else:
                    outs[m][i] = jnp.zeros(outs[m].shape[1:], jnp.float32)


def low_rank_parts(plan, x, down, up, ups, downs, slots, tensor, blocks, former=None, earlier=()):
    per_store, rank, width = down.shape
    share = blocks // tensor
    return pl.pallas_call(
        functools.partial(low_rank_kernel, slots, per_store, former, len(ups), tensor),
        out_shape=[jax.ShapeDtypeStruct((share, rank, BLOCK), jnp.float32)] * tensor
        + [jax.ShapeDtypeStruct((blocks, rank, up.shape[2]), up.dtype)],
        in_specs=[SMEM] + [ANY] * 3 + [VMEM] * len(earlier) + [ANY] * (2 * len(ups)),
        out_specs=[VMEM] * (tensor + 1),
        scratch_shapes=[
            pltpu.VMEM((blocks, BLOCK, width), x.dtype),
            pltpu.VMEM((blocks, rank, width), down.dtype),
            pltpu.SemaphoreType.DMA((2 * blocks,)),
        ],
        compiler_params=pltpu.CompilerParams(vmem_limit_bytes=24 * MIB),
        cost_estimate=pl.CostEstimate(
            flops=2 * blocks * BLOCK * rank * width,
            bytes_accessed=2 * blocks * width * (BLOCK + rank),
            transcendentals=0,
        ),
        name="low_rank",
    )(plan, x, down, up, *earlier, *ups, *downs)


def window_kernel(hops, share, pad, gathered, *refs):
    number = 1 if gathered else share
    pieces = refs[:number]
    own = refs[number]
    messages = refs[number + 1 : number + 2 + hops]
    keys, values, starts, firsts, buffer, sems = refs[number + 2 + hops :]
    rows = own.shape[0]
    part = rows // share
    blocks = rows // BLOCK
    member = lax.rem(lax.axis_index("tensor"), share)
    store = lax.axis_index("store")
    first = jnp.maximum(store - hops, 0)
    mine = pltpu.make_async_copy(own, buffer.at[pl.ds(hops * rows, rows)], sems.at[hops * share])
    mine.start()

    def moves(hop):
        found = []
        for m in range(share):
            who = m if gathered else member ^ m
            piece = pieces[0].at[m * hops + hop] if gathered else pieces[m].at[hop]
            at = pl.multiple_of((hops + first + hop - store) * rows + who * part, part)
            found.append(
                pltpu.make_async_copy(
                    piece, buffer.at[pl.ds(at, part)], sems.at[hop * share + m]
                )
            )
        return found

    for hop in range(hops):

        @pl.when(first + hop < store)
        def _():
            for move in moves(hop):
                move.start()

        @pl.when(store <= hop)
        def _():
            buffer[pl.ds((hops - 1 - hop) * rows, rows), :] = jnp.zeros(
                (rows, buffer.shape[1]), buffer.dtype
            )

    empty = jnp.maximum(hops - store, 0) * rows
    names = messages[0][pl.ds(0, blocks), :]
    start = jnp.zeros(names.shape, jnp.int32) + empty
    for value in range(1, SEGMENTS):
        before = empty.astype(jnp.float32)
        for hop in range(hops + 1):
            below = (messages[hop][pl.ds(0, blocks), :] < value).astype(jnp.float32)
            before = before + jnp.where(hop <= store, jnp.sum(below), 0.0)
        start = jnp.where(names == value, before.astype(jnp.int32), start)
    starts[...] = start.reshape(starts.shape)
    for j in range(blocks):
        firsts[j] = jnp.min(start[j : j + 1].astype(jnp.float32)).astype(jnp.int32)
    mine.wait()
    for hop in range(hops):

        @pl.when(first + hop < store)
        def _():
            for move in moves(hop):
                move.wait()

    keys[pl.ds(0, pad), :] = jnp.zeros((pad, HEAD_SIZE), keys.dtype)
    values[:, pl.ds(0, pad)] = jnp.zeros((HEAD_SIZE, pad), values.dtype)

    def turn(c, _):
        at = pl.ds(pl.multiple_of(c * 256, 256), 256)
        to = pl.ds(pl.multiple_of(pad + c * 256, 256), 256)
        keys[to, :] = buffer[at, pl.ds(0, HEAD_SIZE)]
        values[:, to] = buffer[at, pl.ds(HEAD_SIZE, HEAD_SIZE)].astype(jnp.float32).T.astype(
            values.dtype
        )
        return 0

    lax.fori_loop(0, (hops + 1) * rows // 256, turn, 0)


def window(pieces, own, messages, hops, share, pad):
    rows = own.shape[0]
    length = pad + (hops + 1) * rows
    gathered = len(pieces) < share
    return pl.pallas_call(
        functools.partial(window_kernel, hops, share, pad, gathered),
        out_shape=[
            jax.ShapeDtypeStruct((length, HEAD_SIZE), own.dtype),
            jax.ShapeDtypeStruct((HEAD_SIZE, length), own.dtype),
            jax.ShapeDtypeStruct((rows // BLOCK, 1, BLOCK), jnp.int32),
            jax.ShapeDtypeStruct((rows // BLOCK,), jnp.int32),
        ],
        in_specs=[ANY] * (len(pieces) + 1) + [VMEM] * (hops + 1),
        out_specs=[VMEM, VMEM, VMEM, SMEM],
        scratch_shapes=[
            pltpu.VMEM(((hops + 1) * rows, 2 * HEAD_SIZE), own.dtype),
            pltpu.SemaphoreType.DMA((hops * share + 1,)),
        ],
        compiler_params=pltpu.CompilerParams(vmem_limit_bytes=24 * MIB),
        cost_estimate=pl.CostEstimate(
            flops=0, bytes_accessed=8 * length * HEAD_SIZE, transcendentals=0
        ),
        name="window",
    )(*pieces, own, *messages)


def base_kernel(x, weight, out, total):
    k = pl.program_id(0)
    product = jnp.dot(x[...], weight[...], preferred_element_type=jnp.float32)

    @pl.when(k == 0)
    def _():
        total[...] = product

    @pl.when(k > 0)
    def _():
        total[...] += product

    @pl.when(k == pl.num_programs(0) - 1)
    def _():
        out[...] = total[...].T


def base_queries(x, weight):
    rows, width = x.shape
    columns = weight.shape[1]
    deep = min(width, 1024)
    return pl.pallas_call(
        base_kernel,
        out_shape=jax.ShapeDtypeStruct((columns, rows), jnp.float32),
        grid=(width // deep,),
        in_specs=[
            pl.BlockSpec((rows, deep), lambda k: (0, k)),
            pl.BlockSpec((deep, columns), lambda k: (k, 0)),
        ],
        out_specs=pl.BlockSpec((columns, rows), lambda k: (0, 0)),
        scratch_shapes=[pltpu.VMEM((rows, columns), jnp.float32)],
        compiler_params=pltpu.CompilerParams(vmem_limit_bytes=24 * MIB),
        cost_estimate=pl.CostEstimate(
            flops=2 * rows * width * columns,
            bytes_accessed=2 * width * (rows + columns),
            transcendentals=0,
        ),
        name="base",
    )(x, weight)


def attention_kernel(
    hops, tensor, pad, heads, firsts, base, starts, keys, values, selected, *refs
):
    ranks = refs[:tensor]
    out, even, odd, even_largest, odd_largest, top, total, summed, queries = refs[tensor:]
    j = pl.program_id(0)
    share = ranks[0].shape[0]
    member = lax.axis_index("tensor") if tensor > 1 else 0
    rows = (keys.shape[0] - pad) // (hops + 1)
    low = jnp.zeros(ranks[0].shape[1:], jnp.bfloat16)
    for m in range(tensor):
        for i in range(share):
            low = jnp.where(j == (member ^ m) * share + i, ranks[m][i], low)
    term = lax.dot_general(
        selected[0], low, (((0,), (0,)), ((), ())), preferred_element_type=jnp.float32
    )
    turned = (base[...] + term).astype(jnp.bfloat16)
    for h in range(heads):
        queries[:, h * BLOCK : (h + 1) * BLOCK] = turned[h * HEAD_SIZE : (h + 1) * HEAD_SIZE]
    q = queries[...]
    columns = heads * BLOCK
    start = jnp.concatenate([starts[0]] * heads, axis=1) + pad
    end = pad + hops * rows + (j + 1) * BLOCK
    steps = lax.div(end - pad - firsts[j] + CHUNK - 1, jnp.int32(CHUNK))
    scale = HEAD_SIZE**-0.5 * math.log2(math.e)
    key = lax.broadcasted_iota(jnp.int32, (CHUNK, columns), 0)

    def place_of(c):
        return pl.multiple_of(jnp.maximum(end - (c + 1) * CHUNK, 0), BLOCK)

    def score(c, buffer, largest, diagonal):
        at = place_of(c)
        s = jnp.dot(keys[pl.ds(at, CHUNK), :], q, preferred_element_type=jnp.float32)
        allowed = key >= start - at
        if diagonal:
            token = lax.rem(lax.broadcasted_iota(jnp.int32, (1, columns), 1), BLOCK)
            allowed = allowed & (key <= token + (CHUNK - BLOCK))
        s = jnp.where(allowed, s, jnp.float32(-1e30))
        buffer[...] = s
        largest[...] = jnp.max(s.reshape(CHUNK // 8, 8, columns), axis=0)

    def weigh(c, buffer, largest):
        before = top[...]
        now = jnp.maximum(before, jnp.max(largest[...], axis=0, keepdims=True))
        top[...] = now
        fade = jnp.exp2((before - now) * scale)
        w = jnp.exp2((buffer[...] - now) * scale)
        total[...] = total[...] * fade + jnp.sum(w.reshape(CHUNK // 8, 8, columns), axis=0)
        summed[...] = summed[...] * fade + jnp.dot(
            values[:, pl.ds(place_of(c), CHUNK)],
            w.astype(jnp.bfloat16),
            preferred_element_type=jnp.float32,
        )

    top[...] = jnp.full(top.shape, -1e30, jnp.float32)
    total[...] = jnp.zeros(total.shape, jnp.float32)
    summed[...] = jnp.zeros(summed.shape, jnp.float32)
    score(0, even, even_largest, True)

    def two(i, _):
        score(2 * i + 1, odd, odd_largest, False)
        weigh(2 * i, even, even_largest)

        @pl.when(2 * i + 1 < steps)
        def _():
            score(2 * i + 2, even, even_largest, False)
            weigh(2 * i + 1, odd, odd_largest)

        return 0

    lax.fori_loop(0, lax.div(steps + 1, jnp.int32(2)), two, 0)
    attended = summed[...] / jnp.sum(total[...], axis=0, keepdims=True)
    for h in range(heads):
        out[:, h * HEAD_SIZE : (h + 1) * HEAD_SIZE] = (
            attended[:, h * BLOCK : (h + 1) * BLOCK].T.astype(out.dtype)
        )


def attention(firsts, base, starts, keys, values, selected, ranks, hops, pad, heads):
    columns, rows = base.shape
    blocks = rows // BLOCK
    length = keys.shape[0]
    whole = lambda shape: pl.BlockSpec(shape, lambda j, *_: (0,) * len(shape))
    return pl.pallas_call(
        functools.partial(attention_kernel, hops, len(ranks), pad, heads),
        out_shape=jax.ShapeDtypeStruct((rows, columns), jnp.bfloat16),
        grid_spec=pltpu.PrefetchScalarGridSpec(
            num_scalar_prefetch=1,
            grid=(blocks,),
            in_specs=[
                pl.BlockSpec((columns, BLOCK), lambda j, *_: (0, j)),
                pl.BlockSpec((1, 1, BLOCK), lambda j, *_: (j, 0, 0)),
                whole(keys.shape),
                whole(values.shape),
                pl.BlockSpec((1,) + selected.shape[1:], lambda j, *_: (j, 0, 0)),
            ]
            + [whole(r.shape) for r in ranks],
            out_specs=pl.BlockSpec((BLOCK, columns), lambda j, *_: (j, 0)),
            scratch_shapes=[
                pltpu.VMEM((CHUNK, heads * BLOCK), jnp.float32),
                pltpu.VMEM((CHUNK, heads * BLOCK), jnp.float32),
                pltpu.VMEM((8, heads * BLOCK), jnp.float32),
                pltpu.VMEM((8, heads * BLOCK), jnp.float32),
                pltpu.VMEM((1, heads * BLOCK), jnp.float32),
                pltpu.VMEM((8, heads * BLOCK), jnp.float32),
                pltpu.VMEM((HEAD_SIZE, heads * BLOCK), jnp.float32),
                pltpu.VMEM((HEAD_SIZE, heads * BLOCK), jnp.bfloat16),
            ],
        ),
        compiler_params=pltpu.CompilerParams(vmem_limit_bytes=40 * MIB),
        cost_estimate=pl.CostEstimate(
            flops=2 * rows * columns * length,
            bytes_accessed=8 * length * HEAD_SIZE,
            transcendentals=rows * heads * length,
        ),
        name="attention",
    )(firsts, base, starts, keys, values, selected, *ranks)


def per_device(
    mesh_shape,
    normed_input,
    query_weight,
    down_factors,
    up_factors,
    adapter_per_block,
    key_value_cache,
    token_segment,
):
    groups, tensor, stores = (mesh_shape[a] for a in ("groups", "tensor", "store"))
    rows = normed_input.shape[0]
    blocks = adapter_per_block.shape[0]
    heads = query_weight.shape[1] // HEAD_SIZE
    per_store = down_factors.shape[0]
    member = lax.axis_index("tensor")
    slots = slot_bound(stores, per_store, blocks)
    usual = min(slots, USUAL_SLOTS)
    hops = min(stores - 1, -(-(stores * rows // 2 - 1) // rows))
    share = min(tensor, max(1, GROUP // heads))
    quarter = rows // share
    exchange = tensor if blocks % tensor == 0 else 1
    raise_up = [(i, i + 1) for i in range(stores - 1)]
    raise_down = [(i + 1, i) for i in range(stores - 1)]
    pairs = lambda m: [(t, t ^ m) for t in range(tensor)]

    message = jnp.concatenate(
        [
            token_segment.reshape(-1, BLOCK),
            jnp.pad(adapter_per_block, (0, BLOCK - blocks)).reshape(1, BLOCK),
        ]
    )
    messages = [message] + [
        lax.ppermute(message, "store", [(i, (i + m) % stores) for i in range(stores)])
        for m in range(1, stores)
    ]
    down = jnp.swapaxes(down_factors, 1, 2)
    base = base_queries(normed_input, query_weight)
    messages, base = lax.optimization_barrier((messages, base))
    plan = make_plan(messages, stores, blocks, per_store, slots)

    cache = jnp.swapaxes(key_value_cache, 0, 1)
    cache = lax.dynamic_index_in_dim(cache, member * heads // GROUP, 0, keepdims=False)
    quarters = lax.dynamic_slice_in_dim(cache, lax.rem(member, share) * quarter, quarter, 0)
    quarters = lax.all_gather(quarters, "store")
    oldest = jnp.maximum(lax.axis_index("store") - hops, 0)
    quarters = lax.dynamic_slice_in_dim(quarters, oldest, hops, 0)
    if share == tensor:
        pieces = [lax.all_gather(quarters, "tensor", tiled=True)]
    else:
        pieces = [quarters] + [
            lax.ppermute(quarters, "tensor", pairs(m)) for m in range(1, share)
        ]

    def fetch(first, last, ups, downs, plan):
        sent_up, sent_down = [], []
        head = max(0, min(LAG, last) - first)
        if head:
            sent_up, sent_down = pack(plan, down, up_factors, [], [], range(head), slots)
            sent_up, sent_down = list(sent_up), list(sent_down)
        ups, downs = list(ups), list(downs)
        for k in range(first, last):
            if k >= LAG:
                got = k - LAG + 1
                u, d = pack(plan, down, up_factors, ups[:got], downs[:got], [k], slots)
                plan, *ud = lax.optimization_barrier((plan, *u, *d))
                sent_up += ud[:1]
                sent_down += ud[1:]
            ups.append(lax.ppermute(sent_up[k - first], "store", raise_up))
            downs.append(lax.ppermute(sent_down[k - first], "store", raise_down))
        return ups, downs

    keys, values, starts, firsts = window(
        pieces, cache, messages[: hops + 1], hops, share, CHUNK
    )
    ups, downs = fetch(0, usual, [], [], plan)
    former = max(0, usual - LAG)
    earlier_parts = low_rank_parts(
        plan, normed_input, down, up_factors, ups[:former], downs[:former], slots, exchange, blocks
    )

    def finish(ups, downs, plan):
        *parts, selected = low_rank_parts(
            plan,
            normed_input,
            down,
            up_factors,
            ups,
            downs,
            slots,
            exchange,
            blocks,
            former,
            earlier_parts,
        )
        if exchange > 1:
            total = parts[0]
            for m in range(1, tensor):
                total = total + lax.ppermute(parts[m], "tensor", pairs(m))
            total = total.astype(jnp.bfloat16)
            low = [total] + [lax.ppermute(total, "tensor", pairs(m)) for m in range(1, tensor)]
        else:
            low = [lax.psum(parts[0], "tensor").astype(jnp.bfloat16)]
        return attention(firsts, base, starts, keys, values, selected, low, hops, CHUNK, heads)

    usually = finish(ups, downs, plan)
    if usual == slots:
        return usually
    def with_all(plan, ups, downs, usually):
        return finish(*fetch(usual, slots, ups, downs, plan), plan)

    return lax.cond(
        plan[0] > usual, with_all, lambda plan, ups, downs, usually: usually, plan, ups, downs, usually
    )


def solution(mesh):
    return jax.shard_map(
        functools.partial(per_device, dict(mesh.shape)),
        mesh=mesh,
        in_specs=(
            P(("groups", "store"), None),
            P(None, "tensor"),
            P("store", "tensor", None),
            P("store", None, "tensor"),
            P(("groups", "store")),
            P(("groups", "store"), None, None),
            P(("groups", "store")),
        ),
        out_specs=P(("groups", "store"), "tensor"),
        check_vma=False,
    )
```

```python
import functools
import math

import jax
import jax.numpy as jnp
from jax import lax
from jax.experimental import pallas as pl
from jax.experimental.pallas import tpu as pltpu
from jax.sharding import PartitionSpec as P

HEAD_SIZE = 128
GROUP = 8
BLOCK = 128
ADAPTERS = 64
SEGMENTS = 4
LAG = 2
USUAL_SLOTS = 8
MORE_SLOTS = 2
CHUNK = 512
MIB = 1 << 20
ANY = pl.BlockSpec(memory_space=pl.ANY)
SMEM = pl.BlockSpec(memory_space=pltpu.SMEM)
VMEM = pl.BlockSpec(memory_space=pltpu.VMEM)


def slot_bound(stores, per_store, blocks):
    load = max(
        min(per_store * (link + 1), blocks * (stores - 1 - link)) for link in range(stores - 1)
    )
    return load + (stores - 2) * LAG


def plan_kernel(stores, blocks, per_store, slots, *refs):
    index_refs = refs[:stores]
    plan, names, place, listed, bases, counts = refs[stores:]
    capacity = per_store + 1
    my_store = lax.axis_index("store")
    zero = jnp.int32(0)
    for shift in range(stores):
        origin = lax.rem(my_store + stores - shift, stores)
        for b in range(blocks):
            names[origin * blocks + b] = index_refs[shift][index_refs[shift].shape[0] - 1, b]
    for i in range(2 * ADAPTERS):
        place[i] = jnp.int32(-1)
    for i in range(2 * slots):
        plan[1 + i] = zero
    most = zero
    for way in range(2):
        count = [zero] * stores
        crossing = [[zero] * stores for _ in range(stores)]
        for dest in range(stores - 1, 0, -1):
            real = dest if way == 0 else stores - 1 - dest
            for b in range(blocks):
                name = names[real * blocks + b]
                owner = lax.div(name, jnp.int32(per_store))
                if way == 1:
                    owner = stores - 1 - owner
                held = place[way * ADAPTERS + name]
                new = (owner < dest) & (held < 0)
                at = zero
                for o in range(stores):
                    at = jnp.where(owner == o, count[o], at)
                listed[(way * stores + owner) * capacity + at] = name
                place[way * ADAPTERS + name] = jnp.where(new, at, held)
                step = new.astype(jnp.int32)
                for o in range(dest):
                    count[o] = count[o] + jnp.where(owner == o, step, 0)
            for o in range(dest):
                crossing[o][dest - 1] = count[o]
        base = [[zero] * stores for _ in range(stores)]
        for link in range(stores):
            cursor = zero
            for o in range(stores):
                spot = (way * stores + link) * stores + o
                bases[spot] = zero
                counts[spot] = zero
            if link == stores - 1:
                continue
            for o in range(link, -1, -1):
                start = cursor if o == link else jnp.maximum(cursor, base[link - 1][o] + LAG)
                base[link][o] = start
                number = crossing[o][link]
                spot = (way * stores + link) * stores + o
                bases[spot] = start
                counts[spot] = number
                cursor = jnp.where(number > 0, start + number, cursor)
            most = jnp.maximum(most, cursor)
    plan[0] = most
    for way in range(2):
        mine = my_store if way == 0 else stores - 1 - my_store
        for o in range(stores - 1):
            spot = (way * stores + mine) * stores + o
            before = (way * stores + jnp.maximum(mine - 1, 0)) * stores + o
            start = bases[spot]
            earlier = bases[before]
            row = (way * stores + o) * capacity

            def fill(r, _):
                own = listed[row + r] - my_store * per_store
                plan[1 + way * slots + start + r] = jnp.where(
                    mine == o, own, per_store + way * slots + earlier + r
                )
                return 0

            lax.fori_loop(0, counts[spot], fill, 0)
    for b in range(blocks):
        name = names[my_store * blocks + b]
        owner = lax.div(name, jnp.int32(per_store))
        source = name - my_store * per_store
        for way in range(2):
            mine = my_store if way == 0 else stores - 1 - my_store
            far = owner if way == 0 else stores - 1 - owner
            spot = (way * stores + jnp.maximum(mine - 1, 0)) * stores + far
            arrives = per_store + way * slots + bases[spot] + place[way * ADAPTERS + name]
            source = jnp.where(far < mine, arrives, source)
        plan[1 + 2 * slots + b] = source


def make_plan(shifted, stores, blocks, per_store, slots):
    return pl.pallas_call(
        functools.partial(plan_kernel, stores, blocks, per_store, slots),
        out_shape=jax.ShapeDtypeStruct((1 + 2 * slots + blocks,), jnp.int32),
        in_specs=[SMEM] * len(shifted),
        out_specs=SMEM,
        scratch_shapes=[
            pltpu.SMEM((stores * blocks,), jnp.int32),
            pltpu.SMEM((2 * ADAPTERS,), jnp.int32),
            pltpu.SMEM((2 * stores * (per_store + 1),), jnp.int32),
            pltpu.SMEM((2 * stores * stores,), jnp.int32),
            pltpu.SMEM((2 * stores * stores,), jnp.int32),
        ],
        name="plan",
    )(*shifted)


def pack_kernel(slots, per_store, which, received, plan, down, up, *refs):
    got = [refs[:received], refs[received : 2 * received]]
    out = refs[2 * received : 2 * received + 2 * len(which)]
    sems = refs[-1]
    width = down.shape[2]

    def copies(way, i):
        source = plan[1 + way * slots + which[i]]
        dst = out[way * len(which) + i]
        sem = sems.at[way * len(which) + i]
        own = jnp.minimum(source, per_store - 1)
        pairs = [
            (
                source < per_store,
                [
                    pltpu.make_async_copy(down.at[own], dst.at[:, pl.ds(0, width)], sem),
                    pltpu.make_async_copy(
                        up.at[own], dst.at[:, pl.ds(width, up.shape[2])], sem
                    ),
                ],
            )
        ]
        for j in range(received):
            pairs.append(
                (
                    source == per_store + way * slots + j,
                    [pltpu.make_async_copy(got[way][j], dst, sem)],
                )
            )
        return pairs

    for act in ("start", "wait"):
        for way in range(2):
            for i in range(len(which)):
                for chosen, moves in copies(way, i):

                    @pl.when(chosen)
                    def _():
                        for move in moves:
                            getattr(move, act)()


def pack(plan, down, up, ups, downs, which, slots):
    per_store, rank, width = down.shape
    item = jax.ShapeDtypeStruct((rank, width + up.shape[2]), down.dtype)
    made = 2 * len(which)
    out = pl.pallas_call(
        functools.partial(pack_kernel, slots, per_store, tuple(which), len(ups)),
        out_shape=[item] * made,
        in_specs=[SMEM] + [ANY] * (2 + 2 * len(ups)),
        out_specs=[VMEM] * made,
        scratch_shapes=[pltpu.SemaphoreType.DMA((made,))],
        compiler_params=pltpu.CompilerParams(vmem_limit_bytes=16 * MIB),
        cost_estimate=pl.CostEstimate(
            flops=5 * 10**8, bytes_accessed=made * 4 * math.prod(item.shape), transcendentals=0
        ),
        name="pack",
    )(plan, down, up, *ups, *downs)
    return out[: len(which)], out[len(which) :]


def low_rank_kernel(slots, per_store, former, received, tensor, plan, x, down, up, *refs):
    earlier = refs[: tensor + 1] if former is not None else ()
    refs = refs[len(earlier) :]
    got = refs[: 2 * received]
    outs = refs[2 * received : 2 * received + tensor]
    selected, x_rows, factors, sems = refs[2 * received + tensor :]
    blocks, rank, width = factors.shape
    share = blocks // tensor
    member = lax.axis_index("tensor")
    columns = pl.ds(pl.multiple_of(member * width, 128), width)
    if tensor == 1:
        member = 0

    def within(source, number):
        return (source < per_store + number) | (
            (source >= per_store + slots) & (source < per_store + slots + number)
        )

    def due(b):
        source = plan[1 + 2 * slots + b]
        if former is None:
            return within(source, received)
        return jnp.logical_not(within(source, former))

    def copies(b):
        source = plan[1 + 2 * slots + b]
        source = jnp.where(within(source, received), source, 0)
        own = jnp.minimum(source, per_store - 1)
        pairs = [
            (
                source < per_store,
                [
                    pltpu.make_async_copy(down.at[own], factors.at[b], sems.at[b]),
                    pltpu.make_async_copy(up.at[own], selected.at[b], sems.at[b]),
                ],
            )
        ]
        for j in range(2 * received):
            spot = j if j < received else slots + j - received
            pairs.append(
                (
                    source == per_store + spot,
                    [
                        pltpu.make_async_copy(
                            got[j].at[:, pl.ds(0, width)], factors.at[b], sems.at[b]
                        ),
                        pltpu.make_async_copy(
                            got[j].at[:, pl.ds(width, up.shape[2])], selected.at[b], sems.at[b]
                        ),
                    ],
                )
            )
        return pairs

    def rows_of(b):
        rows = pl.ds(pl.multiple_of(b * BLOCK, BLOCK), BLOCK)
        return pltpu.make_async_copy(x.at[rows, columns], x_rows.at[b], sems.at[blocks + b])

    if former is not None:
        selected[...] = earlier[tensor][...]
    else:
        selected[...] = jnp.zeros_like(selected)

    def start(b, _):
        @pl.when(due(b))
        def _():
            rows_of(b).start()
            for chosen, moves in copies(b):

                @pl.when(chosen)
                def _():
                    for move in moves:
                        move.start()

        return 0

    lax.fori_loop(0, blocks, start, 0)
    for m in range(tensor):
        for i in range(share):
            b = (member ^ m) * share + i
            wanted = due(b)

            @pl.when(wanted)
            def _():
                pltpu.make_async_copy(down.at[0], factors.at[b], sems.at[b]).wait()
                pltpu.make_async_copy(up.at[0], selected.at[b], sems.at[b]).wait()
                rows_of(b).wait()
                outs[m][i] = lax.dot_general(
                    x_rows[b],
                    factors[b],
                    (((1,), (1,)), ((), ())),
                    preferred_element_type=jnp.float32,
                ).T

            @pl.when(jnp.logical_not(wanted))
            def _():
                if former is not None:
                    outs[m][i] = earlier[m][i]
                else:
                    outs[m][i] = jnp.zeros(outs[m].shape[1:], jnp.float32)


def low_rank_parts(plan, x, down, up, ups, downs, slots, tensor, blocks, former=None, earlier=()):
    per_store, rank, width = down.shape
    share = blocks // tensor
    return pl.pallas_call(
        functools.partial(low_rank_kernel, slots, per_store, former, len(ups), tensor),
        out_shape=[jax.ShapeDtypeStruct((share, rank, BLOCK), jnp.float32)] * tensor
        + [jax.ShapeDtypeStruct((blocks, rank, up.shape[2]), up.dtype)],
        in_specs=[SMEM] + [ANY] * 3 + [VMEM] * len(earlier) + [ANY] * (2 * len(ups)),
        out_specs=[VMEM] * (tensor + 1),
        scratch_shapes=[
            pltpu.VMEM((blocks, BLOCK, width), x.dtype),
            pltpu.VMEM((blocks, rank, width), down.dtype),
            pltpu.SemaphoreType.DMA((2 * blocks,)),
        ],
        compiler_params=pltpu.CompilerParams(vmem_limit_bytes=24 * MIB),
        cost_estimate=pl.CostEstimate(
            flops=2 * blocks * BLOCK * rank * width,
            bytes_accessed=2 * blocks * width * (BLOCK + rank),
            transcendentals=0,
        ),
        name="low_rank",
    )(plan, x, down, up, *earlier, *ups, *downs)


def window_kernel(hops, share, pad, *refs):
    pieces = refs[: hops * share]
    own = refs[hops * share]
    messages = refs[hops * share + 1 : hops * share + 2 + hops]
    keys, values, starts, firsts, buffer, sems = refs[hops * share + 2 + hops :]
    rows = own.shape[0]
    part = rows // share
    blocks = rows // BLOCK
    member = lax.rem(lax.axis_index("tensor"), share)
    store = lax.axis_index("store")
    moves = [
        pltpu.make_async_copy(own, buffer.at[pl.ds(hops * rows, rows)], sems.at[hops * share])
    ]
    for hop in range(hops):
        for m in range(share):
            at = pl.multiple_of((hops - 1 - hop) * rows + (member ^ m) * part, part)
            moves.append(
                pltpu.make_async_copy(
                    pieces[hop * share + m], buffer.at[pl.ds(at, part)], sems.at[hop * share + m]
                )
            )
    for move in moves:
        move.start()
    empty = jnp.maximum(hops - store, 0) * rows
    names = messages[0][pl.ds(0, blocks), :]
    start = jnp.zeros(names.shape, jnp.int32) + empty
    for value in range(1, SEGMENTS):
        before = empty.astype(jnp.float32)
        for hop in range(hops + 1):
            below = (messages[hop][pl.ds(0, blocks), :] < value).astype(jnp.float32)
            before = before + jnp.where(hop <= store, jnp.sum(below), 0.0)
        start = jnp.where(names == value, before.astype(jnp.int32), start)
    starts[...] = start.reshape(starts.shape)
    for j in range(blocks):
        firsts[j] = jnp.min(start[j : j + 1].astype(jnp.float32)).astype(jnp.int32)
    for move in moves:
        move.wait()
    keys[pl.ds(0, pad), :] = jnp.zeros((pad, HEAD_SIZE), keys.dtype)
    values[:, pl.ds(0, pad)] = jnp.zeros((HEAD_SIZE, pad), values.dtype)

    def turn(c, _):
        at = pl.ds(pl.multiple_of(c * 256, 256), 256)
        to = pl.ds(pl.multiple_of(pad + c * 256, 256), 256)
        keys[to, :] = buffer[at, pl.ds(0, HEAD_SIZE)]
        values[:, to] = buffer[at, pl.ds(HEAD_SIZE, HEAD_SIZE)].astype(jnp.float32).T.astype(
            values.dtype
        )
        return 0

    lax.fori_loop(0, (hops + 1) * rows // 256, turn, 0)


def window(pieces, own, messages, hops, share, pad):
    rows = own.shape[0]
    length = pad + (hops + 1) * rows
    return pl.pallas_call(
        functools.partial(window_kernel, hops, share, pad),
        out_shape=[
            jax.ShapeDtypeStruct((length, HEAD_SIZE), own.dtype),
            jax.ShapeDtypeStruct((HEAD_SIZE, length), own.dtype),
            jax.ShapeDtypeStruct((rows // BLOCK, 1, BLOCK), jnp.int32),
            jax.ShapeDtypeStruct((rows // BLOCK,), jnp.int32),
        ],
        in_specs=[ANY] * (len(pieces) + 1) + [VMEM] * (hops + 1),
        out_specs=[VMEM, VMEM, VMEM, SMEM],
        scratch_shapes=[
            pltpu.VMEM(((hops + 1) * rows, 2 * HEAD_SIZE), own.dtype),
            pltpu.SemaphoreType.DMA((hops * share + 1,)),
        ],
        compiler_params=pltpu.CompilerParams(vmem_limit_bytes=24 * MIB),
        cost_estimate=pl.CostEstimate(
            flops=0, bytes_accessed=8 * length * HEAD_SIZE, transcendentals=0
        ),
        name="window",
    )(*pieces, own, *messages)


def base_kernel(x, weight, out, total):
    k = pl.program_id(0)
    product = jnp.dot(x[...], weight[...], preferred_element_type=jnp.float32)

    @pl.when(k == 0)
    def _():
        total[...] = product

    @pl.when(k > 0)
    def _():
        total[...] += product

    @pl.when(k == pl.num_programs(0) - 1)
    def _():
        out[...] = total[...].T


def base_queries(x, weight, part, parts):
    rows, width = x.shape
    rows //= parts
    columns = weight.shape[1]
    deep = min(width, 1024)
    return pl.pallas_call(
        base_kernel,
        out_shape=jax.ShapeDtypeStruct((columns, rows), jnp.float32),
        grid=(width // deep,),
        in_specs=[
            pl.BlockSpec((rows, deep), lambda k: (part, k)),
            pl.BlockSpec((deep, columns), lambda k: (k, 0)),
        ],
        out_specs=pl.BlockSpec((columns, rows), lambda k: (0, 0)),
        scratch_shapes=[pltpu.VMEM((rows, columns), jnp.float32)],
        compiler_params=pltpu.CompilerParams(vmem_limit_bytes=24 * MIB),
        cost_estimate=pl.CostEstimate(
            flops=2 * rows * width * columns,
            bytes_accessed=2 * width * (rows + columns),
            transcendentals=0,
        ),
        name="base",
    )(x, weight)


def attention_kernel(
    hops, tensor, pad, heads, firsts, early, late, starts, keys, values, selected, *refs
):
    ranks = refs[:tensor]
    out, even, odd, even_largest, odd_largest, top, total, summed, queries = refs[tensor:]
    j = pl.program_id(0)
    share = ranks[0].shape[0]
    member = lax.axis_index("tensor") if tensor > 1 else 0
    rows = (keys.shape[0] - pad) // (hops + 1)
    low = jnp.zeros(ranks[0].shape[1:], jnp.bfloat16)
    for m in range(tensor):
        for i in range(share):
            low = jnp.where(j == (member ^ m) * share + i, ranks[m][i], low)
    term = lax.dot_general(
        selected[0], low, (((0,), (0,)), ((), ())), preferred_element_type=jnp.float32
    )
    base = jnp.where(j < pl.num_programs(0) // 2, early[...], late[...])
    turned = (base + term).astype(jnp.bfloat16)
    for h in range(heads):
        queries[:, h * BLOCK : (h + 1) * BLOCK] = turned[h * HEAD_SIZE : (h + 1) * HEAD_SIZE]
    q = queries[...]
    columns = heads * BLOCK
    start = jnp.concatenate([starts[0]] * heads, axis=1) + pad
    end = pad + hops * rows + (j + 1) * BLOCK
    steps = lax.div(end - pad - firsts[j] + CHUNK - 1, jnp.int32(CHUNK))
    scale = HEAD_SIZE**-0.5 * math.log2(math.e)
    key = lax.broadcasted_iota(jnp.int32, (CHUNK, columns), 0)

    def place_of(c):
        return pl.multiple_of(jnp.maximum(end - (c + 1) * CHUNK, 0), BLOCK)

    def score(c, buffer, largest, diagonal):
        at = place_of(c)
        s = jnp.dot(keys[pl.ds(at, CHUNK), :], q, preferred_element_type=jnp.float32)
        allowed = key >= start - at
        if diagonal:
            token = lax.rem(lax.broadcasted_iota(jnp.int32, (1, columns), 1), BLOCK)
            allowed = allowed & (key <= token + (CHUNK - BLOCK))
        s = jnp.where(allowed, s, jnp.float32(-1e30))
        buffer[...] = s
        largest[...] = jnp.max(s.reshape(CHUNK // 8, 8, columns), axis=0)

    def weigh(c, buffer, largest):
        before = top[...]
        now = jnp.maximum(before, jnp.max(largest[...], axis=0, keepdims=True))
        top[...] = now
        fade = jnp.exp2((before - now) * scale)
        w = jnp.exp2((buffer[...] - now) * scale)
        total[...] = total[...] * fade + jnp.sum(w.reshape(CHUNK // 8, 8, columns), axis=0)
        summed[...] = summed[...] * fade + jnp.dot(
            values[:, pl.ds(place_of(c), CHUNK)],
            w.astype(jnp.bfloat16),
            preferred_element_type=jnp.float32,
        )

    top[...] = jnp.full(top.shape, -1e30, jnp.float32)
    total[...] = jnp.zeros(total.shape, jnp.float32)
    summed[...] = jnp.zeros(summed.shape, jnp.float32)
    score(0, even, even_largest, True)

    def two(i, _):
        score(2 * i + 1, odd, odd_largest, False)
        weigh(2 * i, even, even_largest)

        @pl.when(2 * i + 1 < steps)
        def _():
            score(2 * i + 2, even, even_largest, False)
            weigh(2 * i + 1, odd, odd_largest)

        return 0

    lax.fori_loop(0, lax.div(steps + 1, jnp.int32(2)), two, 0)
    attended = summed[...] / jnp.sum(total[...], axis=0, keepdims=True)
    for h in range(heads):
        out[:, h * HEAD_SIZE : (h + 1) * HEAD_SIZE] = (
            attended[:, h * BLOCK : (h + 1) * BLOCK].T.astype(out.dtype)
        )


def attention(firsts, base, starts, keys, values, selected, ranks, hops, pad, heads):
    columns, half = base[0].shape
    rows = 2 * half
    blocks = rows // BLOCK
    length = keys.shape[0]
    whole = lambda shape: pl.BlockSpec(shape, lambda j, *_: (0,) * len(shape))
    return pl.pallas_call(
        functools.partial(attention_kernel, hops, len(ranks), pad, heads),
        out_shape=jax.ShapeDtypeStruct((rows, columns), jnp.bfloat16),
        grid_spec=pltpu.PrefetchScalarGridSpec(
            num_scalar_prefetch=1,
            grid=(blocks,),
            in_specs=[
                pl.BlockSpec((columns, BLOCK), lambda j, *_: (0, jnp.minimum(j, blocks // 2 - 1))),
                pl.BlockSpec((columns, BLOCK), lambda j, *_: (0, jnp.maximum(j - blocks // 2, 0))),
                pl.BlockSpec((1, 1, BLOCK), lambda j, *_: (j, 0, 0)),
                whole(keys.shape),
                whole(values.shape),
                pl.BlockSpec((1,) + selected.shape[1:], lambda j, *_: (j, 0, 0)),
            ]
            + [whole(r.shape) for r in ranks],
            out_specs=pl.BlockSpec((BLOCK, columns), lambda j, *_: (j, 0)),
            scratch_shapes=[
                pltpu.VMEM((CHUNK, heads * BLOCK), jnp.float32),
                pltpu.VMEM((CHUNK, heads * BLOCK), jnp.float32),
                pltpu.VMEM((8, heads * BLOCK), jnp.float32),
                pltpu.VMEM((8, heads * BLOCK), jnp.float32),
                pltpu.VMEM((1, heads * BLOCK), jnp.float32),
                pltpu.VMEM((8, heads * BLOCK), jnp.float32),
                pltpu.VMEM((HEAD_SIZE, heads * BLOCK), jnp.float32),
                pltpu.VMEM((HEAD_SIZE, heads * BLOCK), jnp.bfloat16),
            ],
        ),
        compiler_params=pltpu.CompilerParams(vmem_limit_bytes=40 * MIB),
        cost_estimate=pl.CostEstimate(
            flops=2 * rows * columns * length,
            bytes_accessed=8 * length * HEAD_SIZE,
            transcendentals=rows * heads * length,
        ),
        name="attention",
    )(firsts, *base, starts, keys, values, selected, *ranks)


def per_device(
    mesh_shape,
    normed_input,
    query_weight,
    down_factors,
    up_factors,
    adapter_per_block,
    key_value_cache,
    token_segment,
):
    groups, tensor, stores = (mesh_shape[a] for a in ("groups", "tensor", "store"))
    rows = normed_input.shape[0]
    blocks = adapter_per_block.shape[0]
    heads = query_weight.shape[1] // HEAD_SIZE
    per_store = down_factors.shape[0]
    member = lax.axis_index("tensor")
    slots = slot_bound(stores, per_store, blocks)
    usual = min(slots, USUAL_SLOTS)
    hops = min(stores - 1, -(-(stores * rows // 2 - 1) // rows))
    share = min(tensor, max(1, GROUP // heads))
    quarter = rows // share
    exchange = tensor if blocks % tensor == 0 else 1
    raise_up = [(i, i + 1) for i in range(stores - 1)]
    raise_down = [(i + 1, i) for i in range(stores - 1)]
    pairs = lambda m: [(t, t ^ m) for t in range(tensor)]

    message = jnp.concatenate(
        [
            token_segment.reshape(-1, BLOCK),
            jnp.pad(adapter_per_block, (0, BLOCK - blocks)).reshape(1, BLOCK),
        ]
    )
    messages = [message] + [
        lax.ppermute(message, "store", [(i, (i + m) % stores) for i in range(stores)])
        for m in range(1, stores)
    ]
    down = jnp.swapaxes(down_factors, 1, 2)
    base = [base_queries(normed_input, query_weight, i, 2) for i in range(2)]

    cache = jnp.swapaxes(key_value_cache, 0, 1)
    cache = lax.dynamic_index_in_dim(cache, member * heads // GROUP, 0, keepdims=False)
    piece = lax.dynamic_slice_in_dim(cache, lax.rem(member, share) * quarter, quarter, 0)
    quarters = [lax.ppermute(piece, "store", raise_up)]
    messages, base[0], quarters[0] = lax.optimization_barrier((messages, base[0], quarters[0]))
    for hop in range(1, hops):
        quarters.append(lax.ppermute(quarters[hop - 1], "store", raise_up))
    plan = make_plan(messages, stores, blocks, per_store, slots)
    plan, *quarters = lax.optimization_barrier((plan, *quarters))
    pieces = []
    for piece in quarters:
        pieces += [piece] + [lax.ppermute(piece, "tensor", pairs(m)) for m in range(1, share)]

    def fetch(first, last, ups, downs, plan, beside={}):
        sent_up, sent_down = [], []
        head = max(0, min(LAG, last) - first)
        if head:
            sent_up, sent_down = pack(plan, down, up_factors, [], [], range(head), slots)
            sent_up, sent_down = list(sent_up), list(sent_down)
        ups, downs = list(ups), list(downs)
        for k in range(first, last):
            if k in beside:
                plan, *_ = lax.optimization_barrier((plan, *beside[k]))
            if k >= LAG:
                got = k - LAG + 1
                u, d = pack(plan, down, up_factors, ups[:got], downs[:got], [k], slots)
                plan, *ud = lax.optimization_barrier((plan, *u, *d))
                sent_up += ud[:1]
                sent_down += ud[1:]
            ups.append(lax.ppermute(sent_up[k - first], "store", raise_up))
            downs.append(lax.ppermute(sent_down[k - first], "store", raise_down))
        return ups, downs

    keys, values, starts, firsts = window(
        pieces, cache, messages[: hops + 1], hops, share, CHUNK
    )
    ups, downs = fetch(0, usual, [], [], plan, {min(4, usual - 1): pieces[1:share], min(6, usual - 1): pieces})
    former = max(0, usual - LAG)
    earlier_parts = low_rank_parts(
        plan, normed_input, down, up_factors, ups[:former], downs[:former], slots, exchange, blocks
    )

    def low_rank(ups, downs, plan):
        return tuple(
            low_rank_parts(
                plan,
                normed_input,
                down,
                up_factors,
                ups,
                downs,
                slots,
                exchange,
                blocks,
                former,
                earlier_parts,
            )
        )

    def finish(parts, selected):
        if exchange > 1:
            total = parts[0]
            for m in range(1, tensor):
                total = total + lax.ppermute(parts[m], "tensor", pairs(m))
            total = total.astype(jnp.bfloat16)
            low = [total] + [lax.ppermute(total, "tensor", pairs(m)) for m in range(1, tensor)]
        else:
            low = [lax.psum(parts[0], "tensor").astype(jnp.bfloat16)]
        return attention(firsts, base, starts, keys, values, selected, low, hops, CHUNK, heads)

    def with_more(ups, downs, plan):
        return low_rank(*fetch(usual, more, ups, downs, plan), plan)

    def with_all(ups, downs, plan, usually):
        *parts, selected = low_rank(*fetch(usual, slots, ups, downs, plan), plan)
        return finish(parts, selected)

    more = min(slots, usual + MORE_SLOTS)
    *parts, selected = lax.cond(plan[0] > usual, with_more, low_rank, ups, downs, plan)
    usually = finish(parts, selected)
    if more == slots:
        return usually
    return lax.cond(
        plan[0] > more, with_all, lambda ups, downs, plan, usually: usually, ups, downs, plan, usually
    )


def solution(mesh):
    return jax.shard_map(
        functools.partial(per_device, dict(mesh.shape)),
        mesh=mesh,
        in_specs=(
            P(("groups", "store"), None),
            P(None, "tensor"),
            P("store", "tensor", None),
            P("store", None, "tensor"),
            P(("groups", "store")),
            P(("groups", "store"), None, None),
            P(("groups", "store")),
        ),
        out_specs=P(("groups", "store"), "tensor"),
        check_vma=False,
    )
```

```python
import functools
import math

import jax
import jax.numpy as jnp
from jax import lax
from jax.experimental import pallas as pl
from jax.experimental.pallas import tpu as pltpu
from jax.sharding import PartitionSpec as P

HEAD_SIZE = 128
GROUP = 8
BLOCK = 128
ADAPTERS = 64
SEGMENTS = 4
BATCH = 2
LAG = BATCH
USUAL = 4
MORE = 1
CHUNK = 512
MIB = 1 << 20
ANY = pl.BlockSpec(memory_space=pl.ANY)
SMEM = pl.BlockSpec(memory_space=pltpu.SMEM)
VMEM = pl.BlockSpec(memory_space=pltpu.VMEM)


def slot_bound(stores, per_store, blocks):
    load = max(
        min(per_store * (link + 1), blocks * (stores - 1 - link)) for link in range(stores - 1)
    )
    return -(-(load + (stores - 2) * LAG) // BATCH) * BATCH


def plan_kernel(stores, blocks, per_store, slots, *refs):
    index_refs = refs[:stores]
    plan, names, place, listed, bases, counts = refs[stores:]
    capacity = per_store + 1
    my_store = lax.axis_index("store")
    zero = jnp.int32(0)
    for shift in range(stores):
        origin = lax.rem(my_store + stores - shift, stores)
        for b in range(blocks):
            names[origin * blocks + b] = index_refs[shift][b]
    for i in range(2 * ADAPTERS):
        place[i] = jnp.int32(-1)
    for i in range(2 * slots):
        plan[1 + i] = zero
    most = zero
    for way in range(2):
        count = [zero] * stores
        crossing = [[zero] * stores for _ in range(stores)]
        for dest in range(stores - 1, 0, -1):
            real = dest if way == 0 else stores - 1 - dest
            for b in range(blocks):
                name = names[real * blocks + b]
                owner = lax.div(name, jnp.int32(per_store))
                if way == 1:
                    owner = stores - 1 - owner
                held = place[way * ADAPTERS + name]
                new = (owner < dest) & (held < 0)
                at = zero
                for o in range(stores):
                    at = jnp.where(owner == o, count[o], at)
                listed[(way * stores + owner) * capacity + at] = name
                place[way * ADAPTERS + name] = jnp.where(new, at, held)
                step = new.astype(jnp.int32)
                for o in range(dest):
                    count[o] = count[o] + jnp.where(owner == o, step, 0)
            for o in range(dest):
                crossing[o][dest - 1] = count[o]
        base = [[zero] * stores for _ in range(stores)]
        for link in range(stores):
            cursor = zero
            for o in range(stores):
                spot = (way * stores + link) * stores + o
                bases[spot] = zero
                counts[spot] = zero
            if link == stores - 1:
                continue
            for o in range(link, -1, -1):
                start = cursor if o == link else jnp.maximum(cursor, base[link - 1][o] + LAG)
                base[link][o] = start
                number = crossing[o][link]
                spot = (way * stores + link) * stores + o
                bases[spot] = start
                counts[spot] = number
                cursor = jnp.where(number > 0, start + number, cursor)
            most = jnp.maximum(most, cursor)
    plan[0] = most
    for way in range(2):
        mine = my_store if way == 0 else stores - 1 - my_store
        for o in range(stores - 1):
            spot = (way * stores + mine) * stores + o
            before = (way * stores + jnp.maximum(mine - 1, 0)) * stores + o
            start = bases[spot]
            earlier = bases[before]
            row = (way * stores + o) * capacity

            def fill(r, _):
                own = listed[row + r] - my_store * per_store
                plan[1 + way * slots + start + r] = jnp.where(
                    mine == o, own, per_store + way * slots + earlier + r
                )
                return 0

            lax.fori_loop(0, counts[spot], fill, 0)
    for b in range(blocks):
        name = names[my_store * blocks + b]
        owner = lax.div(name, jnp.int32(per_store))
        source = name - my_store * per_store
        for way in range(2):
            mine = my_store if way == 0 else stores - 1 - my_store
            far = owner if way == 0 else stores - 1 - owner
            spot = (way * stores + jnp.maximum(mine - 1, 0)) * stores + far
            arrives = per_store + way * slots + bases[spot] + place[way * ADAPTERS + name]
            source = jnp.where(far < mine, arrives, source)
        plan[1 + 2 * slots + b] = source


def make_plan(shifted, stores, blocks, per_store, slots):
    return pl.pallas_call(
        functools.partial(plan_kernel, stores, blocks, per_store, slots),
        out_shape=jax.ShapeDtypeStruct((1 + 2 * slots + blocks,), jnp.int32),
        in_specs=[SMEM] * len(shifted),
        out_specs=SMEM,
        scratch_shapes=[
            pltpu.SMEM((stores * blocks,), jnp.int32),
            pltpu.SMEM((2 * ADAPTERS,), jnp.int32),
            pltpu.SMEM((2 * stores * (per_store + 1),), jnp.int32),
            pltpu.SMEM((2 * stores * stores,), jnp.int32),
            pltpu.SMEM((2 * stores * stores,), jnp.int32),
        ],
        name="plan",
    )(*shifted)


def pack_kernel(slots, per_store, way, batch, plan, down, up, *refs):
    got = refs[:batch]
    out, sems = refs[batch:]
    width = down.shape[2]

    def copies(i):
        source = plan[1 + way * slots + batch * BATCH + i]
        own = jnp.minimum(source, per_store - 1)
        pairs = [
            (
                source < per_store,
                [
                    pltpu.make_async_copy(
                        down.at[own], out.at[i, :, pl.ds(0, width)], sems.at[i]
                    ),
                    pltpu.make_async_copy(
                        up.at[own], out.at[i, :, pl.ds(width, up.shape[2])], sems.at[i]
                    ),
                ],
            )
        ]
        for j in range(batch * BATCH):
            pairs.append(
                (
                    source == per_store + way * slots + j,
                    [pltpu.make_async_copy(got[j // BATCH].at[j % BATCH], out.at[i], sems.at[i])],
                )
            )
        return pairs

    for act in ("start", "wait"):
        for i in range(BATCH):
            for chosen, moves in copies(i):

                @pl.when(chosen)
                def _():
                    for move in moves:
                        getattr(move, act)()


def pack(plan, down, up, got, way, slots):
    per_store, rank, width = down.shape
    item = jax.ShapeDtypeStruct((BATCH, rank, width + up.shape[2]), down.dtype)
    return pl.pallas_call(
        functools.partial(pack_kernel, slots, per_store, way, len(got)),
        out_shape=item,
        in_specs=[SMEM] + [ANY] * (2 + len(got)),
        out_specs=VMEM,
        scratch_shapes=[pltpu.SemaphoreType.DMA((BATCH,))],
        compiler_params=pltpu.CompilerParams(vmem_limit_bytes=16 * MIB),
        cost_estimate=pl.CostEstimate(
            flops=5 * 10**8, bytes_accessed=4 * math.prod(item.shape), transcendentals=0
        ),
        name="pack",
    )(plan, down, up, *got)


def low_rank_kernel(slots, per_store, former, received, tensor, plan, x, down, up, *refs):
    earlier = refs[: tensor + 1] if former is not None else ()
    refs = refs[len(earlier) :]
    number = 2 * received // BATCH
    got = refs[:number]
    outs = refs[number : number + tensor]
    selected, x_rows, factors, sems = refs[number + tensor :]
    blocks, rank, width = factors.shape
    share = blocks // tensor
    member = lax.axis_index("tensor")
    columns = pl.ds(pl.multiple_of(member * width, 128), width)
    if tensor == 1:
        member = 0

    def within(source, number):
        return (source < per_store + number) | (
            (source >= per_store + slots) & (source < per_store + slots + number)
        )

    def due(b):
        source = plan[1 + 2 * slots + b]
        if former is None:
            return within(source, received)
        return jnp.logical_not(within(source, former))

    def copies(b):
        source = plan[1 + 2 * slots + b]
        source = jnp.where(within(source, received), source, 0)
        own = jnp.minimum(source, per_store - 1)
        pairs = [
            (
                source < per_store,
                [
                    pltpu.make_async_copy(down.at[own], factors.at[b], sems.at[b]),
                    pltpu.make_async_copy(up.at[own], selected.at[b], sems.at[b]),
                ],
            )
        ]
        for j in range(2 * received):
            spot = j if j < received else slots + j - received
            item = got[j // BATCH].at[j % BATCH]
            pairs.append(
                (
                    source == per_store + spot,
                    [
                        pltpu.make_async_copy(
                            item.at[:, pl.ds(0, width)], factors.at[b], sems.at[b]
                        ),
                        pltpu.make_async_copy(
                            item.at[:, pl.ds(width, up.shape[2])], selected.at[b], sems.at[b]
                        ),
                    ],
                )
            )
        return pairs

    def rows_of(b):
        rows = pl.ds(pl.multiple_of(b * BLOCK, BLOCK), BLOCK)
        return pltpu.make_async_copy(x.at[rows, columns], x_rows.at[b], sems.at[blocks + b])

    if former is not None:
        selected[...] = earlier[tensor][...]
    else:
        selected[...] = jnp.zeros_like(selected)

    def start(b, _):
        @pl.when(due(b))
        def _():
            rows_of(b).start()
            for chosen, moves in copies(b):

                @pl.when(chosen)
                def _():
                    for move in moves:
                        move.start()

        return 0

    lax.fori_loop(0, blocks, start, 0)
    for m in range(tensor):
        for i in range(share):
            b = (member ^ m) * share + i
            wanted = due(b)

            @pl.when(wanted)
            def _():
                pltpu.make_async_copy(down.at[0], factors.at[b], sems.at[b]).wait()
                pltpu.make_async_copy(up.at[0], selected.at[b], sems.at[b]).wait()
                rows_of(b).wait()
                outs[m][i] = lax.dot_general(
                    x_rows[b],
                    factors[b],
                    (((1,), (1,)), ((), ())),
                    preferred_element_type=jnp.float32,
                ).T

            @pl.when(jnp.logical_not(wanted))
            def _():
                if former is not None:
                    outs[m][i] = earlier[m][i]
                else:
                    outs[m][i] = jnp.zeros(outs[m].shape[1:], jnp.float32)


def low_rank_parts(plan, x, down, up, ups, downs, slots, tensor, blocks, former=None, earlier=()):
    per_store, rank, width = down.shape
    share = blocks // tensor
    return pl.pallas_call(
        functools.partial(
            low_rank_kernel, slots, per_store, former, BATCH * len(ups), tensor
        ),
        out_shape=[jax.ShapeDtypeStruct((share, rank, BLOCK), jnp.float32)] * tensor
        + [jax.ShapeDtypeStruct((blocks, rank, up.shape[2]), up.dtype)],
        in_specs=[SMEM] + [ANY] * 3 + [VMEM] * len(earlier) + [ANY] * (2 * len(ups)),
        out_specs=[VMEM] * (tensor + 1),
        scratch_shapes=[
            pltpu.VMEM((blocks, BLOCK, width), x.dtype),
            pltpu.VMEM((blocks, rank, width), down.dtype),
            pltpu.SemaphoreType.DMA((2 * blocks,)),
        ],
        compiler_params=pltpu.CompilerParams(vmem_limit_bytes=24 * MIB),
        cost_estimate=pl.CostEstimate(
            flops=2 * blocks * BLOCK * rank * width,
            bytes_accessed=2 * blocks * width * (BLOCK + rank),
            transcendentals=0,
        ),
        name="low_rank",
    )(plan, x, down, up, *earlier, *ups, *downs)


def window_kernel(hops, share, pad, *refs):
    pieces = refs[: hops * share]
    own = refs[hops * share]
    segments = refs[hops * share + 1 : hops * share + 2 + hops]
    keys, values, starts, firsts, buffer, sems = refs[hops * share + 2 + hops :]
    rows = own.shape[0]
    part = rows // share
    blocks = rows // BLOCK
    member = lax.rem(lax.axis_index("tensor"), share)
    store = lax.axis_index("store")
    moves = [
        pltpu.make_async_copy(own, buffer.at[pl.ds(hops * rows, rows)], sems.at[hops * share])
    ]
    for hop in range(hops):
        for m in range(share):
            at = pl.multiple_of((hops - 1 - hop) * rows + (member ^ m) * part, part)
            moves.append(
                pltpu.make_async_copy(
                    pieces[hop * share + m], buffer.at[pl.ds(at, part)], sems.at[hop * share + m]
                )
            )
    for move in moves:
        move.start()
    empty = jnp.maximum(hops - store, 0) * rows
    names = segments[0][...]
    start = jnp.zeros(names.shape, jnp.int32) + empty
    for value in range(1, SEGMENTS):
        before = empty.astype(jnp.float32)
        for hop in range(hops + 1):
            below = (segments[hop][...] < value).astype(jnp.float32)
            before = before + jnp.where(hop <= store, jnp.sum(below), 0.0)
        start = jnp.where(names == value, before.astype(jnp.int32), start)
    starts[...] = start.reshape(starts.shape)
    for j in range(blocks):
        firsts[j] = jnp.min(start[j : j + 1].astype(jnp.float32)).astype(jnp.int32)
    for move in moves:
        move.wait()
    keys[pl.ds(0, pad), :] = jnp.zeros((pad, HEAD_SIZE), keys.dtype)
    values[:, pl.ds(0, pad)] = jnp.zeros((HEAD_SIZE, pad), values.dtype)

    def turn(c, _):
        at = pl.ds(pl.multiple_of(c * 256, 256), 256)
        to = pl.ds(pl.multiple_of(pad + c * 256, 256), 256)
        keys[to, :] = buffer[at, pl.ds(0, HEAD_SIZE)]
        values[:, to] = buffer[at, pl.ds(HEAD_SIZE, HEAD_SIZE)].astype(jnp.float32).T.astype(
            values.dtype
        )
        return 0

    lax.fori_loop(0, (hops + 1) * rows // 256, turn, 0)


def window(pieces, own, segments, hops, share, pad):
    rows = own.shape[0]
    length = pad + (hops + 1) * rows
    return pl.pallas_call(
        functools.partial(window_kernel, hops, share, pad),
        out_shape=[
            jax.ShapeDtypeStruct((length, HEAD_SIZE), own.dtype),
            jax.ShapeDtypeStruct((HEAD_SIZE, length), own.dtype),
            jax.ShapeDtypeStruct((rows // BLOCK, 1, BLOCK), jnp.int32),
            jax.ShapeDtypeStruct((rows // BLOCK,), jnp.int32),
        ],
        in_specs=[ANY] * (len(pieces) + 1) + [VMEM] * (hops + 1),
        out_specs=[VMEM, VMEM, VMEM, SMEM],
        scratch_shapes=[
            pltpu.VMEM(((hops + 1) * rows, 2 * HEAD_SIZE), own.dtype),
            pltpu.SemaphoreType.DMA((hops * share + 1,)),
        ],
        compiler_params=pltpu.CompilerParams(vmem_limit_bytes=24 * MIB),
        cost_estimate=pl.CostEstimate(
            flops=0, bytes_accessed=8 * length * HEAD_SIZE, transcendentals=0
        ),
        name="window",
    )(*pieces, own, *segments)


def base_kernel(x, weight, out, total):
    k = pl.program_id(0)
    product = jnp.dot(x[...], weight[...], preferred_element_type=jnp.float32)

    @pl.when(k == 0)
    def _():
        total[...] = product

    @pl.when(k > 0)
    def _():
        total[...] += product

    @pl.when(k == pl.num_programs(0) - 1)
    def _():
        out[...] = total[...].T


def base_queries(x, weight):
    rows, width = x.shape
    columns = weight.shape[1]
    deep = min(width, 1024)
    return pl.pallas_call(
        base_kernel,
        out_shape=jax.ShapeDtypeStruct((columns, rows), jnp.float32),
        grid=(width // deep,),
        in_specs=[
            pl.BlockSpec((rows, deep), lambda k: (0, k)),
            pl.BlockSpec((deep, columns), lambda k: (k, 0)),
        ],
        out_specs=pl.BlockSpec((columns, rows), lambda k: (0, 0)),
        scratch_shapes=[pltpu.VMEM((rows, columns), jnp.float32)],
        compiler_params=pltpu.CompilerParams(vmem_limit_bytes=24 * MIB),
        cost_estimate=pl.CostEstimate(
            flops=2 * rows * width * columns,
            bytes_accessed=2 * width * (rows + columns),
            transcendentals=0,
        ),
        name="base",
    )(x, weight)


def attention_kernel(
    hops, tensor, pad, heads, firsts, base, starts, keys, values, selected, *refs
):
    ranks = refs[:tensor]
    out, even, odd, even_largest, odd_largest, top, total, summed, queries = refs[tensor:]
    j = pl.program_id(0)
    share = ranks[0].shape[0]
    member = lax.axis_index("tensor") if tensor > 1 else 0
    rows = (keys.shape[0] - pad) // (hops + 1)
    low = jnp.zeros(ranks[0].shape[1:], jnp.bfloat16)
    for m in range(tensor):
        for i in range(share):
            low = jnp.where(j == (member ^ m) * share + i, ranks[m][i], low)
    term = lax.dot_general(
        selected[0], low, (((0,), (0,)), ((), ())), preferred_element_type=jnp.float32
    )
    turned = (base[...] + term).astype(jnp.bfloat16)
    for h in range(heads):
        queries[:, h * BLOCK : (h + 1) * BLOCK] = turned[h * HEAD_SIZE : (h + 1) * HEAD_SIZE]
    q = queries[...]
    columns = heads * BLOCK
    start = jnp.concatenate([starts[0]] * heads, axis=1) + pad
    end = pad + hops * rows + (j + 1) * BLOCK
    steps = lax.div(end - pad - firsts[j] + CHUNK - 1, jnp.int32(CHUNK))
    scale = HEAD_SIZE**-0.5 * math.log2(math.e)
    key = lax.broadcasted_iota(jnp.int32, (CHUNK, columns), 0)

    def place_of(c):
        return pl.multiple_of(jnp.maximum(end - (c + 1) * CHUNK, 0), BLOCK)

    def score(c, buffer, largest, diagonal):
        at = place_of(c)
        s = jnp.dot(keys[pl.ds(at, CHUNK), :], q, preferred_element_type=jnp.float32)
        allowed = key >= start - at
        if diagonal:
            token = lax.rem(lax.broadcasted_iota(jnp.int32, (1, columns), 1), BLOCK)
            allowed = allowed & (key <= token + (CHUNK - BLOCK))
        s = jnp.where(allowed, s, jnp.float32(-1e30))
        buffer[...] = s
        largest[...] = jnp.max(s.reshape(CHUNK // 8, 8, columns), axis=0)

    def weigh(c, buffer, largest):
        before = top[...]
        now = jnp.maximum(before, jnp.max(largest[...], axis=0, keepdims=True))
        top[...] = now
        fade = jnp.exp2((before - now) * scale)
        w = jnp.exp2((buffer[...] - now) * scale)
        total[...] = total[...] * fade + jnp.sum(w.reshape(CHUNK // 8, 8, columns), axis=0)
        summed[...] = summed[...] * fade + jnp.dot(
            values[:, pl.ds(place_of(c), CHUNK)],
            w.astype(jnp.bfloat16),
            preferred_element_type=jnp.float32,
        )

    top[...] = jnp.full(top.shape, -1e30, jnp.float32)
    total[...] = jnp.zeros(total.shape, jnp.float32)
    summed[...] = jnp.zeros(summed.shape, jnp.float32)
    score(0, even, even_largest, True)

    def two(i, _):
        score(2 * i + 1, odd, odd_largest, False)
        weigh(2 * i, even, even_largest)

        @pl.when(2 * i + 1 < steps)
        def _():
            score(2 * i + 2, even, even_largest, False)
            weigh(2 * i + 1, odd, odd_largest)

        return 0

    lax.fori_loop(0, lax.div(steps + 1, jnp.int32(2)), two, 0)
    attended = summed[...] / jnp.sum(total[...], axis=0, keepdims=True)
    for h in range(heads):
        out[:, h * HEAD_SIZE : (h + 1) * HEAD_SIZE] = (
            attended[:, h * BLOCK : (h + 1) * BLOCK].T.astype(out.dtype)
        )


def attention(firsts, base, starts, keys, values, selected, ranks, hops, pad, heads):
    columns, rows = base.shape
    blocks = rows // BLOCK
    length = keys.shape[0]
    whole = lambda shape: pl.BlockSpec(shape, lambda j, *_: (0,) * len(shape))
    return pl.pallas_call(
        functools.partial(attention_kernel, hops, len(ranks), pad, heads),
        out_shape=jax.ShapeDtypeStruct((rows, columns), jnp.bfloat16),
        grid_spec=pltpu.PrefetchScalarGridSpec(
            num_scalar_prefetch=1,
            grid=(blocks,),
            in_specs=[
                pl.BlockSpec((columns, BLOCK), lambda j, *_: (0, j)),
                pl.BlockSpec((1, 1, BLOCK), lambda j, *_: (j, 0, 0)),
                whole(keys.shape),
                whole(values.shape),
                pl.BlockSpec((1,) + selected.shape[1:], lambda j, *_: (j, 0, 0)),
            ]
            + [whole(r.shape) for r in ranks],
            out_specs=pl.BlockSpec((BLOCK, columns), lambda j, *_: (j, 0)),
            scratch_shapes=[
                pltpu.VMEM((CHUNK, heads * BLOCK), jnp.float32),
                pltpu.VMEM((CHUNK, heads * BLOCK), jnp.float32),
                pltpu.VMEM((8, heads * BLOCK), jnp.float32),
                pltpu.VMEM((8, heads * BLOCK), jnp.float32),
                pltpu.VMEM((1, heads * BLOCK), jnp.float32),
                pltpu.VMEM((8, heads * BLOCK), jnp.float32),
                pltpu.VMEM((HEAD_SIZE, heads * BLOCK), jnp.float32),
                pltpu.VMEM((HEAD_SIZE, heads * BLOCK), jnp.bfloat16),
            ],
        ),
        compiler_params=pltpu.CompilerParams(vmem_limit_bytes=40 * MIB),
        cost_estimate=pl.CostEstimate(
            flops=2 * rows * columns * length,
            bytes_accessed=8 * length * HEAD_SIZE,
            transcendentals=rows * heads * length,
        ),
        name="attention",
    )(firsts, base, starts, keys, values, selected, *ranks)


def per_device(
    mesh_shape,
    normed_input,
    query_weight,
    down_factors,
    up_factors,
    adapter_per_block,
    key_value_cache,
    token_segment,
):
    groups, tensor, stores = (mesh_shape[a] for a in ("groups", "tensor", "store"))
    rows = normed_input.shape[0]
    blocks = adapter_per_block.shape[0]
    heads = query_weight.shape[1] // HEAD_SIZE
    per_store = down_factors.shape[0]
    member = lax.axis_index("tensor")
    slots = slot_bound(stores, per_store, blocks)
    batches = slots // BATCH
    usual = min(batches, USUAL)
    more = min(batches, usual + MORE)
    hops = min(stores - 1, -(-(stores * rows // 2 - 1) // rows))
    share = min(tensor, max(1, GROUP // heads))
    quarter = rows // share
    exchange = tensor if blocks % tensor == 0 else 1
    raise_up = [(i, i + 1) for i in range(stores - 1)]
    raise_down = [(i + 1, i) for i in range(stores - 1)]
    pairs = lambda m: [(t, t ^ m) for t in range(tensor)]

    indices = [adapter_per_block] + [
        lax.ppermute(adapter_per_block, "store", [(i, (i + m) % stores) for i in range(stores)])
        for m in range(1, stores)
    ]
    down = jnp.swapaxes(down_factors, 1, 2)

    cache = jnp.swapaxes(key_value_cache, 0, 1)
    cache = lax.dynamic_index_in_dim(cache, member * heads // GROUP, 0, keepdims=False)
    quarters = [lax.dynamic_slice_in_dim(cache, lax.rem(member, share) * quarter, quarter, 0)]
    indices, quarters[0] = lax.optimization_barrier((indices, quarters[0]))
    for hop in range(hops):
        quarters.append(lax.ppermute(quarters[hop], "store", raise_up))
    quarters = quarters[1:]
    plan = make_plan(indices, stores, blocks, per_store, slots)
    plan, quarters[0] = lax.optimization_barrier((plan, quarters[0]))

    def fetch(first, last, ups, downs, plan, beside={}):
        ups, downs = list(ups), list(downs)
        for k in range(first, last):
            if k in beside:
                plan, *_ = lax.optimization_barrier((plan, *beside[k]))
            sent_up = pack(plan, down, up_factors, ups[:k], 0, slots)
            sent_down = pack(plan, down, up_factors, downs[:k], 1, slots)
            if k == 0:
                sent_up, sent_down, *_ = lax.optimization_barrier((sent_up, sent_down, *quarters))
            ups.append(lax.ppermute(sent_up, "store", raise_up))
            downs.append(lax.ppermute(sent_down, "store", raise_down))
        return ups, downs

    base = base_queries(normed_input, query_weight)
    pieces = []
    for piece in quarters:
        pieces += [piece] + [lax.ppermute(piece, "tensor", pairs(m)) for m in range(1, share)]
    segments = [token_segment] + [
        lax.ppermute(token_segment, "store", [(i, i + hop) for i in range(stores - hop)])
        for hop in range(1, hops + 1)
    ]
    segments = [s.reshape(-1, BLOCK) for s in segments]
    keys, values, starts, firsts = window(pieces, cache, segments, hops, share, CHUNK)
    beside = {1: (base,), 2: (*pieces, *segments[1:]), 3: (keys, values, starts, firsts)}
    ups, downs = fetch(0, usual, [], [], plan, beside)
    former = usual - 1
    earlier_parts = low_rank_parts(
        plan, normed_input, down, up_factors, ups[:former], downs[:former], slots, exchange, blocks
    )

    def low_rank(ups, downs, plan):
        return tuple(
            low_rank_parts(
                plan,
                normed_input,
                down,
                up_factors,
                ups,
                downs,
                slots,
                exchange,
                blocks,
                former * BATCH,
                earlier_parts,
            )
        )

    def finish(parts, selected):
        if exchange > 1:
            total = parts[0]
            for m in range(1, tensor):
                total = total + lax.ppermute(parts[m], "tensor", pairs(m))
            total = total.astype(jnp.bfloat16)
            low = [total] + [lax.ppermute(total, "tensor", pairs(m)) for m in range(1, tensor)]
        else:
            low = [lax.psum(parts[0], "tensor").astype(jnp.bfloat16)]
        return attention(firsts, base, starts, keys, values, selected, low, hops, CHUNK, heads)

    def with_more(ups, downs, plan):
        return low_rank(*fetch(usual, more, ups, downs, plan), plan)

    def with_all(ups, downs, plan, usually):
        *parts, selected = low_rank(*fetch(usual, batches, ups, downs, plan), plan)
        return finish(parts, selected)

    *parts, selected = lax.cond(plan[0] > usual * BATCH, with_more, low_rank, ups, downs, plan)
    usually = finish(parts, selected)
    if more == batches:
        return usually
    return lax.cond(
        plan[0] > more * BATCH,
        with_all,
        lambda ups, downs, plan, usually: usually,
        ups,
        downs,
        plan,
        usually,
    )


def solution(mesh):
    return jax.shard_map(
        functools.partial(per_device, dict(mesh.shape)),
        mesh=mesh,
        in_specs=(
            P(("groups", "store"), None),
            P(None, "tensor"),
            P("store", "tensor", None),
            P("store", None, "tensor"),
            P(("groups", "store")),
            P(("groups", "store"), None, None),
            P(("groups", "store")),
        ),
        out_specs=P(("groups", "store"), "tensor"),
        check_vma=False,
    )
```

```python
import functools
import math

import jax
import jax.numpy as jnp
from jax import lax
from jax.experimental import pallas as pl
from jax.experimental.pallas import tpu as pltpu
from jax.sharding import PartitionSpec as P

HEAD_SIZE = 128
GROUP = 8
BLOCK = 128
ADAPTERS = 64
SEGMENTS = 4
BATCH = 2
LAG = BATCH
USUAL = 4
MORE = 1
STRIDE = 2 * BLOCK
CHUNK = 512
MIB = 1 << 20
ANY = pl.BlockSpec(memory_space=pl.ANY)
SMEM = pl.BlockSpec(memory_space=pltpu.SMEM)
VMEM = pl.BlockSpec(memory_space=pltpu.VMEM)


def slot_bound(stores, per_store, blocks):
    load = max(
        min(per_store * (link + 1), blocks * (stores - 1 - link)) for link in range(stores - 1)
    )
    return -(-(load + (stores - 2) * LAG) // BATCH) * BATCH


def plan_kernel(stores, blocks, per_store, slots, *refs):
    index_refs = refs[:stores]
    plan, names, place, listed, bases, counts = refs[stores:]
    capacity = per_store + 1
    my_store = lax.axis_index("store")
    zero = jnp.int32(0)
    for shift in range(stores):
        origin = lax.rem(my_store + stores - shift, stores)
        for b in range(blocks):
            names[origin * blocks + b] = index_refs[shift][b]
    for i in range(2 * ADAPTERS):
        place[i] = jnp.int32(-1)
    for i in range(2 * slots):
        plan[1 + i] = zero
    most = zero
    for way in range(2):
        count = [zero] * stores
        crossing = [[zero] * stores for _ in range(stores)]
        for dest in range(stores - 1, 0, -1):
            real = dest if way == 0 else stores - 1 - dest
            for b in range(blocks):
                name = names[real * blocks + b]
                owner = lax.div(name, jnp.int32(per_store))
                if way == 1:
                    owner = stores - 1 - owner
                held = place[way * ADAPTERS + name]
                new = (owner < dest) & (held < 0)
                at = zero
                for o in range(stores):
                    at = jnp.where(owner == o, count[o], at)
                listed[(way * stores + owner) * capacity + at] = name
                place[way * ADAPTERS + name] = jnp.where(new, at, held)
                step = new.astype(jnp.int32)
                for o in range(dest):
                    count[o] = count[o] + jnp.where(owner == o, step, 0)
            for o in range(dest):
                crossing[o][dest - 1] = count[o]
        base = [[zero] * stores for _ in range(stores)]
        for link in range(stores):
            cursor = zero
            for o in range(stores):
                spot = (way * stores + link) * stores + o
                bases[spot] = zero
                counts[spot] = zero
            if link == stores - 1:
                continue
            for o in range(link, -1, -1):
                start = cursor if o == link else jnp.maximum(cursor, base[link - 1][o] + LAG)
                base[link][o] = start
                number = crossing[o][link]
                spot = (way * stores + link) * stores + o
                bases[spot] = start
                counts[spot] = number
                cursor = jnp.where(number > 0, start + number, cursor)
            most = jnp.maximum(most, cursor)
    plan[0] = most
    for way in range(2):
        mine = my_store if way == 0 else stores - 1 - my_store
        for o in range(stores - 1):
            spot = (way * stores + mine) * stores + o
            before = (way * stores + jnp.maximum(mine - 1, 0)) * stores + o
            start = bases[spot]
            earlier = bases[before]
            row = (way * stores + o) * capacity

            def fill(r, _):
                own = listed[row + r] - my_store * per_store
                plan[1 + way * slots + start + r] = jnp.where(
                    mine == o, own, per_store + way * slots + earlier + r
                )
                return 0

            lax.fori_loop(0, counts[spot], fill, 0)
    for b in range(blocks):
        name = names[my_store * blocks + b]
        owner = lax.div(name, jnp.int32(per_store))
        source = name - my_store * per_store
        for way in range(2):
            mine = my_store if way == 0 else stores - 1 - my_store
            far = owner if way == 0 else stores - 1 - owner
            spot = (way * stores + jnp.maximum(mine - 1, 0)) * stores + far
            arrives = per_store + way * slots + bases[spot] + place[way * ADAPTERS + name]
            source = jnp.where(far < mine, arrives, source)
        plan[1 + 2 * slots + b] = source


def make_plan(shifted, stores, blocks, per_store, slots):
    return pl.pallas_call(
        functools.partial(plan_kernel, stores, blocks, per_store, slots),
        out_shape=jax.ShapeDtypeStruct((1 + 2 * slots + blocks,), jnp.int32),
        in_specs=[SMEM] * len(shifted),
        out_specs=SMEM,
        scratch_shapes=[
            pltpu.SMEM((stores * blocks,), jnp.int32),
            pltpu.SMEM((2 * ADAPTERS,), jnp.int32),
            pltpu.SMEM((2 * stores * (per_store + 1),), jnp.int32),
            pltpu.SMEM((2 * stores * stores,), jnp.int32),
            pltpu.SMEM((2 * stores * stores,), jnp.int32),
        ],
        name="plan",
    )(*shifted)


def pack_kernel(slots, per_store, way, batch, plan, down, up, *refs):
    got = refs[:batch]
    out, sems = refs[batch:]
    width = down.shape[2]

    def copies(i):
        source = plan[1 + way * slots + batch * BATCH + i]
        own = jnp.minimum(source, per_store - 1)
        pairs = [
            (
                source < per_store,
                [
                    pltpu.make_async_copy(
                        down.at[own], out.at[i, :, pl.ds(0, width)], sems.at[i]
                    ),
                    pltpu.make_async_copy(
                        up.at[own], out.at[i, :, pl.ds(width, up.shape[2])], sems.at[i]
                    ),
                ],
            )
        ]
        for j in range(batch * BATCH):
            pairs.append(
                (
                    source == per_store + way * slots + j,
                    [pltpu.make_async_copy(got[j // BATCH].at[j % BATCH], out.at[i], sems.at[i])],
                )
            )
        return pairs

    for act in ("start", "wait"):
        for i in range(BATCH):
            for chosen, moves in copies(i):

                @pl.when(chosen)
                def _():
                    for move in moves:
                        getattr(move, act)()


def pack(plan, down, up, got, way, slots):
    per_store, rank, width = down.shape
    item = jax.ShapeDtypeStruct((BATCH, rank, width + up.shape[2]), down.dtype)
    return pl.pallas_call(
        functools.partial(pack_kernel, slots, per_store, way, len(got)),
        out_shape=item,
        in_specs=[SMEM] + [ANY] * (2 + len(got)),
        out_specs=VMEM,
        scratch_shapes=[pltpu.SemaphoreType.DMA((BATCH,))],
        compiler_params=pltpu.CompilerParams(vmem_limit_bytes=16 * MIB),
        cost_estimate=pl.CostEstimate(
            flops=5 * 10**8, bytes_accessed=4 * math.prod(item.shape), transcendentals=0
        ),
        name="pack",
    )(plan, down, up, *got)


def low_rank_kernel(slots, per_store, former, received, tensor, plan, x, down, up, *refs):
    earlier = refs[: tensor + 1] if former is not None else ()
    refs = refs[len(earlier) :]
    number = 2 * received // BATCH
    got = refs[:number]
    outs = refs[number : number + tensor]
    selected, x_rows, factors, sems = refs[number + tensor :]
    blocks, rank, width = factors.shape
    share = blocks // tensor
    member = lax.axis_index("tensor")
    columns = pl.ds(pl.multiple_of(member * width, 128), width)
    if tensor == 1:
        member = 0

    def within(source, number):
        return (source < per_store + number) | (
            (source >= per_store + slots) & (source < per_store + slots + number)
        )

    def due(b):
        source = plan[1 + 2 * slots + b]
        if former is None:
            return within(source, received)
        return jnp.logical_not(within(source, former))

    def copies(b):
        source = plan[1 + 2 * slots + b]
        source = jnp.where(within(source, received), source, 0)
        own = jnp.minimum(source, per_store - 1)
        pairs = [
            (
                source < per_store,
                [
                    pltpu.make_async_copy(down.at[own], factors.at[b], sems.at[b]),
                    pltpu.make_async_copy(up.at[own], selected.at[b], sems.at[b]),
                ],
            )
        ]
        for j in range(2 * received):
            spot = j if j < received else slots + j - received
            item = got[j // BATCH].at[j % BATCH]
            pairs.append(
                (
                    source == per_store + spot,
                    [
                        pltpu.make_async_copy(
                            item.at[:, pl.ds(0, width)], factors.at[b], sems.at[b]
                        ),
                        pltpu.make_async_copy(
                            item.at[:, pl.ds(width, up.shape[2])], selected.at[b], sems.at[b]
                        ),
                    ],
                )
            )
        return pairs

    def rows_of(b):
        rows = pl.ds(pl.multiple_of(b * BLOCK, BLOCK), BLOCK)
        return pltpu.make_async_copy(x.at[rows, columns], x_rows.at[b], sems.at[blocks + b])

    if former is not None:
        selected[...] = earlier[tensor][...]
    else:
        selected[...] = jnp.zeros_like(selected)

    def start(b, _):
        @pl.when(due(b))
        def _():
            rows_of(b).start()
            for chosen, moves in copies(b):

                @pl.when(chosen)
                def _():
                    for move in moves:
                        move.start()

        return 0

    lax.fori_loop(0, blocks, start, 0)
    for m in range(tensor):
        for i in range(share):
            b = (member ^ m) * share + i
            wanted = due(b)

            @pl.when(wanted)
            def _():
                pltpu.make_async_copy(down.at[0], factors.at[b], sems.at[b]).wait()
                pltpu.make_async_copy(up.at[0], selected.at[b], sems.at[b]).wait()
                rows_of(b).wait()
                outs[m][i] = lax.dot_general(
                    x_rows[b],
                    factors[b],
                    (((1,), (1,)), ((), ())),
                    preferred_element_type=jnp.float32,
                ).T

            @pl.when(jnp.logical_not(wanted))
            def _():
                if former is not None:
                    outs[m][i] = earlier[m][i]
                else:
                    outs[m][i] = jnp.zeros(outs[m].shape[1:], jnp.float32)


def low_rank_parts(plan, x, down, up, ups, downs, slots, tensor, blocks, former=None, earlier=()):
    per_store, rank, width = down.shape
    share = blocks // tensor
    return pl.pallas_call(
        functools.partial(
            low_rank_kernel, slots, per_store, former, BATCH * len(ups), tensor
        ),
        out_shape=[jax.ShapeDtypeStruct((share, rank, BLOCK), jnp.float32)] * tensor
        + [jax.ShapeDtypeStruct((blocks, rank, up.shape[2]), up.dtype)],
        in_specs=[SMEM] + [ANY] * 3 + [VMEM] * len(earlier) + [ANY] * (2 * len(ups)),
        out_specs=[VMEM] * (tensor + 1),
        scratch_shapes=[
            pltpu.VMEM((blocks, BLOCK, width), x.dtype),
            pltpu.VMEM((blocks, rank, width), down.dtype),
            pltpu.SemaphoreType.DMA((2 * blocks,)),
        ],
        compiler_params=pltpu.CompilerParams(vmem_limit_bytes=24 * MIB),
        cost_estimate=pl.CostEstimate(
            flops=2 * blocks * BLOCK * rank * width,
            bytes_accessed=2 * blocks * width * (BLOCK + rank),
            transcendentals=0,
        ),
        name="low_rank",
    )(plan, x, down, up, *earlier, *ups, *downs)


def window_kernel(hops, share, pad, *refs):
    pieces = refs[:share]
    own = refs[share]
    segments = refs[share + 1 : share + 2 + hops]
    keys, values, starts, firsts, buffer, sems = refs[share + 2 + hops :]
    rows = own.shape[0]
    part = rows // share
    blocks = rows // BLOCK
    member = lax.rem(lax.axis_index("tensor"), share)
    store = lax.axis_index("store")
    moves = [
        pltpu.make_async_copy(own, buffer.at[pl.ds(hops * rows, rows)], sems.at[hops * share])
    ]
    for hop in range(hops):
        for m in range(share):
            at = pl.multiple_of((hops - 1 - hop) * rows + (member ^ m) * part, part)
            moves.append(
                pltpu.make_async_copy(
                    pieces[m].at[hop], buffer.at[pl.ds(at, part)], sems.at[hop * share + m]
                )
            )
    for move in moves:
        move.start()
    empty = jnp.maximum(hops - store, 0) * rows
    names = segments[0][...]
    start = jnp.zeros(names.shape, jnp.int32) + empty
    for value in range(1, SEGMENTS):
        before = empty.astype(jnp.float32)
        for hop in range(hops + 1):
            below = (segments[hop][...] < value).astype(jnp.float32)
            before = before + jnp.where(hop <= store, jnp.sum(below), 0.0)
        start = jnp.where(names == value, before.astype(jnp.int32), start)
    starts[...] = start.reshape(starts.shape)
    for j in range(blocks):
        firsts[j] = jnp.min(start[j : j + 1].astype(jnp.float32)).astype(jnp.int32)
    for move in moves:
        move.wait()
    keys[pl.ds(0, pad), :] = jnp.zeros((pad, HEAD_SIZE), keys.dtype)
    values[:, pl.ds(0, pad)] = jnp.zeros((HEAD_SIZE, pad), values.dtype)

    def turn(c, _):
        at = pl.ds(pl.multiple_of(c * 256, 256), 256)
        to = pl.ds(pl.multiple_of(pad + c * 256, 256), 256)
        keys[to, :] = buffer[at, pl.ds(0, HEAD_SIZE)]
        values[:, to] = buffer[at, pl.ds(HEAD_SIZE, HEAD_SIZE)].astype(jnp.float32).T.astype(
            values.dtype
        )
        return 0

    lax.fori_loop(0, (hops + 1) * rows // 256, turn, 0)


def window(pieces, own, segments, hops, share, pad):
    rows = own.shape[0]
    length = pad + (hops + 1) * rows
    return pl.pallas_call(
        functools.partial(window_kernel, hops, share, pad),
        out_shape=[
            jax.ShapeDtypeStruct((length, HEAD_SIZE), own.dtype),
            jax.ShapeDtypeStruct((HEAD_SIZE, length), own.dtype),
            jax.ShapeDtypeStruct((rows // BLOCK, 1, BLOCK), jnp.int32),
            jax.ShapeDtypeStruct((rows // BLOCK,), jnp.int32),
        ],
        in_specs=[ANY] * (len(pieces) + 1) + [VMEM] * (hops + 1),
        out_specs=[VMEM, VMEM, VMEM, SMEM],
        scratch_shapes=[
            pltpu.VMEM(((hops + 1) * rows, 2 * HEAD_SIZE), own.dtype),
            pltpu.SemaphoreType.DMA((hops * share + 1,)),
        ],
        compiler_params=pltpu.CompilerParams(vmem_limit_bytes=24 * MIB),
        cost_estimate=pl.CostEstimate(
            flops=0, bytes_accessed=8 * length * HEAD_SIZE, transcendentals=0
        ),
        name="window",
    )(*pieces, own, *segments)


def base_kernel(x, weight, out, total):
    k = pl.program_id(0)
    product = jnp.dot(x[...], weight[...], preferred_element_type=jnp.float32)

    @pl.when(k == 0)
    def _():
        total[...] = product

    @pl.when(k > 0)
    def _():
        total[...] += product

    @pl.when(k == pl.num_programs(0) - 1)
    def _():
        out[...] = total[...].T


def base_queries(x, weight):
    rows, width = x.shape
    columns = weight.shape[1]
    deep = min(width, 1024)
    return pl.pallas_call(
        base_kernel,
        out_shape=jax.ShapeDtypeStruct((columns, rows), jnp.float32),
        grid=(width // deep,),
        in_specs=[
            pl.BlockSpec((rows, deep), lambda k: (0, k)),
            pl.BlockSpec((deep, columns), lambda k: (k, 0)),
        ],
        out_specs=pl.BlockSpec((columns, rows), lambda k: (0, 0)),
        scratch_shapes=[pltpu.VMEM((rows, columns), jnp.float32)],
        compiler_params=pltpu.CompilerParams(vmem_limit_bytes=24 * MIB),
        cost_estimate=pl.CostEstimate(
            flops=2 * rows * width * columns,
            bytes_accessed=2 * width * (rows + columns),
            transcendentals=0,
        ),
        name="base",
    )(x, weight)


def attention_kernel(
    hops, tensor, pad, heads, firsts, base, starts, keys, values, selected, *refs
):
    ranks = refs[:tensor]
    out, even, odd, even_largest, odd_largest, top, total, summed, queries = refs[tensor:]
    j = pl.program_id(0)
    share = ranks[0].shape[0]
    member = lax.axis_index("tensor") if tensor > 1 else 0
    rows = (keys.shape[0] - pad) // (hops + 1)
    for t in range(STRIDE // BLOCK):
        block = j * (STRIDE // BLOCK) + t
        low = jnp.zeros(ranks[0].shape[1:], jnp.bfloat16)
        for m in range(tensor):
            for i in range(share):
                low = jnp.where(block == (member ^ m) * share + i, ranks[m][i], low)
        term = lax.dot_general(
            selected[t], low, (((0,), (0,)), ((), ())), preferred_element_type=jnp.float32
        )
        turned = (base[:, t * BLOCK : (t + 1) * BLOCK] + term).astype(jnp.bfloat16)
        for h in range(heads):
            queries[:, h * STRIDE + t * BLOCK : h * STRIDE + (t + 1) * BLOCK] = turned[
                h * HEAD_SIZE : (h + 1) * HEAD_SIZE
            ]
    q = queries[...]
    columns = heads * STRIDE
    start = jnp.concatenate([starts[t] for t in range(STRIDE // BLOCK)] * heads, axis=1) + pad
    end = pad + hops * rows + (j + 1) * STRIDE
    steps = lax.div(
        end - pad - firsts[j * (STRIDE // BLOCK)] + CHUNK - 1, jnp.int32(CHUNK)
    )
    scale = HEAD_SIZE**-0.5 * math.log2(math.e)
    key = lax.broadcasted_iota(jnp.int32, (CHUNK, columns), 0)

    def place_of(c):
        return pl.multiple_of(jnp.maximum(end - (c + 1) * CHUNK, 0), BLOCK)

    def score(c, buffer, largest, diagonal):
        at = place_of(c)
        s = jnp.dot(keys[pl.ds(at, CHUNK), :], q, preferred_element_type=jnp.float32)
        allowed = key >= start - at
        if diagonal:
            token = lax.rem(lax.broadcasted_iota(jnp.int32, (1, columns), 1), STRIDE)
            allowed = allowed & (key <= token + (CHUNK - STRIDE))
        s = jnp.where(allowed, s, jnp.float32(-1e30))
        buffer[...] = s
        largest[...] = jnp.max(s.reshape(CHUNK // 8, 8, columns), axis=0)

    def weigh(c, buffer, largest):
        before = top[...]
        now = jnp.maximum(before, jnp.max(largest[...], axis=0, keepdims=True))
        top[...] = now
        fade = jnp.exp2((before - now) * scale)
        w = jnp.exp2((buffer[...] - now) * scale)
        total[...] = total[...] * fade + jnp.sum(w.reshape(CHUNK // 8, 8, columns), axis=0)
        summed[...] = summed[...] * fade + jnp.dot(
            values[:, pl.ds(place_of(c), CHUNK)],
            w.astype(jnp.bfloat16),
            preferred_element_type=jnp.float32,
        )

    top[...] = jnp.full(top.shape, -1e30, jnp.float32)
    total[...] = jnp.zeros(total.shape, jnp.float32)
    summed[...] = jnp.zeros(summed.shape, jnp.float32)
    score(0, even, even_largest, True)

    def two(i, _):
        score(2 * i + 1, odd, odd_largest, False)
        weigh(2 * i, even, even_largest)

        @pl.when(2 * i + 1 < steps)
        def _():
            score(2 * i + 2, even, even_largest, False)
            weigh(2 * i + 1, odd, odd_largest)

        return 0

    lax.fori_loop(0, lax.div(steps + 1, jnp.int32(2)), two, 0)
    attended = summed[...] / jnp.sum(total[...], axis=0, keepdims=True)
    for h in range(heads):
        out[:, h * HEAD_SIZE : (h + 1) * HEAD_SIZE] = (
            attended[:, h * STRIDE : (h + 1) * STRIDE].T.astype(out.dtype)
        )


def attention(firsts, base, starts, keys, values, selected, ranks, hops, pad, heads):
    columns, rows = base.shape
    group = STRIDE // BLOCK
    length = keys.shape[0]
    whole = lambda shape: pl.BlockSpec(shape, lambda j, *_: (0,) * len(shape))
    return pl.pallas_call(
        functools.partial(attention_kernel, hops, len(ranks), pad, heads),
        out_shape=jax.ShapeDtypeStruct((rows, columns), jnp.bfloat16),
        grid_spec=pltpu.PrefetchScalarGridSpec(
            num_scalar_prefetch=1,
            grid=(rows // STRIDE,),
            in_specs=[
                pl.BlockSpec((columns, STRIDE), lambda j, *_: (0, j)),
                pl.BlockSpec((group, 1, BLOCK), lambda j, *_: (j, 0, 0)),
                whole(keys.shape),
                whole(values.shape),
                pl.BlockSpec((group,) + selected.shape[1:], lambda j, *_: (j, 0, 0)),
            ]
            + [whole(r.shape) for r in ranks],
            out_specs=pl.BlockSpec((STRIDE, columns), lambda j, *_: (j, 0)),
            scratch_shapes=[
                pltpu.VMEM((CHUNK, heads * STRIDE), jnp.float32),
                pltpu.VMEM((CHUNK, heads * STRIDE), jnp.float32),
                pltpu.VMEM((8, heads * STRIDE), jnp.float32),
                pltpu.VMEM((8, heads * STRIDE), jnp.float32),
                pltpu.VMEM((1, heads * STRIDE), jnp.float32),
                pltpu.VMEM((8, heads * STRIDE), jnp.float32),
                pltpu.VMEM((HEAD_SIZE, heads * STRIDE), jnp.float32),
                pltpu.VMEM((HEAD_SIZE, heads * STRIDE), jnp.bfloat16),
            ],
        ),
        compiler_params=pltpu.CompilerParams(vmem_limit_bytes=40 * MIB),
        cost_estimate=pl.CostEstimate(
            flops=2 * rows * columns * length,
            bytes_accessed=8 * length * HEAD_SIZE,
            transcendentals=rows * heads * length,
        ),
        name="attention",
    )(firsts, base, starts, keys, values, selected, *ranks)


def per_device(
    mesh_shape,
    normed_input,
    query_weight,
    down_factors,
    up_factors,
    adapter_per_block,
    key_value_cache,
    token_segment,
):
    groups, tensor, stores = (mesh_shape[a] for a in ("groups", "tensor", "store"))
    rows = normed_input.shape[0]
    blocks = adapter_per_block.shape[0]
    heads = query_weight.shape[1] // HEAD_SIZE
    per_store = down_factors.shape[0]
    member = lax.axis_index("tensor")
    slots = slot_bound(stores, per_store, blocks)
    batches = slots // BATCH
    usual = min(batches, USUAL)
    more = min(batches, usual + MORE)
    hops = min(stores - 1, -(-(stores * rows // 2 - 1) // rows))
    share = min(tensor, max(1, GROUP // heads))
    quarter = rows // share
    exchange = tensor if blocks % tensor == 0 else 1
    raise_up = [(i, i + 1) for i in range(stores - 1)]
    raise_down = [(i + 1, i) for i in range(stores - 1)]
    pairs = lambda m: [(t, t ^ m) for t in range(tensor)]

    indices = [adapter_per_block] + [
        lax.ppermute(adapter_per_block, "store", [(i, (i + m) % stores) for i in range(stores)])
        for m in range(1, stores)
    ]
    down = jnp.swapaxes(down_factors, 1, 2)

    cache = jnp.swapaxes(key_value_cache, 0, 1)
    cache = lax.dynamic_index_in_dim(cache, member * heads // GROUP, 0, keepdims=False)
    quarters = [lax.dynamic_slice_in_dim(cache, lax.rem(member, share) * quarter, quarter, 0)]
    plan = make_plan(indices, stores, blocks, per_store, slots)
    later = lambda v: lax.ppermute(v, "store", raise_up)
    segments = [token_segment]

    def fetch(first, last, ups, downs, plan, beside=()):
        ups, downs = list(ups), list(downs)
        for k in range(first, last):
            sent_up = pack(plan, down, up_factors, ups[:k], 0, slots)
            sent_down = pack(plan, down, up_factors, downs[:k], 1, slots)
            ups.append(lax.ppermute(sent_up, "store", raise_up))
            downs.append(lax.ppermute(sent_down, "store", raise_down))
            if k < len(beside):
                plan, done = lax.optimization_barrier((plan, beside[k]()))
                found.append(done)
        return ups, downs, plan

    def one_hop():
        quarters.append(later(quarters[-1]))
        segments.append(later(segments[-1]))
        return quarters[-1], segments[-1]

    found = []
    beside = [lambda: base_queries(normed_input, query_weight)]
    beside += [one_hop] * (hops if hops <= usual - 2 else 0)
    ups, downs, plan = fetch(0, usual, [], [], plan, beside)
    base = found[0]
    for _ in range(hops - (len(beside) - 1)):
        one_hop()
    quarters = jnp.stack(quarters[1:])
    pieces = [quarters] + [lax.ppermute(quarters, "tensor", pairs(m)) for m in range(1, share)]
    plan, *pieces = lax.optimization_barrier((plan, *pieces))
    segments = [s.reshape(-1, BLOCK) for s in segments]
    keys, values, starts, firsts = window(pieces, cache, segments, hops, share, CHUNK)
    former = usual - 1
    earlier_parts = low_rank_parts(
        plan, normed_input, down, up_factors, ups[:former], downs[:former], slots, exchange, blocks
    )

    def low_rank(ups, downs, plan):
        return tuple(
            low_rank_parts(
                plan,
                normed_input,
                down,
                up_factors,
                ups,
                downs,
                slots,
                exchange,
                blocks,
                former * BATCH,
                earlier_parts,
            )
        )

    def finish(parts, selected):
        if exchange > 1:
            total = parts[0]
            for m in range(1, tensor):
                total = total + lax.ppermute(parts[m], "tensor", pairs(m))
            total = total.astype(jnp.bfloat16)
            low = [total] + [lax.ppermute(total, "tensor", pairs(m)) for m in range(1, tensor)]
        else:
            low = [lax.psum(parts[0], "tensor").astype(jnp.bfloat16)]
        return attention(firsts, base, starts, keys, values, selected, low, hops, CHUNK, heads)

    def with_more(ups, downs, plan):
        return low_rank(*fetch(usual, more, ups, downs, plan))

    def with_all(ups, downs, plan, usually):
        *parts, selected = low_rank(*fetch(usual, batches, ups, downs, plan))
        return finish(parts, selected)

    *parts, selected = lax.cond(plan[0] > usual * BATCH, with_more, low_rank, ups, downs, plan)
    usually = finish(parts, selected)
    if more == batches:
        return usually
    return lax.cond(
        plan[0] > more * BATCH,
        with_all,
        lambda ups, downs, plan, usually: usually,
        ups,
        downs,
        plan,
        usually,
    )


def solution(mesh):
    return jax.shard_map(
        functools.partial(per_device, dict(mesh.shape)),
        mesh=mesh,
        in_specs=(
            P(("groups", "store"), None),
            P(None, "tensor"),
            P("store", "tensor", None),
            P("store", None, "tensor"),
            P(("groups", "store")),
            P(("groups", "store"), None, None),
            P(("groups", "store")),
        ),
        out_specs=P(("groups", "store"), "tensor"),
        check_vma=False,
    )
```

```python
import functools
import math

import jax
import jax.numpy as jnp
from jax import lax
from jax.experimental import pallas as pl
from jax.experimental.pallas import tpu as pltpu
from jax.sharding import PartitionSpec as P

HEAD_SIZE = 128
GROUP = 8
BLOCK = 128
ADAPTERS = 64
SEGMENTS = 4
SEGMENT_ROWS = 16
BATCH = 2
LAG = BATCH
USUAL = 4
MORE = 1
STRIDE = 2 * BLOCK
CHUNK = 512
MIB = 1 << 20
ANY = pl.BlockSpec(memory_space=pl.ANY)
SMEM = pl.BlockSpec(memory_space=pltpu.SMEM)
VMEM = pl.BlockSpec(memory_space=pltpu.VMEM)


def slot_bound(stores, per_store, blocks):
    load = max(
        min(per_store * (link + 1), blocks * (stores - 1 - link)) for link in range(stores - 1)
    )
    return -(-(load + (stores - 2) * LAG) // BATCH) * BATCH


def plan_kernel(stores, blocks, per_store, slots, *refs):
    index_refs = refs[:stores]
    plan, names, place, listed, bases, counts = refs[stores:]
    capacity = per_store + 1
    my_store = lax.axis_index("store")
    zero = jnp.int32(0)
    for shift in range(stores):
        origin = lax.rem(my_store + stores - shift, stores)
        for b in range(blocks):
            names[origin * blocks + b] = index_refs[shift][b]
    for i in range(2 * ADAPTERS):
        place[i] = jnp.int32(-1)
    for i in range(2 * slots):
        plan[1 + i] = zero
    most = zero
    for way in range(2):
        count = [zero] * stores
        crossing = [[zero] * stores for _ in range(stores)]
        for dest in range(stores - 1, 0, -1):
            real = dest if way == 0 else stores - 1 - dest
            for b in range(blocks):
                name = names[real * blocks + b]
                owner = lax.div(name, jnp.int32(per_store))
                if way == 1:
                    owner = stores - 1 - owner
                held = place[way * ADAPTERS + name]
                new = (owner < dest) & (held < 0)
                at = zero
                for o in range(stores):
                    at = jnp.where(owner == o, count[o], at)
                listed[(way * stores + owner) * capacity + at] = name
                place[way * ADAPTERS + name] = jnp.where(new, at, held)
                step = new.astype(jnp.int32)
                for o in range(dest):
                    count[o] = count[o] + jnp.where(owner == o, step, 0)
            for o in range(dest):
                crossing[o][dest - 1] = count[o]
        base = [[zero] * stores for _ in range(stores)]
        for link in range(stores):
            cursor = zero
            for o in range(stores):
                spot = (way * stores + link) * stores + o
                bases[spot] = zero
                counts[spot] = zero
            if link == stores - 1:
                continue
            for o in range(link, -1, -1):
                start = cursor if o == link else jnp.maximum(cursor, base[link - 1][o] + LAG)
                base[link][o] = start
                number = crossing[o][link]
                spot = (way * stores + link) * stores + o
                bases[spot] = start
                counts[spot] = number
                cursor = jnp.where(number > 0, start + number, cursor)
            most = jnp.maximum(most, cursor)
    plan[0] = most
    for way in range(2):
        mine = my_store if way == 0 else stores - 1 - my_store
        for o in range(stores - 1):
            spot = (way * stores + mine) * stores + o
            before = (way * stores + jnp.maximum(mine - 1, 0)) * stores + o
            start = bases[spot]
            earlier = bases[before]
            row = (way * stores + o) * capacity

            def fill(r, _):
                own = listed[row + r] - my_store * per_store
                plan[1 + way * slots + start + r] = jnp.where(
                    mine == o, own, per_store + way * slots + earlier + r
                )
                return 0

            lax.fori_loop(0, counts[spot], fill, 0)
    for b in range(blocks):
        name = names[my_store * blocks + b]
        owner = lax.div(name, jnp.int32(per_store))
        source = name - my_store * per_store
        for way in range(2):
            mine = my_store if way == 0 else stores - 1 - my_store
            far = owner if way == 0 else stores - 1 - owner
            spot = (way * stores + jnp.maximum(mine - 1, 0)) * stores + far
            arrives = per_store + way * slots + bases[spot] + place[way * ADAPTERS + name]
            source = jnp.where(far < mine, arrives, source)
        plan[1 + 2 * slots + b] = source


def make_plan(shifted, stores, blocks, per_store, slots):
    return pl.pallas_call(
        functools.partial(plan_kernel, stores, blocks, per_store, slots),
        out_shape=jax.ShapeDtypeStruct((1 + 2 * slots + blocks,), jnp.int32),
        in_specs=[SMEM] * len(shifted),
        out_specs=SMEM,
        scratch_shapes=[
            pltpu.SMEM((stores * blocks,), jnp.int32),
            pltpu.SMEM((2 * ADAPTERS,), jnp.int32),
            pltpu.SMEM((2 * stores * (per_store + 1),), jnp.int32),
            pltpu.SMEM((2 * stores * stores,), jnp.int32),
            pltpu.SMEM((2 * stores * stores,), jnp.int32),
        ],
        name="plan",
    )(*shifted)


def pack_kernel(slots, per_store, way, batch, plan, down, up, *refs):
    got = refs[:batch]
    out, sems = refs[batch:]
    width = down.shape[2]

    def copies(i):
        source = plan[1 + way * slots + batch * BATCH + i]
        own = jnp.minimum(source, per_store - 1)
        pairs = [
            (
                source < per_store,
                [
                    pltpu.make_async_copy(
                        down.at[own], out.at[i, :, pl.ds(0, width)], sems.at[i]
                    ),
                    pltpu.make_async_copy(
                        up.at[own], out.at[i, :, pl.ds(width, up.shape[2])], sems.at[i]
                    ),
                ],
            )
        ]
        for j in range(batch * BATCH):
            pairs.append(
                (
                    source == per_store + way * slots + j,
                    [pltpu.make_async_copy(got[j // BATCH].at[j % BATCH], out.at[i], sems.at[i])],
                )
            )
        return pairs

    for act in ("start", "wait"):
        for i in range(BATCH):
            for chosen, moves in copies(i):

                @pl.when(chosen)
                def _():
                    for move in moves:
                        getattr(move, act)()


def pack(plan, down, up, got, way, slots):
    per_store, rank, width = down.shape
    item = jax.ShapeDtypeStruct((BATCH, rank, width + up.shape[2]), down.dtype)
    return pl.pallas_call(
        functools.partial(pack_kernel, slots, per_store, way, len(got)),
        out_shape=item,
        in_specs=[SMEM] + [ANY] * (2 + len(got)),
        out_specs=VMEM,
        scratch_shapes=[pltpu.SemaphoreType.DMA((BATCH,))],
        compiler_params=pltpu.CompilerParams(vmem_limit_bytes=16 * MIB),
        cost_estimate=pl.CostEstimate(
            flops=5 * 10**8, bytes_accessed=4 * math.prod(item.shape), transcendentals=0
        ),
        name="pack",
    )(plan, down, up, *got)


def low_rank_kernel(slots, per_store, former, received, tensor, plan, x, down, up, *refs):
    earlier = refs[: tensor + 1] if former is not None else ()
    refs = refs[len(earlier) :]
    number = 2 * received // BATCH
    got = refs[:number]
    outs = refs[number : number + tensor]
    selected, x_rows, factors, sems = refs[number + tensor :]
    blocks, rank, width = factors.shape
    share = blocks // tensor
    member = lax.axis_index("tensor")
    columns = pl.ds(pl.multiple_of(member * width, 128), width)
    if tensor == 1:
        member = 0

    def within(source, number):
        return (source < per_store + number) | (
            (source >= per_store + slots) & (source < per_store + slots + number)
        )

    def due(b):
        source = plan[1 + 2 * slots + b]
        if former is None:
            return within(source, received)
        return jnp.logical_not(within(source, former))

    def copies(b):
        source = plan[1 + 2 * slots + b]
        source = jnp.where(within(source, received), source, 0)
        own = jnp.minimum(source, per_store - 1)
        pairs = [
            (
                source < per_store,
                [
                    pltpu.make_async_copy(down.at[own], factors.at[b], sems.at[b]),
                    pltpu.make_async_copy(up.at[own], selected.at[b], sems.at[b]),
                ],
            )
        ]
        for j in range(2 * received):
            spot = j if j < received else slots + j - received
            item = got[j // BATCH].at[j % BATCH]
            pairs.append(
                (
                    source == per_store + spot,
                    [
                        pltpu.make_async_copy(
                            item.at[:, pl.ds(0, width)], factors.at[b], sems.at[b]
                        ),
                        pltpu.make_async_copy(
                            item.at[:, pl.ds(width, up.shape[2])], selected.at[b], sems.at[b]
                        ),
                    ],
                )
            )
        return pairs

    def rows_of(b):
        rows = pl.ds(pl.multiple_of(b * BLOCK, BLOCK), BLOCK)
        return pltpu.make_async_copy(x.at[rows, columns], x_rows.at[b], sems.at[blocks + b])

    if former is not None:
        selected[...] = earlier[tensor][...]
    else:
        selected[...] = jnp.zeros_like(selected)

    def start(b, _):
        @pl.when(due(b))
        def _():
            rows_of(b).start()
            for chosen, moves in copies(b):

                @pl.when(chosen)
                def _():
                    for move in moves:
                        move.start()

        return 0

    lax.fori_loop(0, blocks, start, 0)
    for m in range(tensor):
        for i in range(share):
            b = (member ^ m) * share + i
            wanted = due(b)

            @pl.when(wanted)
            def _():
                pltpu.make_async_copy(down.at[0], factors.at[b], sems.at[b]).wait()
                pltpu.make_async_copy(up.at[0], selected.at[b], sems.at[b]).wait()
                rows_of(b).wait()
                outs[m][i] = lax.dot_general(
                    x_rows[b],
                    factors[b],
                    (((1,), (1,)), ((), ())),
                    preferred_element_type=jnp.float32,
                ).T

            @pl.when(jnp.logical_not(wanted))
            def _():
                if former is not None:
                    outs[m][i] = earlier[m][i]
                else:
                    outs[m][i] = jnp.zeros(outs[m].shape[1:], jnp.float32)


def low_rank_parts(plan, x, down, up, ups, downs, slots, tensor, blocks, former=None, earlier=()):
    per_store, rank, width = down.shape
    share = blocks // tensor
    return pl.pallas_call(
        functools.partial(
            low_rank_kernel, slots, per_store, former, BATCH * len(ups), tensor
        ),
        out_shape=[jax.ShapeDtypeStruct((share, rank, BLOCK), jnp.float32)] * tensor
        + [jax.ShapeDtypeStruct((blocks, rank, up.shape[2]), up.dtype)],
        in_specs=[SMEM] + [ANY] * 3 + [VMEM] * len(earlier) + [ANY] * (2 * len(ups)),
        out_specs=[VMEM] * (tensor + 1),
        scratch_shapes=[
            pltpu.VMEM((blocks, BLOCK, width), x.dtype),
            pltpu.VMEM((blocks, rank, width), down.dtype),
            pltpu.SemaphoreType.DMA((2 * blocks,)),
        ],
        compiler_params=pltpu.CompilerParams(vmem_limit_bytes=50 * MIB),
        cost_estimate=pl.CostEstimate(
            flops=6 * 10**9,
            bytes_accessed=2 * blocks * width * (BLOCK + rank),
            transcendentals=0,
        ),
        name="low_rank",
    )(plan, x, down, up, *earlier, *ups, *downs)


def window_kernel(hops, share, pad, *refs):
    pieces = refs[:share]
    own, segments, keys, values, starts, firsts, buffer, others, sems = refs[share:]
    rows = own.shape[0]
    part = rows // share
    blocks = rows // BLOCK
    member = lax.rem(lax.axis_index("tensor"), share)
    store = lax.axis_index("store")
    moves = [
        pltpu.make_async_copy(own, buffer.at[pl.ds(hops * rows, rows)], sems.at[hops * share])
    ]
    for hop in range(hops):
        for m in range(share):
            at = pl.multiple_of((hops - 1 - hop) * rows + (member ^ m) * part, part)
            moves.append(
                pltpu.make_async_copy(
                    pieces[m].at[hop, pl.ds(0, part)],
                    buffer.at[pl.ds(at, part)],
                    sems.at[hop * share + m],
                )
            )
        moves.append(
            pltpu.make_async_copy(
                pieces[0].at[hop, pl.ds(part, SEGMENT_ROWS)],
                others.at[hop],
                sems.at[hops * share + 1 + hop],
            )
        )
    for move in moves:
        move.start()
    empty = jnp.maximum(hops - store, 0) * rows
    names = segments[...]
    for move in moves:
        move.wait()
    start = jnp.zeros(names.shape, jnp.int32) + empty
    for value in range(1, SEGMENTS):
        before = empty.astype(jnp.float32)
        before = before + jnp.sum((names < value).astype(jnp.float32))
        for hop in range(hops):
            below = (others[hop].astype(jnp.float32) < value).astype(jnp.float32)
            before = before + jnp.where(hop < store, jnp.sum(below), 0.0)
        start = jnp.where(names == value, before.astype(jnp.int32), start)
    starts[...] = start.reshape(starts.shape)
    for j in range(blocks):
        firsts[j] = jnp.min(start[j : j + 1].astype(jnp.float32)).astype(jnp.int32)
    keys[pl.ds(0, pad), :] = jnp.zeros((pad, HEAD_SIZE), keys.dtype)
    values[:, pl.ds(0, pad)] = jnp.zeros((HEAD_SIZE, pad), values.dtype)

    def turn(c, _):
        at = pl.ds(pl.multiple_of(c * 256, 256), 256)
        to = pl.ds(pl.multiple_of(pad + c * 256, 256), 256)
        keys[to, :] = buffer[at, pl.ds(0, HEAD_SIZE)]
        values[:, to] = buffer[at, pl.ds(HEAD_SIZE, HEAD_SIZE)].astype(jnp.float32).T.astype(
            values.dtype
        )
        return 0

    lax.fori_loop(0, (hops + 1) * rows // 256, turn, 0)


def window(pieces, own, segments, hops, share, pad):
    rows = own.shape[0]
    length = pad + (hops + 1) * rows
    return pl.pallas_call(
        functools.partial(window_kernel, hops, share, pad),
        out_shape=[
            jax.ShapeDtypeStruct((length, HEAD_SIZE), own.dtype),
            jax.ShapeDtypeStruct((HEAD_SIZE, length), own.dtype),
            jax.ShapeDtypeStruct((rows // BLOCK, 1, BLOCK), jnp.int32),
            jax.ShapeDtypeStruct((rows // BLOCK,), jnp.int32),
        ],
        in_specs=[ANY] * (len(pieces) + 1) + [VMEM],
        out_specs=[VMEM, VMEM, VMEM, SMEM],
        scratch_shapes=[
            pltpu.VMEM(((hops + 1) * rows, 2 * HEAD_SIZE), own.dtype),
            pltpu.VMEM((hops, SEGMENT_ROWS, own.shape[1]), own.dtype),
            pltpu.SemaphoreType.DMA((hops * share + 1 + hops,)),
        ],
        compiler_params=pltpu.CompilerParams(vmem_limit_bytes=24 * MIB),
        cost_estimate=pl.CostEstimate(
            flops=0, bytes_accessed=8 * length * HEAD_SIZE, transcendentals=0
        ),
        name="window",
    )(*pieces, own, segments)


def base_kernel(x, weight, out, total):
    k = pl.program_id(0)
    product = jnp.dot(x[...], weight[...], preferred_element_type=jnp.float32)

    @pl.when(k == 0)
    def _():
        total[...] = product

    @pl.when(k > 0)
    def _():
        total[...] += product

    @pl.when(k == pl.num_programs(0) - 1)
    def _():
        out[...] = total[...].T


def base_queries(x, weight):
    rows, width = x.shape
    columns = weight.shape[1]
    deep = min(width, 1024)
    return pl.pallas_call(
        base_kernel,
        out_shape=jax.ShapeDtypeStruct((columns, rows), jnp.float32),
        grid=(width // deep,),
        in_specs=[
            pl.BlockSpec((rows, deep), lambda k: (0, k)),
            pl.BlockSpec((deep, columns), lambda k: (k, 0)),
        ],
        out_specs=pl.BlockSpec((columns, rows), lambda k: (0, 0)),
        scratch_shapes=[pltpu.VMEM((rows, columns), jnp.float32)],
        compiler_params=pltpu.CompilerParams(vmem_limit_bytes=24 * MIB),
        cost_estimate=pl.CostEstimate(
            flops=2 * rows * width * columns,
            bytes_accessed=2 * width * (rows + columns),
            transcendentals=0,
        ),
        name="base",
    )(x, weight)


def attention_kernel(
    hops, tensor, pad, heads, firsts, base, starts, keys, values, selected, *refs
):
    ranks = refs[:tensor]
    out, even, odd, even_largest, odd_largest, top, total, summed, queries = refs[tensor:]
    j = pl.program_id(0)
    share = ranks[0].shape[0]
    member = lax.axis_index("tensor") if tensor > 1 else 0
    rows = (keys.shape[0] - pad) // (hops + 1)
    for t in range(STRIDE // BLOCK):
        block = j * (STRIDE // BLOCK) + t
        low = jnp.zeros(ranks[0].shape[1:], jnp.bfloat16)
        for m in range(tensor):
            for i in range(share):
                low = jnp.where(block == (member ^ m) * share + i, ranks[m][i], low)
        term = lax.dot_general(
            selected[t], low, (((0,), (0,)), ((), ())), preferred_element_type=jnp.float32
        )
        turned = (base[:, t * BLOCK : (t + 1) * BLOCK] + term).astype(jnp.bfloat16)
        for h in range(heads):
            queries[:, h * STRIDE + t * BLOCK : h * STRIDE + (t + 1) * BLOCK] = turned[
                h * HEAD_SIZE : (h + 1) * HEAD_SIZE
            ]
    q = queries[...]
    columns = heads * STRIDE
    start = jnp.concatenate([starts[t] for t in range(STRIDE // BLOCK)] * heads, axis=1) + pad
    end = pad + hops * rows + (j + 1) * STRIDE
    steps = lax.div(
        end - pad - firsts[j * (STRIDE // BLOCK)] + CHUNK - 1, jnp.int32(CHUNK)
    )
    scale = HEAD_SIZE**-0.5 * math.log2(math.e)
    key = lax.broadcasted_iota(jnp.int32, (CHUNK, columns), 0)

    def place_of(c):
        return pl.multiple_of(jnp.maximum(end - (c + 1) * CHUNK, 0), BLOCK)

    def score(c, buffer, largest, diagonal):
        at = place_of(c)
        s = jnp.dot(keys[pl.ds(at, CHUNK), :], q, preferred_element_type=jnp.float32)
        allowed = key >= start - at
        if diagonal:
            token = lax.rem(lax.broadcasted_iota(jnp.int32, (1, columns), 1), STRIDE)
            allowed = allowed & (key <= token + (CHUNK - STRIDE))
        s = jnp.where(allowed, s, jnp.float32(-1e30))
        buffer[...] = s
        largest[...] = jnp.max(s.reshape(CHUNK // 8, 8, columns), axis=0)

    def weigh(c, buffer, largest):
        before = top[...]
        now = jnp.maximum(before, jnp.max(largest[...], axis=0, keepdims=True))
        top[...] = now
        fade = jnp.exp2((before - now) * scale)
        w = jnp.exp2((buffer[...] - now) * scale)
        total[...] = total[...] * fade + jnp.sum(w.reshape(CHUNK // 8, 8, columns), axis=0)
        summed[...] = summed[...] * fade + jnp.dot(
            values[:, pl.ds(place_of(c), CHUNK)],
            w.astype(jnp.bfloat16),
            preferred_element_type=jnp.float32,
        )

    top[...] = jnp.full(top.shape, -1e30, jnp.float32)
    total[...] = jnp.zeros(total.shape, jnp.float32)
    summed[...] = jnp.zeros(summed.shape, jnp.float32)
    score(0, even, even_largest, True)

    def two(i, _):
        score(2 * i + 1, odd, odd_largest, False)
        weigh(2 * i, even, even_largest)

        @pl.when(2 * i + 1 < steps)
        def _():
            score(2 * i + 2, even, even_largest, False)
            weigh(2 * i + 1, odd, odd_largest)

        return 0

    lax.fori_loop(0, lax.div(steps + 1, jnp.int32(2)), two, 0)
    attended = summed[...] / jnp.sum(total[...], axis=0, keepdims=True)
    for h in range(heads):
        out[:, h * HEAD_SIZE : (h + 1) * HEAD_SIZE] = (
            attended[:, h * STRIDE : (h + 1) * STRIDE].T.astype(out.dtype)
        )


def attention(firsts, base, starts, keys, values, selected, ranks, hops, pad, heads):
    columns, rows = base.shape
    group = STRIDE // BLOCK
    length = keys.shape[0]
    whole = lambda shape: pl.BlockSpec(shape, lambda j, *_: (0,) * len(shape))
    return pl.pallas_call(
        functools.partial(attention_kernel, hops, len(ranks), pad, heads),
        out_shape=jax.ShapeDtypeStruct((rows, columns), jnp.bfloat16),
        grid_spec=pltpu.PrefetchScalarGridSpec(
            num_scalar_prefetch=1,
            grid=(rows // STRIDE,),
            in_specs=[
                pl.BlockSpec((columns, STRIDE), lambda j, *_: (0, j)),
                pl.BlockSpec((group, 1, BLOCK), lambda j, *_: (j, 0, 0)),
                whole(keys.shape),
                whole(values.shape),
                pl.BlockSpec((group,) + selected.shape[1:], lambda j, *_: (j, 0, 0)),
            ]
            + [whole(r.shape) for r in ranks],
            out_specs=pl.BlockSpec((STRIDE, columns), lambda j, *_: (j, 0)),
            scratch_shapes=[
                pltpu.VMEM((CHUNK, heads * STRIDE), jnp.float32),
                pltpu.VMEM((CHUNK, heads * STRIDE), jnp.float32),
                pltpu.VMEM((8, heads * STRIDE), jnp.float32),
                pltpu.VMEM((8, heads * STRIDE), jnp.float32),
                pltpu.VMEM((1, heads * STRIDE), jnp.float32),
                pltpu.VMEM((8, heads * STRIDE), jnp.float32),
                pltpu.VMEM((HEAD_SIZE, heads * STRIDE), jnp.float32),
                pltpu.VMEM((HEAD_SIZE, heads * STRIDE), jnp.bfloat16),
            ],
        ),
        compiler_params=pltpu.CompilerParams(vmem_limit_bytes=40 * MIB),
        cost_estimate=pl.CostEstimate(
            flops=2 * rows * columns * length,
            bytes_accessed=8 * length * HEAD_SIZE,
            transcendentals=rows * heads * length,
        ),
        name="attention",
    )(firsts, base, starts, keys, values, selected, *ranks)


def per_device(
    mesh_shape,
    normed_input,
    query_weight,
    down_factors,
    up_factors,
    adapter_per_block,
    key_value_cache,
    token_segment,
):
    groups, tensor, stores = (mesh_shape[a] for a in ("groups", "tensor", "store"))
    rows = normed_input.shape[0]
    blocks = adapter_per_block.shape[0]
    heads = query_weight.shape[1] // HEAD_SIZE
    per_store = down_factors.shape[0]
    member = lax.axis_index("tensor")
    slots = slot_bound(stores, per_store, blocks)
    batches = slots // BATCH
    usual = min(batches, USUAL)
    more = min(batches, usual + MORE)
    hops = min(stores - 1, -(-(stores * rows // 2 - 1) // rows))
    share = min(tensor, max(1, GROUP // heads))
    quarter = rows // share
    exchange = tensor if blocks % tensor == 0 else 1
    raise_up = [(i, i + 1) for i in range(stores - 1)]
    raise_down = [(i + 1, i) for i in range(stores - 1)]
    pairs = lambda m: [(t, t ^ m) for t in range(tensor)]

    indices = [adapter_per_block] + [
        lax.ppermute(adapter_per_block, "store", [(i, (i + m) % stores) for i in range(stores)])
        for m in range(1, stores)
    ]
    down = jnp.swapaxes(down_factors, 1, 2)

    cache = jnp.swapaxes(key_value_cache, 0, 1)
    cache = lax.dynamic_index_in_dim(cache, member * heads // GROUP, 0, keepdims=False)
    quarters = [lax.dynamic_slice_in_dim(cache, lax.rem(member, share) * quarter, quarter, 0)]
    plan = make_plan(indices, stores, blocks, per_store, slots)
    width = quarters[0].shape[1]
    numbers = token_segment.astype(quarters[0].dtype).reshape(-1, width)
    numbers = jnp.pad(numbers, ((0, SEGMENT_ROWS - rows // width), (0, 0)), constant_values=SEGMENTS)
    quarters[0] = jnp.concatenate([quarters[0], numbers])

    def fetch(first, last, ups, downs, plan, beside=()):
        ups, downs = list(ups), list(downs)
        for k in range(first, last):
            sent_up = pack(plan, down, up_factors, ups[:k], 0, slots)
            sent_down = pack(plan, down, up_factors, downs[:k], 1, slots)
            ups.append(lax.ppermute(sent_up, "store", raise_up))
            downs.append(lax.ppermute(sent_down, "store", raise_down))
            if k < len(beside):
                plan, done = lax.optimization_barrier((plan, beside[k]()))
                found.append(done)
        return ups, downs, plan

    def one_hop():
        quarters.append(lax.ppermute(quarters[-1], "store", raise_up))
        return quarters[-1]

    found = []
    beside = [lambda: base_queries(normed_input, query_weight)]
    beside += [one_hop] * (hops if hops <= usual - 2 else 0)
    ups, downs, plan = fetch(0, usual, [], [], plan, beside)
    base = found[0]
    for _ in range(hops - (len(beside) - 1)):
        one_hop()
    quarters = jnp.stack(quarters[1:])
    pieces = [quarters] + [lax.ppermute(quarters, "tensor", pairs(m)) for m in range(1, share)]
    keys, values, starts, firsts = window(
        pieces, cache, token_segment.reshape(-1, BLOCK), hops, share, CHUNK
    )
    former = usual - 1
    earlier_parts = low_rank_parts(
        plan, normed_input, down, up_factors, ups[:former], downs[:former], slots, exchange, blocks
    )

    plan, *_ = lax.optimization_barrier((plan, *pieces))

    def low_rank(ups, downs, plan):
        return tuple(
            low_rank_parts(
                plan,
                normed_input,
                down,
                up_factors,
                ups,
                downs,
                slots,
                exchange,
                blocks,
                former * BATCH,
                earlier_parts,
            )
        )

    def finish(parts, selected):
        if exchange > 1:
            total = parts[0]
            for m in range(1, tensor):
                total = total + lax.ppermute(parts[m], "tensor", pairs(m))
            total = total.astype(jnp.bfloat16)
            low = [total] + [lax.ppermute(total, "tensor", pairs(m)) for m in range(1, tensor)]
        else:
            low = [lax.psum(parts[0], "tensor").astype(jnp.bfloat16)]
        return attention(firsts, base, starts, keys, values, selected, low, hops, CHUNK, heads)

    def with_more(ups, downs, plan):
        return low_rank(*fetch(usual, more, ups, downs, plan))

    def with_all(ups, downs, plan, usually):
        *parts, selected = low_rank(*fetch(usual, batches, ups, downs, plan))
        return finish(parts, selected)

    *parts, selected = lax.cond(plan[0] > usual * BATCH, with_more, low_rank, ups, downs, plan)
    usually = finish(parts, selected)
    if more == batches:
        return usually
    return lax.cond(
        plan[0] > more * BATCH,
        with_all,
        lambda ups, downs, plan, usually: usually,
        ups,
        downs,
        plan,
        usually,
    )


def solution(mesh):
    return jax.shard_map(
        functools.partial(per_device, dict(mesh.shape)),
        mesh=mesh,
        in_specs=(
            P(("groups", "store"), None),
            P(None, "tensor"),
            P("store", "tensor", None),
            P("store", None, "tensor"),
            P(("groups", "store")),
            P(("groups", "store"), None, None),
            P(("groups", "store")),
        ),
        out_specs=P(("groups", "store"), "tensor"),
        check_vma=False,
    )
```

```python
import functools
import math

import jax
import jax.numpy as jnp
from jax import lax
from jax.experimental import pallas as pl
from jax.experimental.pallas import tpu as pltpu
from jax.sharding import PartitionSpec as P

HEAD_SIZE = 128
GROUP = 8
BLOCK = 128
ADAPTERS = 64
SEGMENTS = 4
SEGMENT_ROWS = 16
BATCH = 2
LAG = BATCH
USUAL = 4
MORE = 1
STRIDE = 2 * BLOCK
CHUNK = 512
MIB = 1 << 20
ANY = pl.BlockSpec(memory_space=pl.ANY)
SMEM = pl.BlockSpec(memory_space=pltpu.SMEM)
VMEM = pl.BlockSpec(memory_space=pltpu.VMEM)


def slot_bound(stores, per_store, blocks):
    load = max(
        min(per_store * (link + 1), blocks * (stores - 1 - link)) for link in range(stores - 1)
    )
    return -(-(load + (stores - 2) * LAG) // BATCH) * BATCH


def plan_kernel(stores, blocks, per_store, slots, *refs):
    index_refs = refs[:stores]
    plan, names, place, listed, far, when = refs[stores:]
    capacity = per_store + 1
    unused = 1 + 2 * slots + blocks
    my_store = lax.axis_index("store")
    zero = jnp.int32(0)
    for shift in range(stores):
        origin = lax.rem(my_store + stores - shift, stores)
        for b in range(blocks):
            names[origin * blocks + b] = index_refs[shift][b]
    for i in range(2 * ADAPTERS):
        place[i] = jnp.int32(-1)
    for i in range(2 * slots):
        plan[1 + i] = zero
    most = zero
    for way in range(2):
        mine = my_store if way == 0 else stores - 1 - my_store
        count = [zero] * stores
        crossing = [[zero] * stores for _ in range(stores)]
        for dest in range(stores - 1, 0, -1):
            real = dest if way == 0 else stores - 1 - dest
            for b in range(blocks):
                name = names[real * blocks + b]
                owner = lax.div(name, jnp.int32(per_store))
                if way == 1:
                    owner = stores - 1 - owner
                held = place[way * ADAPTERS + name]
                new = (owner < dest) & (held < 0)
                at = zero
                for o in range(stores):
                    at = jnp.where(owner == o, count[o], at)
                listed[(way * stores + owner) * capacity + at] = name
                far[(way * stores + owner) * capacity + at] = jnp.int32(dest)
                place[way * ADAPTERS + name] = jnp.where(new, at, held)
                step = new.astype(jnp.int32)
                for o in range(dest):
                    count[o] = count[o] + jnp.where(owner == o, step, 0)
            for o in range(dest):
                crossing[o][dest - 1] = count[o]
        for link in range(stores - 1):
            number = [crossing[o][link] for o in range(link + 1)]

            def fill(carry):
                t, left, *heads = carry
                best, chosen, row = jnp.int32(-1), zero, zero
                for o in range(link, -1, -1):
                    spot = (way * stores + o) * capacity + heads[o]
                    ready = heads[o] < number[o]
                    if o < link:
                        former = ((way * stores + link - 1) * stores + o) * capacity + heads[o]
                        ready = ready & (when[former] + LAG <= t)
                    goes = jnp.where(ready, far[spot], -1)
                    better = goes > best
                    best = jnp.where(better, goes, best)
                    chosen = jnp.where(better, o, chosen)
                    row = jnp.where(better, heads[o], row)
                found = best >= 0
                before = ((way * stores + max(link - 1, 0)) * stores + chosen) * capacity + row
                source = jnp.where(
                    chosen == link,
                    listed[(way * stores + chosen) * capacity + row] - my_store * per_store,
                    per_store + way * slots + when[before],
                )
                plan[jnp.where(found & (mine == link), 1 + way * slots + t, unused)] = source
                now = ((way * stores + link) * stores + chosen) * capacity + row
                when[jnp.where(found, now, when.shape[0] - 1)] = t
                step = found.astype(jnp.int32)
                heads = [heads[o] + jnp.where(chosen == o, step, 0) for o in range(link + 1)]
                return (t + 1, left - step, *heads)

            last, *_ = lax.while_loop(
                lambda carry: carry[1] > 0, fill, (zero, sum(number), *([zero] * (link + 1)))
            )
            most = jnp.maximum(most, last)
    plan[0] = most
    for b in range(blocks):
        name = names[my_store * blocks + b]
        owner = lax.div(name, jnp.int32(per_store))
        source = name - my_store * per_store
        for way in range(2):
            mine = my_store if way == 0 else stores - 1 - my_store
            origin = owner if way == 0 else stores - 1 - owner
            comes = origin < mine
            row = jnp.maximum(place[way * ADAPTERS + name], 0)
            spot = ((way * stores + jnp.maximum(mine - 1, 0)) * stores + origin) * capacity + row
            arrives = per_store + way * slots + when[jnp.where(comes, spot, 0)]
            source = jnp.where(comes, arrives, source)
        plan[1 + 2 * slots + b] = source


def make_plan(indices, stores, blocks, per_store, slots):
    lists = 2 * stores * (per_store + 1)
    return pl.pallas_call(
        functools.partial(plan_kernel, stores, blocks, per_store, slots),
        out_shape=jax.ShapeDtypeStruct((2 + 2 * slots + blocks,), jnp.int32),
        in_specs=[SMEM] * len(indices),
        out_specs=SMEM,
        scratch_shapes=[
            pltpu.SMEM((stores * blocks,), jnp.int32),
            pltpu.SMEM((2 * ADAPTERS,), jnp.int32),
            pltpu.SMEM((lists,), jnp.int32),
            pltpu.SMEM((lists,), jnp.int32),
            pltpu.SMEM((lists * stores + 1,), jnp.int32),
        ],
        name="plan",
    )(*indices)


def adapter_rows(down, up):
    return down.shape[1] * (down.shape[2] // up.shape[2] + 1)


def adapter_moves(down, up, item, sem, into_item):
    rank, width = down.shape
    columns = up.shape[1]
    moves = []
    for c in range(width // columns + 1):
        rows = item.at[pl.ds(c * rank, rank)]
        factor = up if c == width // columns else down.at[:, pl.ds(c * columns, columns)]
        source, target = (factor, rows) if into_item else (rows, factor)
        moves.append(pltpu.make_async_copy(source, target, sem))
    return moves


def pack_kernel(slots, per_store, way, batch, carried, plan, down, up, *refs):
    if carried and batch == 0:
        cache, numbers = refs[:2]
        refs = refs[2:]
    got = refs[:batch]
    out, sems = refs[batch:]
    size = adapter_rows(down, up)
    along = []
    if carried and batch == 0:
        part = carried - SEGMENT_ROWS
        member = lax.rem(lax.axis_index("tensor"), cache.shape[0] // part)
        along = [
            (cache.at[pl.ds(pl.multiple_of(member * part, part), part)], 0, part),
            (numbers, part, SEGMENT_ROWS),
        ]
    elif carried:
        along = [(got[batch - 1].at[pl.ds(BATCH * size, carried)], 0, carried)]
    along = [
        pltpu.make_async_copy(source, out.at[pl.ds(BATCH * size + at, rows)], sems.at[BATCH])
        for source, at, rows in along
    ]

    def copies(i):
        source = plan[1 + way * slots + batch * BATCH + i]
        own = jnp.minimum(source, per_store - 1)
        item = out.at[pl.ds(i * size, size)]
        pairs = [
            (
                source < per_store,
                adapter_moves(down.at[own], up.at[own], item, sems.at[i], True),
            )
        ]
        for j in range(batch * BATCH):
            held = got[j // BATCH].at[pl.ds(j % BATCH * size, size)]
            pairs.append(
                (
                    source == per_store + way * slots + j,
                    [pltpu.make_async_copy(held, item, sems.at[i])],
                )
            )
        return pairs

    for act in ("start", "wait"):
        for i in range(BATCH):
            for chosen, moves in copies(i):

                @pl.when(chosen)
                def _():
                    for move in moves:
                        getattr(move, act)()

        for move in along:
            getattr(move, act)()


def pack(plan, down, up, got, way, slots, carried=0, along=()):
    rows = BATCH * adapter_rows(down, up) + carried
    return pl.pallas_call(
        functools.partial(pack_kernel, slots, down.shape[0], way, len(got), carried),
        out_shape=jax.ShapeDtypeStruct((rows, up.shape[2]), down.dtype),
        in_specs=[SMEM] + [ANY] * (2 + len(along) + len(got)),
        out_specs=VMEM,
        scratch_shapes=[pltpu.SemaphoreType.DMA((BATCH + 1,))],
        compiler_params=pltpu.CompilerParams(vmem_limit_bytes=16 * MIB),
        cost_estimate=pl.CostEstimate(
            flops=5 * 10**8, bytes_accessed=4 * rows * up.shape[2], transcendentals=0
        ),
        name="pack",
    )(plan, down, up, *along, *got)


def low_rank_kernel(slots, per_store, former, received, tensor, plan, x, down, up, *refs):
    earlier = refs[: tensor + 1] if former is not None else ()
    refs = refs[len(earlier) :]
    number = 2 * received // BATCH
    got = refs[:number]
    outs = refs[number : number + tensor]
    selected, x_rows, factors, sems = refs[number + tensor :]
    blocks, rank, width = factors.shape
    share = blocks // tensor
    member = lax.axis_index("tensor")
    columns = pl.ds(pl.multiple_of(member * width, 128), width)
    if tensor == 1:
        member = 0

    size = adapter_rows(down, up)

    def within(source, number):
        return (source < per_store + number) | (
            (source >= per_store + slots) & (source < per_store + slots + number)
        )

    def due(b):
        source = plan[1 + 2 * slots + b]
        if former is None:
            return within(source, received)
        return jnp.logical_not(within(source, former))

    def copies(b):
        source = plan[1 + 2 * slots + b]
        source = jnp.where(within(source, received), source, 0)
        own = jnp.minimum(source, per_store - 1)
        pairs = [
            (
                source < per_store,
                [
                    pltpu.make_async_copy(down.at[own], factors.at[b], sems.at[b]),
                    pltpu.make_async_copy(up.at[own], selected.at[b], sems.at[b]),
                ],
            )
        ]
        for j in range(2 * received):
            spot = j if j < received else slots + j - received
            item = got[j // BATCH].at[pl.ds(j % BATCH * size, size)]
            pairs.append(
                (
                    source == per_store + spot,
                    adapter_moves(factors.at[b], selected.at[b], item, sems.at[b], False),
                )
            )
        return pairs

    def rows_of(b):
        rows = pl.ds(pl.multiple_of(b * BLOCK, BLOCK), BLOCK)
        return pltpu.make_async_copy(x.at[rows, columns], x_rows.at[b], sems.at[blocks + b])

    if former is not None:
        selected[...] = earlier[tensor][...]
    else:
        selected[...] = jnp.zeros_like(selected)

    def start(b, _):
        @pl.when(due(b))
        def _():
            rows_of(b).start()
            for chosen, moves in copies(b):

                @pl.when(chosen)
                def _():
                    for move in moves:
                        move.start()

        return 0

    lax.fori_loop(0, blocks, start, 0)
    for m in range(tensor):
        for i in range(share):
            b = (member ^ m) * share + i
            wanted = due(b)

            @pl.when(wanted)
            def _():
                pltpu.make_async_copy(down.at[0], factors.at[b], sems.at[b]).wait()
                pltpu.make_async_copy(up.at[0], selected.at[b], sems.at[b]).wait()
                rows_of(b).wait()
                outs[m][i] = lax.dot_general(
                    x_rows[b],
                    factors[b],
                    (((1,), (1,)), ((), ())),
                    preferred_element_type=jnp.float32,
                ).T

            @pl.when(jnp.logical_not(wanted))
            def _():
                if former is not None:
                    outs[m][i] = earlier[m][i]
                else:
                    outs[m][i] = jnp.zeros(outs[m].shape[1:], jnp.float32)


def low_rank_parts(plan, x, down, up, ups, downs, slots, tensor, blocks, former=None, earlier=()):
    per_store, rank, width = down.shape
    share = blocks // tensor
    return pl.pallas_call(
        functools.partial(
            low_rank_kernel, slots, per_store, former, BATCH * len(ups), tensor
        ),
        out_shape=[jax.ShapeDtypeStruct((share, rank, BLOCK), jnp.float32)] * tensor
        + [jax.ShapeDtypeStruct((blocks, rank, up.shape[2]), up.dtype)],
        in_specs=[SMEM] + [ANY] * 3 + [VMEM] * len(earlier) + [ANY] * (2 * len(ups)),
        out_specs=[VMEM] * (tensor + 1),
        scratch_shapes=[
            pltpu.VMEM((blocks, BLOCK, width), x.dtype),
            pltpu.VMEM((blocks, rank, width), down.dtype),
            pltpu.SemaphoreType.DMA((2 * blocks,)),
        ],
        compiler_params=pltpu.CompilerParams(vmem_limit_bytes=50 * MIB),
        cost_estimate=pl.CostEstimate(
            flops=6 * 10**9,
            bytes_accessed=2 * blocks * width * (BLOCK + rank),
            transcendentals=0,
        ),
        name="low_rank",
    )(plan, x, down, up, *earlier, *ups, *downs)


def window_kernel(hops, share, pad, *refs):
    pieces = refs[:share]
    own, segments, keys, values, starts, firsts, buffer, others, sems = refs[share:]
    rows = own.shape[0]
    part = rows // share
    blocks = rows // BLOCK
    member = lax.rem(lax.axis_index("tensor"), share)
    store = lax.axis_index("store")
    moves = [
        pltpu.make_async_copy(own, buffer.at[pl.ds(hops * rows, rows)], sems.at[hops * share])
    ]
    for hop in range(hops):
        for m in range(share):
            at = pl.multiple_of((hops - 1 - hop) * rows + (member ^ m) * part, part)
            moves.append(
                pltpu.make_async_copy(
                    pieces[m].at[hop, pl.ds(0, part)],
                    buffer.at[pl.ds(at, part)],
                    sems.at[hop * share + m],
                )
            )
        moves.append(
            pltpu.make_async_copy(
                pieces[0].at[hop, pl.ds(part, SEGMENT_ROWS)],
                others.at[hop],
                sems.at[hops * share + 1 + hop],
            )
        )
    for move in moves:
        move.start()
    empty = jnp.maximum(hops - store, 0) * rows
    names = segments[...]
    for move in moves:
        move.wait()
    start = jnp.zeros(names.shape, jnp.int32) + empty
    for value in range(1, SEGMENTS):
        before = empty.astype(jnp.float32)
        before = before + jnp.sum((names < value).astype(jnp.float32))
        for hop in range(hops):
            below = (others[hop].astype(jnp.float32) < value).astype(jnp.float32)
            before = before + jnp.where(hop < store, jnp.sum(below), 0.0)
        start = jnp.where(names == value, before.astype(jnp.int32), start)
    starts[...] = start.reshape(starts.shape)
    for j in range(blocks):
        firsts[j] = jnp.min(start[j : j + 1].astype(jnp.float32)).astype(jnp.int32)
    keys[pl.ds(0, pad), :] = jnp.zeros((pad, HEAD_SIZE), keys.dtype)
    values[:, pl.ds(0, pad)] = jnp.zeros((HEAD_SIZE, pad), values.dtype)

    def turn(c, _):
        at = pl.ds(pl.multiple_of(c * 256, 256), 256)
        to = pl.ds(pl.multiple_of(pad + c * 256, 256), 256)
        keys[to, :] = buffer[at, pl.ds(0, HEAD_SIZE)]
        values[:, to] = buffer[at, pl.ds(HEAD_SIZE, HEAD_SIZE)].astype(jnp.float32).T.astype(
            values.dtype
        )
        return 0

    lax.fori_loop(0, (hops + 1) * rows // 256, turn, 0)


def window(pieces, own, segments, hops, share, pad):
    rows = own.shape[0]
    length = pad + (hops + 1) * rows
    return pl.pallas_call(
        functools.partial(window_kernel, hops, share, pad),
        out_shape=[
            jax.ShapeDtypeStruct((length, HEAD_SIZE), own.dtype),
            jax.ShapeDtypeStruct((HEAD_SIZE, length), own.dtype),
            jax.ShapeDtypeStruct((rows // BLOCK, 1, BLOCK), jnp.int32),
            jax.ShapeDtypeStruct((rows // BLOCK,), jnp.int32),
        ],
        in_specs=[ANY] * (len(pieces) + 1) + [VMEM],
        out_specs=[VMEM, VMEM, VMEM, SMEM],
        scratch_shapes=[
            pltpu.VMEM(((hops + 1) * rows, 2 * HEAD_SIZE), own.dtype),
            pltpu.VMEM((hops, SEGMENT_ROWS, own.shape[1]), own.dtype),
            pltpu.SemaphoreType.DMA((hops * share + 1 + hops,)),
        ],
        compiler_params=pltpu.CompilerParams(vmem_limit_bytes=24 * MIB),
        cost_estimate=pl.CostEstimate(
            flops=0, bytes_accessed=8 * length * HEAD_SIZE, transcendentals=0
        ),
        name="window",
    )(*pieces, own, segments)


def base_kernel(x, weight, out, total):
    k = pl.program_id(0)
    product = jnp.dot(x[...], weight[...], preferred_element_type=jnp.float32)

    @pl.when(k == 0)
    def _():
        total[...] = product

    @pl.when(k > 0)
    def _():
        total[...] += product

    @pl.when(k == pl.num_programs(0) - 1)
    def _():
        out[...] = total[...].T


def base_queries(x, weight):
    rows, width = x.shape
    columns = weight.shape[1]
    deep = min(width, 1024)
    return pl.pallas_call(
        base_kernel,
        out_shape=jax.ShapeDtypeStruct((columns, rows), jnp.float32),
        grid=(width // deep,),
        in_specs=[
            pl.BlockSpec((rows, deep), lambda k: (0, k)),
            pl.BlockSpec((deep, columns), lambda k: (k, 0)),
        ],
        out_specs=pl.BlockSpec((columns, rows), lambda k: (0, 0)),
        scratch_shapes=[pltpu.VMEM((rows, columns), jnp.float32)],
        compiler_params=pltpu.CompilerParams(vmem_limit_bytes=24 * MIB),
        cost_estimate=pl.CostEstimate(
            flops=2 * rows * width * columns,
            bytes_accessed=2 * width * (rows + columns),
            transcendentals=0,
        ),
        name="base",
    )(x, weight)


def attention_kernel(
    hops, tensor, pad, heads, firsts, base, starts, keys, values, selected, *refs
):
    ranks = refs[:tensor]
    out, even, odd, even_largest, odd_largest, top, total, summed, queries = refs[tensor:]
    j = pl.program_id(0)
    share = ranks[0].shape[0]
    member = lax.axis_index("tensor") if tensor > 1 else 0
    rows = (keys.shape[0] - pad) // (hops + 1)
    for t in range(STRIDE // BLOCK):
        block = j * (STRIDE // BLOCK) + t
        low = jnp.zeros(ranks[0].shape[1:], jnp.bfloat16)
        for m in range(tensor):
            for i in range(share):
                low = jnp.where(block == (member ^ m) * share + i, ranks[m][i], low)
        term = lax.dot_general(
            selected[t], low, (((0,), (0,)), ((), ())), preferred_element_type=jnp.float32
        )
        turned = (base[:, t * BLOCK : (t + 1) * BLOCK] + term).astype(jnp.bfloat16)
        for h in range(heads):
            queries[:, h * STRIDE + t * BLOCK : h * STRIDE + (t + 1) * BLOCK] = turned[
                h * HEAD_SIZE : (h + 1) * HEAD_SIZE
            ]
    q = queries[...]
    columns = heads * STRIDE
    start = jnp.concatenate([starts[t] for t in range(STRIDE // BLOCK)] * heads, axis=1) + pad
    end = pad + hops * rows + (j + 1) * STRIDE
    steps = lax.div(
        end - pad - firsts[j * (STRIDE // BLOCK)] + CHUNK - 1, jnp.int32(CHUNK)
    )
    scale = HEAD_SIZE**-0.5 * math.log2(math.e)
    key = lax.broadcasted_iota(jnp.int32, (CHUNK, columns), 0)

    def place_of(c):
        return pl.multiple_of(jnp.maximum(end - (c + 1) * CHUNK, 0), BLOCK)

    def score(c, buffer, largest, diagonal):
        at = place_of(c)
        s = jnp.dot(keys[pl.ds(at, CHUNK), :], q, preferred_element_type=jnp.float32)
        allowed = key >= start - at
        if diagonal:
            token = lax.rem(lax.broadcasted_iota(jnp.int32, (1, columns), 1), STRIDE)
            allowed = allowed & (key <= token + (CHUNK - STRIDE))
        s = jnp.where(allowed, s, jnp.float32(-1e30))
        buffer[...] = s
        largest[...] = jnp.max(s.reshape(CHUNK // 8, 8, columns), axis=0)

    def weigh(c, buffer, largest):
        before = top[...]
        now = jnp.maximum(before, jnp.max(largest[...], axis=0, keepdims=True))
        top[...] = now
        fade = jnp.exp2((before - now) * scale)
        w = jnp.exp2((buffer[...] - now) * scale)
        total[...] = total[...] * fade + jnp.sum(w.reshape(CHUNK // 8, 8, columns), axis=0)
        summed[...] = summed[...] * fade + jnp.dot(
            values[:, pl.ds(place_of(c), CHUNK)],
            w.astype(jnp.bfloat16),
            preferred_element_type=jnp.float32,
        )

    top[...] = jnp.full(top.shape, -1e30, jnp.float32)
    total[...] = jnp.zeros(total.shape, jnp.float32)
    summed[...] = jnp.zeros(summed.shape, jnp.float32)
    score(0, even, even_largest, True)

    def two(i, _):
        score(2 * i + 1, odd, odd_largest, False)
        weigh(2 * i, even, even_largest)

        @pl.when(2 * i + 1 < steps)
        def _():
            score(2 * i + 2, even, even_largest, False)
            weigh(2 * i + 1, odd, odd_largest)

        return 0

    lax.fori_loop(0, lax.div(steps + 1, jnp.int32(2)), two, 0)
    attended = summed[...] / jnp.sum(total[...], axis=0, keepdims=True)
    for h in range(heads):
        out[:, h * HEAD_SIZE : (h + 1) * HEAD_SIZE] = (
            attended[:, h * STRIDE : (h + 1) * STRIDE].T.astype(out.dtype)
        )


def attention(firsts, base, starts, keys, values, selected, ranks, hops, pad, heads):
    columns, rows = base.shape
    group = STRIDE // BLOCK
    length = keys.shape[0]
    whole = lambda shape: pl.BlockSpec(shape, lambda j, *_: (0,) * len(shape))
    return pl.pallas_call(
        functools.partial(attention_kernel, hops, len(ranks), pad, heads),
        out_shape=jax.ShapeDtypeStruct((rows, columns), jnp.bfloat16),
        grid_spec=pltpu.PrefetchScalarGridSpec(
            num_scalar_prefetch=1,
            grid=(rows // STRIDE,),
            in_specs=[
                pl.BlockSpec((columns, STRIDE), lambda j, *_: (0, j)),
                pl.BlockSpec((group, 1, BLOCK), lambda j, *_: (j, 0, 0)),
                whole(keys.shape),
                whole(values.shape),
                pl.BlockSpec((group,) + selected.shape[1:], lambda j, *_: (j, 0, 0)),
            ]
            + [whole(r.shape) for r in ranks],
            out_specs=pl.BlockSpec((STRIDE, columns), lambda j, *_: (j, 0)),
            scratch_shapes=[
                pltpu.VMEM((CHUNK, heads * STRIDE), jnp.float32),
                pltpu.VMEM((CHUNK, heads * STRIDE), jnp.float32),
                pltpu.VMEM((8, heads * STRIDE), jnp.float32),
                pltpu.VMEM((8, heads * STRIDE), jnp.float32),
                pltpu.VMEM((1, heads * STRIDE), jnp.float32),
                pltpu.VMEM((8, heads * STRIDE), jnp.float32),
                pltpu.VMEM((HEAD_SIZE, heads * STRIDE), jnp.float32),
                pltpu.VMEM((HEAD_SIZE, heads * STRIDE), jnp.bfloat16),
            ],
        ),
        compiler_params=pltpu.CompilerParams(vmem_limit_bytes=40 * MIB),
        cost_estimate=pl.CostEstimate(
            flops=2 * rows * columns * length,
            bytes_accessed=8 * length * HEAD_SIZE,
            transcendentals=rows * heads * length,
        ),
        name="attention",
    )(firsts, base, starts, keys, values, selected, *ranks)


def per_device(
    mesh_shape,
    normed_input,
    query_weight,
    down_factors,
    up_factors,
    adapter_per_block,
    key_value_cache,
    token_segment,
):
    groups, tensor, stores = (mesh_shape[a] for a in ("groups", "tensor", "store"))
    rows = normed_input.shape[0]
    blocks = adapter_per_block.shape[0]
    heads = query_weight.shape[1] // HEAD_SIZE
    per_store = down_factors.shape[0]
    member = lax.axis_index("tensor")
    slots = slot_bound(stores, per_store, blocks)
    batches = slots // BATCH
    usual = min(batches, USUAL)
    more = min(batches, usual + MORE)
    hops = min(stores - 1, -(-(stores * rows // 2 - 1) // rows))
    share = min(tensor, max(1, GROUP // heads))
    exchange = tensor if blocks % tensor == 0 else 1
    raise_up = [(i, i + 1) for i in range(stores - 1)]
    raise_down = [(i + 1, i) for i in range(stores - 1)]
    pairs = lambda m: [(t, t ^ m) for t in range(tensor)]

    indices = [adapter_per_block] + [
        lax.ppermute(adapter_per_block, "store", [(i, (i + m) % stores) for i in range(stores)])
        for m in range(1, stores)
    ]
    down = jnp.swapaxes(down_factors, 1, 2)

    cache = jnp.swapaxes(key_value_cache, 0, 1)
    cache = lax.dynamic_index_in_dim(cache, member * heads // GROUP, 0, keepdims=False)
    numbers = token_segment.astype(cache.dtype).reshape(-1, cache.shape[1])
    numbers = jnp.pad(
        numbers, ((0, SEGMENT_ROWS - numbers.shape[0]), (0, 0)), constant_values=SEGMENTS
    )
    carried = rows // share + SEGMENT_ROWS
    plan = make_plan(indices, stores, blocks, per_store, slots)

    def fetch(first, last, ups, downs, plan, beside={}):
        ups, downs = list(ups), list(downs)
        for k in range(first, last):
            if k in beside:
                done = beside[k](ups)
                plan, done = lax.optimization_barrier((plan, done))
                found.append(done)
            along = (cache, numbers) if k == 0 else ()
            sent_up = pack(
                plan, down, up_factors, ups[:k], 0, slots, carried if k < hops else 0, along
            )
            sent_down = pack(plan, down, up_factors, downs[:k], 1, slots)
            ups.append(lax.ppermute(sent_up, "store", raise_up))
            downs.append(lax.ppermute(sent_down, "store", raise_down))
        return ups, downs, plan

    def exchanged(ups):
        quarters = jnp.stack([up[up.shape[0] - carried :] for up in ups[:hops]])
        return [quarters] + [lax.ppermute(quarters, "tensor", pairs(m)) for m in range(1, share)]

    found = []
    beside = {1: lambda ups: base_queries(normed_input, query_weight)}
    early = hops < usual - 1
    if early:
        beside[hops + 1] = exchanged
    ups, downs, plan = fetch(0, usual, [], [], plan, beside)
    base = found[0]
    pieces = found[1] if early else exchanged(ups)
    keys, values, starts, firsts = window(
        pieces, cache, token_segment.reshape(-1, BLOCK), hops, share, CHUNK
    )
    former = usual - 1
    earlier_parts = low_rank_parts(
        plan, normed_input, down, up_factors, ups[:former], downs[:former], slots, exchange, blocks
    )

    plan, *_ = lax.optimization_barrier((plan, keys, values, starts, firsts))

    def low_rank(ups, downs, plan):
        return tuple(
            low_rank_parts(
                plan,
                normed_input,
                down,
                up_factors,
                ups,
                downs,
                slots,
                exchange,
                blocks,
                former * BATCH,
                earlier_parts,
            )
        )

    def finish(parts, selected):
        if exchange > 1:
            total = parts[0]
            for m in range(1, tensor):
                total = total + lax.ppermute(parts[m], "tensor", pairs(m))
            total = total.astype(jnp.bfloat16)
            low = [total] + [lax.ppermute(total, "tensor", pairs(m)) for m in range(1, tensor)]
        else:
            low = [lax.psum(parts[0], "tensor").astype(jnp.bfloat16)]
        return attention(firsts, base, starts, keys, values, selected, low, hops, CHUNK, heads)

    def with_more(ups, downs, plan):
        return low_rank(*fetch(usual, more, ups, downs, plan))

    def with_all(ups, downs, plan, usually):
        *parts, selected = low_rank(*fetch(usual, batches, ups, downs, plan))
        return finish(parts, selected)

    *parts, selected = lax.cond(plan[0] > usual * BATCH, with_more, low_rank, ups, downs, plan)
    usually = finish(parts, selected)
    if more == batches:
        return usually
    return lax.cond(
        plan[0] > more * BATCH,
        with_all,
        lambda ups, downs, plan, usually: usually,
        ups,
        downs,
        plan,
        usually,
    )


def solution(mesh):
    return jax.shard_map(
        functools.partial(per_device, dict(mesh.shape)),
        mesh=mesh,
        in_specs=(
            P(("groups", "store"), None),
            P(None, "tensor"),
            P("store", "tensor", None),
            P("store", None, "tensor"),
            P(("groups", "store")),
            P(("groups", "store"), None, None),
            P(("groups", "store")),
        ),
        out_specs=P(("groups", "store"), "tensor"),
        check_vma=False,
    )
```

```python
import functools
import math

import jax
import jax.numpy as jnp
from jax import lax
from jax.experimental import pallas as pl
from jax.experimental.pallas import tpu as pltpu
from jax.sharding import PartitionSpec as P

HEAD_SIZE = 128
GROUP = 8
BLOCK = 128
ADAPTERS = 64
SEGMENTS = 4
SEGMENT_ROWS = 16
BATCH = 2
LAG = BATCH
USUAL = 4
MORE = 1
STRIDE = 2 * BLOCK
CHUNK = 512
MIB = 1 << 20
ANY = pl.BlockSpec(memory_space=pl.ANY)
SMEM = pl.BlockSpec(memory_space=pltpu.SMEM)
VMEM = pl.BlockSpec(memory_space=pltpu.VMEM)


def slot_bound(stores, per_store, blocks):
    load = max(
        min(per_store * (link + 1), blocks * (stores - 1 - link)) for link in range(stores - 1)
    )
    return -(-(load + (stores - 2) * LAG) // BATCH) * BATCH


def plan_kernel(stores, blocks, per_store, slots, *refs):
    index_refs = refs[:stores]
    plan, names, place, listed, far, when = refs[stores:]
    capacity = per_store + 1
    unused = 1 + 2 * slots + blocks
    my_store = lax.axis_index("store")
    zero = jnp.int32(0)
    for shift in range(stores):
        origin = lax.rem(my_store + stores - shift, stores)
        for b in range(blocks):
            names[origin * blocks + b] = index_refs[shift][b]
    for i in range(2 * ADAPTERS):
        place[i] = jnp.int32(-1)
    for i in range(2 * slots):
        plan[1 + i] = zero
    most = zero
    for way in range(2):
        mine = my_store if way == 0 else stores - 1 - my_store
        count = [zero] * stores
        crossing = [[zero] * stores for _ in range(stores)]
        for dest in range(stores - 1, 0, -1):
            real = dest if way == 0 else stores - 1 - dest
            for b in range(blocks):
                name = names[real * blocks + b]
                owner = lax.div(name, jnp.int32(per_store))
                if way == 1:
                    owner = stores - 1 - owner
                held = place[way * ADAPTERS + name]
                new = (owner < dest) & (held < 0)
                at = zero
                for o in range(stores):
                    at = jnp.where(owner == o, count[o], at)
                listed[(way * stores + owner) * capacity + at] = name
                far[(way * stores + owner) * capacity + at] = jnp.int32(dest)
                place[way * ADAPTERS + name] = jnp.where(new, at, held)
                step = new.astype(jnp.int32)
                for o in range(dest):
                    count[o] = count[o] + jnp.where(owner == o, step, 0)
            for o in range(dest):
                crossing[o][dest - 1] = count[o]
        for link in range(stores - 1):
            number = [crossing[o][link] for o in range(link + 1)]

            def fill(carry):
                t, left, *heads = carry
                best, chosen, row = jnp.int32(-1), zero, zero
                for o in range(link, -1, -1):
                    spot = (way * stores + o) * capacity + heads[o]
                    ready = heads[o] < number[o]
                    if o < link:
                        former = ((way * stores + link - 1) * stores + o) * capacity + heads[o]
                        ready = ready & (when[former] + LAG <= t)
                    goes = jnp.where(ready, far[spot], -1)
                    better = goes > best
                    best = jnp.where(better, goes, best)
                    chosen = jnp.where(better, o, chosen)
                    row = jnp.where(better, heads[o], row)
                found = best >= 0
                before = ((way * stores + max(link - 1, 0)) * stores + chosen) * capacity + row
                source = jnp.where(
                    chosen == link,
                    listed[(way * stores + chosen) * capacity + row] - my_store * per_store,
                    per_store + way * slots + when[before],
                )
                plan[jnp.where(found & (mine == link), 1 + way * slots + t, unused)] = source
                now = ((way * stores + link) * stores + chosen) * capacity + row
                when[jnp.where(found, now, when.shape[0] - 1)] = t
                step = found.astype(jnp.int32)
                heads = [heads[o] + jnp.where(chosen == o, step, 0) for o in range(link + 1)]
                return (t + 1, left - step, *heads)

            last, *_ = lax.while_loop(
                lambda carry: carry[1] > 0, fill, (zero, sum(number), *([zero] * (link + 1)))
            )
            most = jnp.maximum(most, last)
    plan[0] = most
    for b in range(blocks):
        name = names[my_store * blocks + b]
        owner = lax.div(name, jnp.int32(per_store))
        source = name - my_store * per_store
        for way in range(2):
            mine = my_store if way == 0 else stores - 1 - my_store
            origin = owner if way == 0 else stores - 1 - owner
            comes = origin < mine
            row = jnp.maximum(place[way * ADAPTERS + name], 0)
            spot = ((way * stores + jnp.maximum(mine - 1, 0)) * stores + origin) * capacity + row
            arrives = per_store + way * slots + when[jnp.where(comes, spot, 0)]
            source = jnp.where(comes, arrives, source)
        plan[1 + 2 * slots + b] = source


def make_plan(indices, stores, blocks, per_store, slots):
    lists = 2 * stores * (per_store + 1)
    return pl.pallas_call(
        functools.partial(plan_kernel, stores, blocks, per_store, slots),
        out_shape=jax.ShapeDtypeStruct((2 + 2 * slots + blocks,), jnp.int32),
        in_specs=[SMEM] * len(indices),
        out_specs=SMEM,
        scratch_shapes=[
            pltpu.SMEM((stores * blocks,), jnp.int32),
            pltpu.SMEM((2 * ADAPTERS,), jnp.int32),
            pltpu.SMEM((lists,), jnp.int32),
            pltpu.SMEM((lists,), jnp.int32),
            pltpu.SMEM((lists * stores + 1,), jnp.int32),
        ],
        name="plan",
    )(*indices)


def adapter_rows(down, up):
    return down.shape[1] * (down.shape[2] // up.shape[2] + 1)


def adapter_moves(down, up, item, sem, into_item):
    rank, width = down.shape
    columns = up.shape[1]
    moves = []
    for c in range(width // columns + 1):
        rows = item.at[pl.ds(c * rank, rank)]
        factor = up if c == width // columns else down.at[:, pl.ds(c * columns, columns)]
        source, target = (factor, rows) if into_item else (rows, factor)
        moves.append(pltpu.make_async_copy(source, target, sem))
    return moves


def pack_kernel(slots, per_store, way, batch, carried, plan, down, up, *refs):
    if carried and batch == 0:
        cache, numbers = refs[:2]
        refs = refs[2:]
    got = refs[:batch]
    out, sems = refs[batch:]
    size = adapter_rows(down, up)
    along = []
    if carried and batch == 0:
        part = carried - SEGMENT_ROWS
        member = lax.rem(lax.axis_index("tensor"), cache.shape[0] // part)
        along = [
            (cache.at[pl.ds(pl.multiple_of(member * part, part), part)], 0, part),
            (numbers, part, SEGMENT_ROWS),
        ]
    elif carried:
        along = [(got[batch - 1].at[pl.ds(BATCH * size, carried)], 0, carried)]
    along = [
        pltpu.make_async_copy(source, out.at[pl.ds(BATCH * size + at, rows)], sems.at[BATCH])
        for source, at, rows in along
    ]

    def copies(i):
        source = plan[1 + way * slots + batch * BATCH + i]
        own = jnp.minimum(source, per_store - 1)
        item = out.at[pl.ds(i * size, size)]
        pairs = [
            (
                source < per_store,
                adapter_moves(down.at[own], up.at[own], item, sems.at[i], True),
            )
        ]
        for j in range(batch * BATCH):
            held = got[j // BATCH].at[pl.ds(j % BATCH * size, size)]
            pairs.append(
                (
                    source == per_store + way * slots + j,
                    [pltpu.make_async_copy(held, item, sems.at[i])],
                )
            )
        return pairs

    for act in ("start", "wait"):
        for i in range(BATCH):
            for chosen, moves in copies(i):

                @pl.when(chosen)
                def _():
                    for move in moves:
                        getattr(move, act)()

        for move in along:
            getattr(move, act)()


def pack(plan, down, up, got, way, slots, carried=0, along=()):
    rows = BATCH * adapter_rows(down, up) + carried
    return pl.pallas_call(
        functools.partial(pack_kernel, slots, down.shape[0], way, len(got), carried),
        out_shape=jax.ShapeDtypeStruct((rows, up.shape[2]), down.dtype),
        in_specs=[SMEM] + [ANY] * (2 + len(along) + len(got)),
        out_specs=VMEM,
        scratch_shapes=[pltpu.SemaphoreType.DMA((BATCH + 1,))],
        compiler_params=pltpu.CompilerParams(vmem_limit_bytes=16 * MIB),
        cost_estimate=pl.CostEstimate(
            flops=5 * 10**8, bytes_accessed=4 * rows * up.shape[2], transcendentals=0
        ),
        name="pack",
    )(plan, down, up, *along, *got)


def low_rank_kernel(slots, per_store, former, received, tensor, plan, x, down, up, *refs):
    earlier = refs[: tensor + 1] if former is not None else ()
    refs = refs[len(earlier) :]
    number = 2 * received // BATCH
    got = refs[:number]
    outs = refs[number : number + tensor]
    selected, x_rows, factors, sems = refs[number + tensor :]
    blocks, rank, width = factors.shape
    share = blocks // tensor
    member = lax.axis_index("tensor")
    columns = pl.ds(pl.multiple_of(member * width, 128), width)
    if tensor == 1:
        member = 0

    size = adapter_rows(down, up)

    def within(source, number):
        return (source < per_store + number) | (
            (source >= per_store + slots) & (source < per_store + slots + number)
        )

    def due(b):
        source = plan[1 + 2 * slots + b]
        if former is None:
            return within(source, received)
        return jnp.logical_not(within(source, former))

    def copies(b):
        source = plan[1 + 2 * slots + b]
        source = jnp.where(within(source, received), source, 0)
        own = jnp.minimum(source, per_store - 1)
        pairs = [
            (
                source < per_store,
                [
                    pltpu.make_async_copy(down.at[own], factors.at[b], sems.at[b]),
                    pltpu.make_async_copy(up.at[own], selected.at[b], sems.at[b]),
                ],
            )
        ]
        for j in range(2 * received):
            spot = j if j < received else slots + j - received
            item = got[j // BATCH].at[pl.ds(j % BATCH * size, size)]
            pairs.append(
                (
                    source == per_store + spot,
                    adapter_moves(factors.at[b], selected.at[b], item, sems.at[b], False),
                )
            )
        return pairs

    def rows_of(b):
        rows = pl.ds(pl.multiple_of(b * BLOCK, BLOCK), BLOCK)
        return pltpu.make_async_copy(x.at[rows, columns], x_rows.at[b], sems.at[blocks + b])

    if former is not None:
        selected[...] = earlier[tensor][...]
    else:
        selected[...] = jnp.zeros_like(selected)

    def start(b, _):
        @pl.when(due(b))
        def _():
            rows_of(b).start()
            for chosen, moves in copies(b):

                @pl.when(chosen)
                def _():
                    for move in moves:
                        move.start()

        return 0

    lax.fori_loop(0, blocks, start, 0)
    for m in range(tensor):
        for i in range(share):
            b = (member ^ m) * share + i
            wanted = due(b)

            @pl.when(wanted)
            def _():
                pltpu.make_async_copy(down.at[0], factors.at[b], sems.at[b]).wait()
                pltpu.make_async_copy(up.at[0], selected.at[b], sems.at[b]).wait()
                rows_of(b).wait()
                outs[m][i] = lax.dot_general(
                    x_rows[b],
                    factors[b],
                    (((1,), (1,)), ((), ())),
                    preferred_element_type=jnp.float32,
                ).T

            @pl.when(jnp.logical_not(wanted))
            def _():
                if former is not None:
                    outs[m][i] = earlier[m][i]
                else:
                    outs[m][i] = jnp.zeros(outs[m].shape[1:], jnp.float32)


def low_rank_parts(plan, x, down, up, ups, downs, slots, tensor, blocks, former=None, earlier=()):
    per_store, rank, width = down.shape
    share = blocks // tensor
    return pl.pallas_call(
        functools.partial(
            low_rank_kernel, slots, per_store, former, BATCH * len(ups), tensor
        ),
        out_shape=[jax.ShapeDtypeStruct((share, rank, BLOCK), jnp.float32)] * tensor
        + [jax.ShapeDtypeStruct((blocks, rank, up.shape[2]), up.dtype)],
        in_specs=[SMEM] + [ANY] * 3 + [VMEM] * len(earlier) + [ANY] * (2 * len(ups)),
        out_specs=[VMEM] * (tensor + 1),
        scratch_shapes=[
            pltpu.VMEM((blocks, BLOCK, width), x.dtype),
            pltpu.VMEM((blocks, rank, width), down.dtype),
            pltpu.SemaphoreType.DMA((2 * blocks,)),
        ],
        compiler_params=pltpu.CompilerParams(vmem_limit_bytes=50 * MIB),
        cost_estimate=pl.CostEstimate(
            flops=6 * 10**9,
            bytes_accessed=2 * blocks * width * (BLOCK + rank),
            transcendentals=0,
        ),
        name="low_rank",
    )(plan, x, down, up, *earlier, *ups, *downs)


def window_kernel(hops, share, pad, *refs):
    pieces = refs[:share]
    own, segments, keys, values, starts, firsts, buffer, others, sems = refs[share:]
    rows = own.shape[0]
    part = rows // share
    blocks = rows // BLOCK
    member = lax.rem(lax.axis_index("tensor"), share)
    store = lax.axis_index("store")
    moves = [
        pltpu.make_async_copy(own, buffer.at[pl.ds(hops * rows, rows)], sems.at[hops * share])
    ]
    for hop in range(hops):
        for m in range(share):
            at = pl.multiple_of((hops - 1 - hop) * rows + (member ^ m) * part, part)
            moves.append(
                pltpu.make_async_copy(
                    pieces[m].at[hop, pl.ds(0, part)],
                    buffer.at[pl.ds(at, part)],
                    sems.at[hop * share + m],
                )
            )
        moves.append(
            pltpu.make_async_copy(
                pieces[0].at[hop, pl.ds(part, SEGMENT_ROWS)],
                others.at[hop],
                sems.at[hops * share + 1 + hop],
            )
        )
    for move in moves:
        move.start()
    empty = jnp.maximum(hops - store, 0) * rows
    names = segments[...]
    for move in moves:
        move.wait()
    start = jnp.zeros(names.shape, jnp.int32) + empty
    for value in range(1, SEGMENTS):
        before = empty.astype(jnp.float32)
        before = before + jnp.sum((names < value).astype(jnp.float32))
        for hop in range(hops):
            below = (others[hop].astype(jnp.float32) < value).astype(jnp.float32)
            before = before + jnp.where(hop < store, jnp.sum(below), 0.0)
        start = jnp.where(names == value, before.astype(jnp.int32), start)
    starts[...] = start.reshape(starts.shape)
    for j in range(blocks):
        firsts[j] = jnp.min(start[j : j + 1].astype(jnp.float32)).astype(jnp.int32)
    keys[pl.ds(0, pad), :] = jnp.zeros((pad, HEAD_SIZE), keys.dtype)
    values[:, pl.ds(0, pad)] = jnp.zeros((HEAD_SIZE, pad), values.dtype)

    def turn(c, _):
        at = pl.ds(pl.multiple_of(c * 256, 256), 256)
        to = pl.ds(pl.multiple_of(pad + c * 256, 256), 256)
        keys[to, :] = buffer[at, pl.ds(0, HEAD_SIZE)]
        values[:, to] = buffer[at, pl.ds(HEAD_SIZE, HEAD_SIZE)].astype(jnp.float32).T.astype(
            values.dtype
        )
        return 0

    lax.fori_loop(0, (hops + 1) * rows // 256, turn, 0)


def window(pieces, own, segments, hops, share, pad):
    rows = own.shape[0]
    length = pad + (hops + 1) * rows
    return pl.pallas_call(
        functools.partial(window_kernel, hops, share, pad),
        out_shape=[
            jax.ShapeDtypeStruct((length, HEAD_SIZE), own.dtype),
            jax.ShapeDtypeStruct((HEAD_SIZE, length), own.dtype),
            jax.ShapeDtypeStruct((rows // BLOCK, 1, BLOCK), jnp.int32),
            jax.ShapeDtypeStruct((rows // BLOCK,), jnp.int32),
        ],
        in_specs=[ANY] * (len(pieces) + 1) + [VMEM],
        out_specs=[VMEM, VMEM, VMEM, SMEM],
        scratch_shapes=[
            pltpu.VMEM(((hops + 1) * rows, 2 * HEAD_SIZE), own.dtype),
            pltpu.VMEM((hops, SEGMENT_ROWS, own.shape[1]), own.dtype),
            pltpu.SemaphoreType.DMA((hops * share + 1 + hops,)),
        ],
        compiler_params=pltpu.CompilerParams(vmem_limit_bytes=24 * MIB),
        cost_estimate=pl.CostEstimate(
            flops=0, bytes_accessed=8 * length * HEAD_SIZE, transcendentals=0
        ),
        name="window",
    )(*pieces, own, segments)


def base_kernel(x, weight, out, total):
    k = pl.program_id(0)
    product = jnp.dot(x[...], weight[...], preferred_element_type=jnp.float32)

    @pl.when(k == 0)
    def _():
        total[...] = product

    @pl.when(k > 0)
    def _():
        total[...] += product

    @pl.when(k == pl.num_programs(0) - 1)
    def _():
        out[...] = total[...].T


def base_queries(x, weight):
    rows, width = x.shape
    columns = weight.shape[1]
    deep = min(width, 1024)
    return pl.pallas_call(
        base_kernel,
        out_shape=jax.ShapeDtypeStruct((columns, rows), jnp.float32),
        grid=(width // deep,),
        in_specs=[
            pl.BlockSpec((rows, deep), lambda k: (0, k)),
            pl.BlockSpec((deep, columns), lambda k: (k, 0)),
        ],
        out_specs=pl.BlockSpec((columns, rows), lambda k: (0, 0)),
        scratch_shapes=[pltpu.VMEM((rows, columns), jnp.float32)],
        compiler_params=pltpu.CompilerParams(vmem_limit_bytes=24 * MIB),
        cost_estimate=pl.CostEstimate(
            flops=2 * rows * width * columns,
            bytes_accessed=2 * width * (rows + columns),
            transcendentals=0,
        ),
        name="base",
    )(x, weight)


def attention_kernel(
    hops, tensor, pad, heads, firsts, base, starts, keys, values, selected, *refs
):
    ranks = refs[:tensor]
    out, even, odd, even_largest, odd_largest, top, total, summed, queries = refs[tensor:]
    j = pl.program_id(0)
    share = ranks[0].shape[0]
    member = lax.axis_index("tensor") if tensor > 1 else 0
    rows = (keys.shape[0] - pad) // (hops + 1)
    for t in range(STRIDE // BLOCK):
        block = j * (STRIDE // BLOCK) + t
        low = jnp.zeros(ranks[0].shape[1:], jnp.bfloat16)
        for m in range(tensor):
            for i in range(share):
                low = jnp.where(block == (member ^ m) * share + i, ranks[m][i], low)
        term = lax.dot_general(
            selected[t], low, (((0,), (0,)), ((), ())), preferred_element_type=jnp.float32
        )
        turned = (base[:, t * BLOCK : (t + 1) * BLOCK] + term).astype(jnp.bfloat16)
        for h in range(heads):
            queries[:, h * STRIDE + t * BLOCK : h * STRIDE + (t + 1) * BLOCK] = turned[
                h * HEAD_SIZE : (h + 1) * HEAD_SIZE
            ]
    q = queries[...]
    columns = heads * STRIDE
    start = jnp.concatenate([starts[t] for t in range(STRIDE // BLOCK)] * heads, axis=1) + pad
    end = pad + hops * rows + (j + 1) * STRIDE
    steps = lax.div(
        end - pad - firsts[j * (STRIDE // BLOCK)] + CHUNK - 1, jnp.int32(CHUNK)
    )
    scale = HEAD_SIZE**-0.5 * math.log2(math.e)
    key = lax.broadcasted_iota(jnp.int32, (CHUNK, columns), 0)

    def place_of(c):
        return pl.multiple_of(jnp.maximum(end - (c + 1) * CHUNK, 0), BLOCK)

    def score(c, buffer, largest, diagonal):
        at = place_of(c)
        s = jnp.dot(keys[pl.ds(at, CHUNK), :], q, preferred_element_type=jnp.float32)
        allowed = key >= start - at
        if diagonal:
            token = lax.rem(lax.broadcasted_iota(jnp.int32, (1, columns), 1), STRIDE)
            allowed = allowed & (key <= token + (CHUNK - STRIDE))
        s = jnp.where(allowed, s, jnp.float32(-1e30))
        buffer[...] = s
        largest[...] = jnp.max(s.reshape(CHUNK // 8, 8, columns), axis=0)

    def weigh(c, buffer, largest):
        before = top[...]
        now = jnp.maximum(before, jnp.max(largest[...], axis=0, keepdims=True))
        top[...] = now
        fade = jnp.exp2((before - now) * scale)
        w = jnp.exp2((buffer[...] - now) * scale)
        total[...] = total[...] * fade + jnp.sum(w.reshape(CHUNK // 8, 8, columns), axis=0)
        summed[...] = summed[...] * fade + jnp.dot(
            values[:, pl.ds(place_of(c), CHUNK)],
            w.astype(jnp.bfloat16),
            preferred_element_type=jnp.float32,
        )

    top[...] = jnp.full(top.shape, -1e30, jnp.float32)
    total[...] = jnp.zeros(total.shape, jnp.float32)
    summed[...] = jnp.zeros(summed.shape, jnp.float32)
    score(0, even, even_largest, True)

    def two(i, _):
        score(2 * i + 1, odd, odd_largest, False)
        weigh(2 * i, even, even_largest)

        @pl.when(2 * i + 1 < steps)
        def _():
            score(2 * i + 2, even, even_largest, False)
            weigh(2 * i + 1, odd, odd_largest)

        return 0

    lax.fori_loop(0, lax.div(steps + 1, jnp.int32(2)), two, 0)
    attended = summed[...] / jnp.sum(total[...], axis=0, keepdims=True)
    for h in range(heads):
        out[:, h * HEAD_SIZE : (h + 1) * HEAD_SIZE] = (
            attended[:, h * STRIDE : (h + 1) * STRIDE].T.astype(out.dtype)
        )


def attention(firsts, base, starts, keys, values, selected, ranks, hops, pad, heads):
    columns, rows = base.shape
    group = STRIDE // BLOCK
    length = keys.shape[0]
    whole = lambda shape: pl.BlockSpec(shape, lambda j, *_: (0,) * len(shape))
    return pl.pallas_call(
        functools.partial(attention_kernel, hops, len(ranks), pad, heads),
        out_shape=jax.ShapeDtypeStruct((rows, columns), jnp.bfloat16),
        grid_spec=pltpu.PrefetchScalarGridSpec(
            num_scalar_prefetch=1,
            grid=(rows // STRIDE,),
            in_specs=[
                pl.BlockSpec((columns, STRIDE), lambda j, *_: (0, j)),
                pl.BlockSpec((group, 1, BLOCK), lambda j, *_: (j, 0, 0)),
                whole(keys.shape),
                whole(values.shape),
                pl.BlockSpec((group,) + selected.shape[1:], lambda j, *_: (j, 0, 0)),
            ]
            + [whole(r.shape) for r in ranks],
            out_specs=pl.BlockSpec((STRIDE, columns), lambda j, *_: (j, 0)),
            scratch_shapes=[
                pltpu.VMEM((CHUNK, heads * STRIDE), jnp.float32),
                pltpu.VMEM((CHUNK, heads * STRIDE), jnp.float32),
                pltpu.VMEM((8, heads * STRIDE), jnp.float32),
                pltpu.VMEM((8, heads * STRIDE), jnp.float32),
                pltpu.VMEM((1, heads * STRIDE), jnp.float32),
                pltpu.VMEM((8, heads * STRIDE), jnp.float32),
                pltpu.VMEM((HEAD_SIZE, heads * STRIDE), jnp.float32),
                pltpu.VMEM((HEAD_SIZE, heads * STRIDE), jnp.bfloat16),
            ],
        ),
        compiler_params=pltpu.CompilerParams(vmem_limit_bytes=40 * MIB),
        cost_estimate=pl.CostEstimate(
            flops=2 * rows * columns * length,
            bytes_accessed=8 * length * HEAD_SIZE,
            transcendentals=rows * heads * length,
        ),
        name="attention",
    )(firsts, base, starts, keys, values, selected, *ranks)


def per_device(
    mesh_shape,
    normed_input,
    query_weight,
    down_factors,
    up_factors,
    adapter_per_block,
    key_value_cache,
    token_segment,
):
    groups, tensor, stores = (mesh_shape[a] for a in ("groups", "tensor", "store"))
    rows = normed_input.shape[0]
    blocks = adapter_per_block.shape[0]
    heads = query_weight.shape[1] // HEAD_SIZE
    per_store = down_factors.shape[0]
    member = lax.axis_index("tensor")
    slots = slot_bound(stores, per_store, blocks)
    batches = slots // BATCH
    usual = min(batches, USUAL)
    more = min(batches, usual + MORE)
    hops = min(stores - 1, -(-(stores * rows // 2 - 1) // rows))
    share = min(tensor, max(1, GROUP // heads))
    exchange = tensor if blocks % tensor == 0 else 1
    raise_up = [(i, i + 1) for i in range(stores - 1)]
    raise_down = [(i + 1, i) for i in range(stores - 1)]
    pairs = lambda m: [(t, t ^ m) for t in range(tensor)]

    indices = [adapter_per_block] + [
        lax.ppermute(adapter_per_block, "store", [(i, (i + m) % stores) for i in range(stores)])
        for m in range(1, stores)
    ]
    down = jnp.swapaxes(down_factors, 1, 2)

    cache = jnp.swapaxes(key_value_cache, 0, 1)
    cache = lax.dynamic_index_in_dim(cache, member * heads // GROUP, 0, keepdims=False)
    numbers = token_segment.astype(cache.dtype).reshape(-1, cache.shape[1])
    numbers = jnp.pad(
        numbers, ((0, SEGMENT_ROWS - numbers.shape[0]), (0, 0)), constant_values=SEGMENTS
    )
    carried = rows // share + SEGMENT_ROWS
    plan = make_plan(indices, stores, blocks, per_store, slots)

    def fetch(first, last, ups, downs, plan, beside={}):
        ups, downs = list(ups), list(downs)
        for k in range(first, last):
            if k in beside:
                done = beside[k](ups)
                plan, done = lax.optimization_barrier((plan, done))
                found.append(done)
            along = (cache, numbers) if k == 0 else ()
            sent_up = pack(
                plan, down, up_factors, ups[:k], 0, slots, carried if k < hops else 0, along
            )
            plan, sent_up = lax.optimization_barrier((plan, sent_up))
            sent_down = pack(plan, down, up_factors, downs[:k], 1, slots)
            ups.append(lax.ppermute(sent_up, "store", raise_up))
            downs.append(lax.ppermute(sent_down, "store", raise_down))
        return ups, downs, plan

    def exchanged(ups):
        quarters = jnp.stack([up[up.shape[0] - carried :] for up in ups[:hops]])
        shares = [quarters]
        for m in range(1, share):
            bit = m & -m
            shares.append(lax.ppermute(shares[m ^ bit], "tensor", pairs(bit)))
        return shares

    found = []
    beside = {1: lambda ups: base_queries(normed_input, query_weight)}
    early = hops < usual - 1
    if early:
        beside[hops + 1] = exchanged
    ups, downs, plan = fetch(0, usual, [], [], plan, beside)
    base = found[0]
    pieces = found[1] if early else exchanged(ups)
    keys, values, starts, firsts = window(
        pieces, cache, token_segment.reshape(-1, BLOCK), hops, share, CHUNK
    )
    former = usual - 1
    earlier_parts = low_rank_parts(
        plan, normed_input, down, up_factors, ups[:former], downs[:former], slots, exchange, blocks
    )

    plan, *_ = lax.optimization_barrier((plan, keys, values, starts, firsts))

    def low_rank(ups, downs, plan):
        return tuple(
            low_rank_parts(
                plan,
                normed_input,
                down,
                up_factors,
                ups,
                downs,
                slots,
                exchange,
                blocks,
                former * BATCH,
                earlier_parts,
            )
        )

    def finish(parts, selected):
        if exchange > 1:
            total = parts[0]
            for m in range(1, tensor):
                total = total + lax.ppermute(parts[m], "tensor", pairs(m))
            total = total.astype(jnp.bfloat16)
            low = [total] + [lax.ppermute(total, "tensor", pairs(m)) for m in range(1, tensor)]
        else:
            low = [lax.psum(parts[0], "tensor").astype(jnp.bfloat16)]
        return attention(firsts, base, starts, keys, values, selected, low, hops, CHUNK, heads)

    def with_more(ups, downs, plan):
        return low_rank(*fetch(usual, more, ups, downs, plan))

    def with_all(ups, downs, plan, usually):
        *parts, selected = low_rank(*fetch(usual, batches, ups, downs, plan))
        return finish(parts, selected)

    *parts, selected = lax.cond(plan[0] > usual * BATCH, with_more, low_rank, ups, downs, plan)
    usually = finish(parts, selected)
    if more == batches:
        return usually
    return lax.cond(
        plan[0] > more * BATCH,
        with_all,
        lambda ups, downs, plan, usually: usually,
        ups,
        downs,
        plan,
        usually,
    )


def solution(mesh):
    return jax.shard_map(
        functools.partial(per_device, dict(mesh.shape)),
        mesh=mesh,
        in_specs=(
            P(("groups", "store"), None),
            P(None, "tensor"),
            P("store", "tensor", None),
            P("store", None, "tensor"),
            P(("groups", "store")),
            P(("groups", "store"), None, None),
            P(("groups", "store")),
        ),
        out_specs=P(("groups", "store"), "tensor"),
        check_vma=False,
    )
```

```python
import functools
import math

import jax
import jax.numpy as jnp
from jax import lax
from jax.experimental import pallas as pl
from jax.experimental.pallas import tpu as pltpu
from jax.sharding import PartitionSpec as P

HEAD_SIZE = 128
GROUP = 8
BLOCK = 128
ADAPTERS = 64
SEGMENTS = 4
SEGMENT_ROWS = 16
BATCH = 2
LAG = BATCH
USUAL = 4
MORE = 1
STRIDE = 2 * BLOCK
CHUNK = 512
MIB = 1 << 20
ANY = pl.BlockSpec(memory_space=pl.ANY)
SMEM = pl.BlockSpec(memory_space=pltpu.SMEM)
VMEM = pl.BlockSpec(memory_space=pltpu.VMEM)


def slot_bound(stores, per_store, blocks):
    load = max(
        min(per_store * (link + 1), blocks * (stores - 1 - link)) for link in range(stores - 1)
    )
    return -(-(load + (stores - 2) * LAG) // BATCH) * BATCH


def plan_kernel(stores, blocks, per_store, slots, *refs):
    index_refs = refs[:stores]
    plan, names, place, listed, far, when = refs[stores:]
    capacity = per_store + 1
    unused = 1 + 2 * slots + blocks
    my_store = lax.axis_index("store")
    zero = jnp.int32(0)
    for shift in range(stores):
        origin = lax.rem(my_store + stores - shift, stores)
        for b in range(blocks):
            names[origin * blocks + b] = index_refs[shift][b]
    for i in range(2 * ADAPTERS):
        place[i] = jnp.int32(-1)
    for i in range(2 * slots):
        plan[1 + i] = zero
    most = zero
    for way in range(2):
        mine = my_store if way == 0 else stores - 1 - my_store
        count = [zero] * stores
        crossing = [[zero] * stores for _ in range(stores)]
        for dest in range(stores - 1, 0, -1):
            real = dest if way == 0 else stores - 1 - dest
            for b in range(blocks):
                name = names[real * blocks + b]
                owner = lax.div(name, jnp.int32(per_store))
                if way == 1:
                    owner = stores - 1 - owner
                held = place[way * ADAPTERS + name]
                new = (owner < dest) & (held < 0)
                at = zero
                for o in range(stores):
                    at = jnp.where(owner == o, count[o], at)
                listed[(way * stores + owner) * capacity + at] = name
                far[(way * stores + owner) * capacity + at] = jnp.int32(dest)
                place[way * ADAPTERS + name] = jnp.where(new, at, held)
                step = new.astype(jnp.int32)
                for o in range(dest):
                    count[o] = count[o] + jnp.where(owner == o, step, 0)
            for o in range(dest):
                crossing[o][dest - 1] = count[o]
        for link in range(stores - 1):
            number = [crossing[o][link] for o in range(link + 1)]

            def fill(carry):
                t, left, *heads = carry
                best, chosen, row = jnp.int32(-1), zero, zero
                for o in range(link, -1, -1):
                    spot = (way * stores + o) * capacity + heads[o]
                    ready = heads[o] < number[o]
                    if o < link:
                        former = ((way * stores + link - 1) * stores + o) * capacity + heads[o]
                        ready = ready & (when[former] + LAG <= t)
                    goes = jnp.where(ready, far[spot], -1)
                    better = goes > best
                    best = jnp.where(better, goes, best)
                    chosen = jnp.where(better, o, chosen)
                    row = jnp.where(better, heads[o], row)
                found = best >= 0
                before = ((way * stores + max(link - 1, 0)) * stores + chosen) * capacity + row
                source = jnp.where(
                    chosen == link,
                    listed[(way * stores + chosen) * capacity + row] - my_store * per_store,
                    per_store + way * slots + when[before],
                )
                plan[jnp.where(found & (mine == link), 1 + way * slots + t, unused)] = source
                now = ((way * stores + link) * stores + chosen) * capacity + row
                when[jnp.where(found, now, when.shape[0] - 1)] = t
                step = found.astype(jnp.int32)
                heads = [heads[o] + jnp.where(chosen == o, step, 0) for o in range(link + 1)]
                return (t + 1, left - step, *heads)

            last, *_ = lax.while_loop(
                lambda carry: carry[1] > 0, fill, (zero, sum(number), *([zero] * (link + 1)))
            )
            most = jnp.maximum(most, last)
    plan[0] = most
    for b in range(blocks):
        name = names[my_store * blocks + b]
        owner = lax.div(name, jnp.int32(per_store))
        source = name - my_store * per_store
        for way in range(2):
            mine = my_store if way == 0 else stores - 1 - my_store
            origin = owner if way == 0 else stores - 1 - owner
            comes = origin < mine
            row = jnp.maximum(place[way * ADAPTERS + name], 0)
            spot = ((way * stores + jnp.maximum(mine - 1, 0)) * stores + origin) * capacity + row
            arrives = per_store + way * slots + when[jnp.where(comes, spot, 0)]
            source = jnp.where(comes, arrives, source)
        plan[1 + 2 * slots + b] = source


def make_plan(indices, stores, blocks, per_store, slots):
    lists = 2 * stores * (per_store + 1)
    return pl.pallas_call(
        functools.partial(plan_kernel, stores, blocks, per_store, slots),
        out_shape=jax.ShapeDtypeStruct((2 + 2 * slots + blocks,), jnp.int32),
        in_specs=[SMEM] * len(indices),
        out_specs=SMEM,
        scratch_shapes=[
            pltpu.SMEM((stores * blocks,), jnp.int32),
            pltpu.SMEM((2 * ADAPTERS,), jnp.int32),
            pltpu.SMEM((lists,), jnp.int32),
            pltpu.SMEM((lists,), jnp.int32),
            pltpu.SMEM((lists * stores + 1,), jnp.int32),
        ],
        name="plan",
    )(*indices)


def adapter_rows(down, up):
    return down.shape[1] * (down.shape[2] // up.shape[2] + 1)


def adapter_moves(down, up, item, sem, into_item):
    rank, width = down.shape
    columns = up.shape[1]
    moves = []
    for c in range(width // columns + 1):
        rows = item.at[pl.ds(c * rank, rank)]
        factor = up if c == width // columns else down.at[:, pl.ds(c * columns, columns)]
        source, target = (factor, rows) if into_item else (rows, factor)
        moves.append(pltpu.make_async_copy(source, target, sem))
    return moves


def pack_kernel(slots, per_store, way, batch, carried, plan, down, up, *refs):
    if carried and batch == 0:
        cache, numbers = refs[:2]
        refs = refs[2:]
    got = refs[:batch]
    out, sems = refs[batch:]
    size = adapter_rows(down, up)
    along = []
    if carried and batch == 0:
        part = carried - SEGMENT_ROWS
        member = lax.rem(lax.axis_index("tensor"), cache.shape[0] // part)
        along = [
            (cache.at[pl.ds(pl.multiple_of(member * part, part), part)], 0, part),
            (numbers, part, SEGMENT_ROWS),
        ]
    elif carried:
        along = [(got[batch - 1].at[pl.ds(BATCH * size, carried)], 0, carried)]
    along = [
        pltpu.make_async_copy(source, out.at[pl.ds(BATCH * size + at, rows)], sems.at[BATCH])
        for source, at, rows in along
    ]

    def copies(i):
        source = plan[1 + way * slots + batch * BATCH + i]
        own = jnp.minimum(source, per_store - 1)
        item = out.at[pl.ds(i * size, size)]
        pairs = [
            (
                source < per_store,
                adapter_moves(down.at[own], up.at[own], item, sems.at[i], True),
            )
        ]
        for j in range(batch * BATCH):
            held = got[j // BATCH].at[pl.ds(j % BATCH * size, size)]
            pairs.append(
                (
                    source == per_store + way * slots + j,
                    [pltpu.make_async_copy(held, item, sems.at[i])],
                )
            )
        return pairs

    for act in ("start", "wait"):
        for i in range(BATCH):
            for chosen, moves in copies(i):

                @pl.when(chosen)
                def _():
                    for move in moves:
                        getattr(move, act)()

        for move in along:
            getattr(move, act)()


def pack(plan, down, up, got, way, slots, carried=0, along=()):
    rows = BATCH * adapter_rows(down, up) + carried
    return pl.pallas_call(
        functools.partial(pack_kernel, slots, down.shape[0], way, len(got), carried),
        out_shape=jax.ShapeDtypeStruct((rows, up.shape[2]), down.dtype),
        in_specs=[SMEM] + [ANY] * (2 + len(along) + len(got)),
        out_specs=VMEM,
        scratch_shapes=[pltpu.SemaphoreType.DMA((BATCH + 1,))],
        compiler_params=pltpu.CompilerParams(vmem_limit_bytes=16 * MIB),
        cost_estimate=pl.CostEstimate(
            flops=5 * 10**8, bytes_accessed=4 * rows * up.shape[2], transcendentals=0
        ),
        name="pack",
    )(plan, down, up, *along, *got)


def low_rank_kernel(slots, per_store, former, received, tensor, plan, x, down, up, *refs):
    earlier = refs[: tensor + 1] if former is not None else ()
    refs = refs[len(earlier) :]
    number = 2 * received // BATCH
    got = refs[:number]
    outs = refs[number : number + tensor]
    selected, x_rows, factors, sems = refs[number + tensor :]
    blocks, rank, width = factors.shape
    share = blocks // tensor
    member = lax.axis_index("tensor")
    columns = pl.ds(pl.multiple_of(member * width, 128), width)
    if tensor == 1:
        member = 0

    size = adapter_rows(down, up)

    def within(source, number):
        return (source < per_store + number) | (
            (source >= per_store + slots) & (source < per_store + slots + number)
        )

    def due(b):
        source = plan[1 + 2 * slots + b]
        if former is None:
            return within(source, received)
        return jnp.logical_not(within(source, former))

    def copies(b):
        source = plan[1 + 2 * slots + b]
        source = jnp.where(within(source, received), source, 0)
        own = jnp.minimum(source, per_store - 1)
        pairs = [
            (
                source < per_store,
                [
                    pltpu.make_async_copy(down.at[own], factors.at[b], sems.at[b]),
                    pltpu.make_async_copy(up.at[own], selected.at[b], sems.at[b]),
                ],
            )
        ]
        for j in range(2 * received):
            spot = j if j < received else slots + j - received
            item = got[j // BATCH].at[pl.ds(j % BATCH * size, size)]
            pairs.append(
                (
                    source == per_store + spot,
                    adapter_moves(factors.at[b], selected.at[b], item, sems.at[b], False),
                )
            )
        return pairs

    def rows_of(b):
        rows = pl.ds(pl.multiple_of(b * BLOCK, BLOCK), BLOCK)
        return pltpu.make_async_copy(x.at[rows, columns], x_rows.at[b], sems.at[blocks + b])

    if former is not None:
        selected[...] = earlier[tensor][...]
    else:
        selected[...] = jnp.zeros_like(selected)

    def start(b, _):
        @pl.when(due(b))
        def _():
            rows_of(b).start()
            for chosen, moves in copies(b):

                @pl.when(chosen)
                def _():
                    for move in moves:
                        move.start()

        return 0

    lax.fori_loop(0, blocks, start, 0)
    for m in range(tensor):
        for i in range(share):
            b = (member ^ m) * share + i
            wanted = due(b)

            @pl.when(wanted)
            def _():
                pltpu.make_async_copy(down.at[0], factors.at[b], sems.at[b]).wait()
                pltpu.make_async_copy(up.at[0], selected.at[b], sems.at[b]).wait()
                rows_of(b).wait()
                outs[m][i] = lax.dot_general(
                    x_rows[b],
                    factors[b],
                    (((1,), (1,)), ((), ())),
                    preferred_element_type=jnp.float32,
                ).T

            @pl.when(jnp.logical_not(wanted))
            def _():
                if former is not None:
                    outs[m][i] = earlier[m][i]
                else:
                    outs[m][i] = jnp.zeros(outs[m].shape[1:], jnp.float32)


def low_rank_parts(plan, x, down, up, ups, downs, slots, tensor, blocks, former=None, earlier=()):
    per_store, rank, width = down.shape
    share = blocks // tensor
    return pl.pallas_call(
        functools.partial(
            low_rank_kernel, slots, per_store, former, BATCH * len(ups), tensor
        ),
        out_shape=[jax.ShapeDtypeStruct((share, rank, BLOCK), jnp.float32)] * tensor
        + [jax.ShapeDtypeStruct((blocks, rank, up.shape[2]), up.dtype)],
        in_specs=[SMEM] + [ANY] * 3 + [VMEM] * len(earlier) + [ANY] * (2 * len(ups)),
        out_specs=[VMEM] * (tensor + 1),
        scratch_shapes=[
            pltpu.VMEM((blocks, BLOCK, width), x.dtype),
            pltpu.VMEM((blocks, rank, width), down.dtype),
            pltpu.SemaphoreType.DMA((2 * blocks,)),
        ],
        compiler_params=pltpu.CompilerParams(vmem_limit_bytes=50 * MIB),
        cost_estimate=pl.CostEstimate(
            flops=6 * 10**9,
            bytes_accessed=2 * blocks * width * (BLOCK + rank),
            transcendentals=0,
        ),
        name="low_rank",
    )(plan, x, down, up, *earlier, *ups, *downs)


def window_kernel(hops, share, pad, *refs):
    pieces = refs[:share]
    own, segments, keys, values, starts, firsts, buffer, others, sems = refs[share:]
    rows = own.shape[0]
    part = rows // share
    blocks = rows // BLOCK
    member = lax.rem(lax.axis_index("tensor"), share)
    store = lax.axis_index("store")
    moves = [
        pltpu.make_async_copy(own, buffer.at[pl.ds(hops * rows, rows)], sems.at[hops * share])
    ]
    for hop in range(hops):
        for m in range(share):
            at = pl.multiple_of((hops - 1 - hop) * rows + (member ^ m) * part, part)
            moves.append(
                pltpu.make_async_copy(
                    pieces[m].at[hop, pl.ds(0, part)],
                    buffer.at[pl.ds(at, part)],
                    sems.at[hop * share + m],
                )
            )
        moves.append(
            pltpu.make_async_copy(
                pieces[0].at[hop, pl.ds(part, SEGMENT_ROWS)],
                others.at[hop],
                sems.at[hops * share + 1 + hop],
            )
        )
    for move in moves:
        move.start()
    empty = jnp.maximum(hops - store, 0) * rows
    names = segments[...]
    for move in moves:
        move.wait()
    start = jnp.zeros(names.shape, jnp.int32) + empty
    for value in range(1, SEGMENTS):
        before = empty.astype(jnp.float32)
        before = before + jnp.sum((names < value).astype(jnp.float32))
        for hop in range(hops):
            below = (others[hop].astype(jnp.float32) < value).astype(jnp.float32)
            before = before + jnp.where(hop < store, jnp.sum(below), 0.0)
        start = jnp.where(names == value, before.astype(jnp.int32), start)
    starts[...] = start.reshape(starts.shape)
    for j in range(blocks):
        firsts[j] = jnp.min(start[j : j + 1].astype(jnp.float32)).astype(jnp.int32)
    keys[pl.ds(0, pad), :] = jnp.zeros((pad, HEAD_SIZE), keys.dtype)
    values[:, pl.ds(0, pad)] = jnp.zeros((HEAD_SIZE, pad), values.dtype)

    def turn(c, _):
        at = pl.ds(pl.multiple_of(c * 256, 256), 256)
        to = pl.ds(pl.multiple_of(pad + c * 256, 256), 256)
        keys[to, :] = buffer[at, pl.ds(0, HEAD_SIZE)]
        values[:, to] = buffer[at, pl.ds(HEAD_SIZE, HEAD_SIZE)].astype(jnp.float32).T.astype(
            values.dtype
        )
        return 0

    lax.fori_loop(0, (hops + 1) * rows // 256, turn, 0)


def window(pieces, own, segments, hops, share, pad):
    rows = own.shape[0]
    length = pad + (hops + 1) * rows
    return pl.pallas_call(
        functools.partial(window_kernel, hops, share, pad),
        out_shape=[
            jax.ShapeDtypeStruct((length, HEAD_SIZE), own.dtype),
            jax.ShapeDtypeStruct((HEAD_SIZE, length), own.dtype),
            jax.ShapeDtypeStruct((rows // BLOCK, 1, BLOCK), jnp.int32),
            jax.ShapeDtypeStruct((rows // BLOCK,), jnp.int32),
        ],
        in_specs=[ANY] * (len(pieces) + 1) + [VMEM],
        out_specs=[VMEM, VMEM, VMEM, SMEM],
        scratch_shapes=[
            pltpu.VMEM(((hops + 1) * rows, 2 * HEAD_SIZE), own.dtype),
            pltpu.VMEM((hops, SEGMENT_ROWS, own.shape[1]), own.dtype),
            pltpu.SemaphoreType.DMA((hops * share + 1 + hops,)),
        ],
        compiler_params=pltpu.CompilerParams(vmem_limit_bytes=24 * MIB),
        cost_estimate=pl.CostEstimate(
            flops=0, bytes_accessed=8 * length * HEAD_SIZE, transcendentals=0
        ),
        name="window",
    )(*pieces, own, segments)


def base_kernel(x, weight, out, total):
    k = pl.program_id(0)
    product = jnp.dot(x[...], weight[...], preferred_element_type=jnp.float32)

    @pl.when(k == 0)
    def _():
        total[...] = product

    @pl.when(k > 0)
    def _():
        total[...] += product

    @pl.when(k == pl.num_programs(0) - 1)
    def _():
        out[...] = total[...].T


def base_queries(x, weight):
    rows, width = x.shape
    columns = weight.shape[1]
    deep = min(width, 1024)
    return pl.pallas_call(
        base_kernel,
        out_shape=jax.ShapeDtypeStruct((columns, rows), jnp.float32),
        grid=(width // deep,),
        in_specs=[
            pl.BlockSpec((rows, deep), lambda k: (0, k)),
            pl.BlockSpec((deep, columns), lambda k: (k, 0)),
        ],
        out_specs=pl.BlockSpec((columns, rows), lambda k: (0, 0)),
        scratch_shapes=[pltpu.VMEM((rows, columns), jnp.float32)],
        compiler_params=pltpu.CompilerParams(vmem_limit_bytes=24 * MIB),
        cost_estimate=pl.CostEstimate(
            flops=2 * rows * width * columns,
            bytes_accessed=2 * width * (rows + columns),
            transcendentals=0,
        ),
        name="base",
    )(x, weight)


def attention_kernel(
    hops, tensor, pad, heads, firsts, base, starts, keys, values, selected, *refs
):
    ranks = refs[:tensor]
    out, even, odd, even_largest, odd_largest, top, total, summed, queries = refs[tensor:]
    j = pl.program_id(0)
    share = ranks[0].shape[0]
    member = lax.axis_index("tensor") if tensor > 1 else 0
    rows = (keys.shape[0] - pad) // (hops + 1)
    for t in range(STRIDE // BLOCK):
        block = j * (STRIDE // BLOCK) + t
        low = jnp.zeros(ranks[0].shape[1:], jnp.bfloat16)
        for m in range(tensor):
            for i in range(share):
                low = jnp.where(block == (member ^ m) * share + i, ranks[m][i], low)
        term = lax.dot_general(
            selected[t], low, (((0,), (0,)), ((), ())), preferred_element_type=jnp.float32
        )
        turned = (base[:, t * BLOCK : (t + 1) * BLOCK] + term).astype(jnp.bfloat16)
        for h in range(heads):
            queries[:, h * STRIDE + t * BLOCK : h * STRIDE + (t + 1) * BLOCK] = turned[
                h * HEAD_SIZE : (h + 1) * HEAD_SIZE
            ]
    q = queries[...]
    columns = heads * STRIDE
    start = jnp.concatenate([starts[t] for t in range(STRIDE // BLOCK)] * heads, axis=1) + pad
    end = pad + hops * rows + (j + 1) * STRIDE
    steps = lax.div(
        end - pad - firsts[j * (STRIDE // BLOCK)] + CHUNK - 1, jnp.int32(CHUNK)
    )
    scale = HEAD_SIZE**-0.5 * math.log2(math.e)
    key = lax.broadcasted_iota(jnp.int32, (CHUNK, columns), 0)

    def place_of(c):
        return pl.multiple_of(jnp.maximum(end - (c + 1) * CHUNK, 0), BLOCK)

    def score(c, buffer, largest, diagonal):
        at = place_of(c)
        s = jnp.dot(keys[pl.ds(at, CHUNK), :], q, preferred_element_type=jnp.float32)
        allowed = key >= start - at
        if diagonal:
            token = lax.rem(lax.broadcasted_iota(jnp.int32, (1, columns), 1), STRIDE)
            allowed = allowed & (key <= token + (CHUNK - STRIDE))
        s = jnp.where(allowed, s, jnp.float32(-1e30))
        buffer[...] = s
        largest[...] = jnp.max(s.reshape(CHUNK // 8, 8, columns), axis=0)

    def weigh(c, buffer, largest):
        before = top[...]
        now = jnp.maximum(before, jnp.max(largest[...], axis=0, keepdims=True))
        top[...] = now
        fade = jnp.exp2((before - now) * scale)
        w = jnp.exp2((buffer[...] - now) * scale)
        total[...] = total[...] * fade + jnp.sum(w.reshape(CHUNK // 8, 8, columns), axis=0)
        summed[...] = summed[...] * fade + jnp.dot(
            values[:, pl.ds(place_of(c), CHUNK)],
            w.astype(jnp.bfloat16),
            preferred_element_type=jnp.float32,
        )

    top[...] = jnp.full(top.shape, -1e30, jnp.float32)
    total[...] = jnp.zeros(total.shape, jnp.float32)
    summed[...] = jnp.zeros(summed.shape, jnp.float32)
    even, odd = (even, even_largest), (odd, odd_largest)
    score(0, *even, True)

    def two(i, _):
        for c, now, after in ((2 * i, even, odd), (2 * i + 1, odd, even)):

            @pl.when(c + 1 < steps)
            def _():
                score(c + 1, *after, False)
                weigh(c, *now)

            @pl.when(c + 1 == steps)
            def _():
                weigh(c, *now)

        return 0

    lax.fori_loop(0, lax.div(steps + 1, jnp.int32(2)), two, 0)
    attended = summed[...] / jnp.sum(total[...], axis=0, keepdims=True)
    for h in range(heads):
        out[:, h * HEAD_SIZE : (h + 1) * HEAD_SIZE] = (
            attended[:, h * STRIDE : (h + 1) * STRIDE].T.astype(out.dtype)
        )


def attention(firsts, base, starts, keys, values, selected, ranks, hops, pad, heads):
    columns, rows = base.shape
    group = STRIDE // BLOCK
    length = keys.shape[0]
    whole = lambda shape: pl.BlockSpec(shape, lambda j, *_: (0,) * len(shape))
    return pl.pallas_call(
        functools.partial(attention_kernel, hops, len(ranks), pad, heads),
        out_shape=jax.ShapeDtypeStruct((rows, columns), jnp.bfloat16),
        grid_spec=pltpu.PrefetchScalarGridSpec(
            num_scalar_prefetch=1,
            grid=(rows // STRIDE,),
            in_specs=[
                pl.BlockSpec((columns, STRIDE), lambda j, *_: (0, j)),
                pl.BlockSpec((group, 1, BLOCK), lambda j, *_: (j, 0, 0)),
                whole(keys.shape),
                whole(values.shape),
                pl.BlockSpec((group,) + selected.shape[1:], lambda j, *_: (j, 0, 0)),
            ]
            + [whole(r.shape) for r in ranks],
            out_specs=pl.BlockSpec((STRIDE, columns), lambda j, *_: (j, 0)),
            scratch_shapes=[
                pltpu.VMEM((CHUNK, heads * STRIDE), jnp.float32),
                pltpu.VMEM((CHUNK, heads * STRIDE), jnp.float32),
                pltpu.VMEM((8, heads * STRIDE), jnp.float32),
                pltpu.VMEM((8, heads * STRIDE), jnp.float32),
                pltpu.VMEM((1, heads * STRIDE), jnp.float32),
                pltpu.VMEM((8, heads * STRIDE), jnp.float32),
                pltpu.VMEM((HEAD_SIZE, heads * STRIDE), jnp.float32),
                pltpu.VMEM((HEAD_SIZE, heads * STRIDE), jnp.bfloat16),
            ],
        ),
        compiler_params=pltpu.CompilerParams(vmem_limit_bytes=40 * MIB),
        cost_estimate=pl.CostEstimate(
            flops=2 * rows * columns * length,
            bytes_accessed=8 * length * HEAD_SIZE,
            transcendentals=rows * heads * length,
        ),
        name="attention",
    )(firsts, base, starts, keys, values, selected, *ranks)


def per_device(
    mesh_shape,
    normed_input,
    query_weight,
    down_factors,
    up_factors,
    adapter_per_block,
    key_value_cache,
    token_segment,
):
    groups, tensor, stores = (mesh_shape[a] for a in ("groups", "tensor", "store"))
    rows = normed_input.shape[0]
    blocks = adapter_per_block.shape[0]
    heads = query_weight.shape[1] // HEAD_SIZE
    per_store = down_factors.shape[0]
    member = lax.axis_index("tensor")
    slots = slot_bound(stores, per_store, blocks)
    batches = slots // BATCH
    usual = min(batches, USUAL)
    more = min(batches, usual + MORE)
    hops = min(stores - 1, -(-(stores * rows // 2 - 1) // rows))
    share = min(tensor, max(1, GROUP // heads))
    exchange = tensor if blocks % tensor == 0 else 1
    raise_up = [(i, i + 1) for i in range(stores - 1)]
    raise_down = [(i + 1, i) for i in range(stores - 1)]
    pairs = lambda m: [(t, t ^ m) for t in range(tensor)]

    indices = [adapter_per_block] + [
        lax.ppermute(adapter_per_block, "store", [(i, (i + m) % stores) for i in range(stores)])
        for m in range(1, stores)
    ]
    down = jnp.swapaxes(down_factors, 1, 2)

    cache = jnp.swapaxes(key_value_cache, 0, 1)
    cache = lax.dynamic_index_in_dim(cache, member * heads // GROUP, 0, keepdims=False)
    numbers = token_segment.astype(cache.dtype).reshape(-1, cache.shape[1])
    numbers = jnp.pad(
        numbers, ((0, SEGMENT_ROWS - numbers.shape[0]), (0, 0)), constant_values=SEGMENTS
    )
    carried = rows // share + SEGMENT_ROWS
    plan = make_plan(indices, stores, blocks, per_store, slots)

    def fetch(first, last, ups, downs, plan, beside={}):
        ups, downs = list(ups), list(downs)
        for k in range(first, last):
            if k in beside:
                done = beside[k](ups)
                plan, done = lax.optimization_barrier((plan, done))
                found.append(done)
            along = (cache, numbers) if k == 0 else ()
            sent_up = pack(
                plan, down, up_factors, ups[:k], 0, slots, carried if k < hops else 0, along
            )
            plan, sent_up = lax.optimization_barrier((plan, sent_up))
            sent_down = pack(plan, down, up_factors, downs[:k], 1, slots)
            ups.append(lax.ppermute(sent_up, "store", raise_up))
            downs.append(lax.ppermute(sent_down, "store", raise_down))
        return ups, downs, plan

    def exchanged(ups):
        quarters = jnp.stack([up[up.shape[0] - carried :] for up in ups[:hops]])
        shares = [quarters]
        for m in range(1, share):
            bit = m & -m
            shares.append(lax.ppermute(shares[m ^ bit], "tensor", pairs(bit)))
        return shares

    found = []
    beside = {1: lambda ups: base_queries(normed_input, query_weight)}
    early = hops < usual - 1
    if early:
        beside[hops + 1] = exchanged
    ups, downs, plan = fetch(0, usual, [], [], plan, beside)
    base = found[0]
    pieces = found[1] if early else exchanged(ups)
    keys, values, starts, firsts = window(
        pieces, cache, token_segment.reshape(-1, BLOCK), hops, share, CHUNK
    )
    former = usual - 1
    earlier_parts = low_rank_parts(
        plan, normed_input, down, up_factors, ups[:former], downs[:former], slots, exchange, blocks
    )

    plan, *_ = lax.optimization_barrier((plan, keys, values, starts, firsts))

    def low_rank(ups, downs, plan):
        return tuple(
            low_rank_parts(
                plan,
                normed_input,
                down,
                up_factors,
                ups,
                downs,
                slots,
                exchange,
                blocks,
                former * BATCH,
                earlier_parts,
            )
        )

    def finish(parts, selected):
        if exchange > 1:
            total = parts[0]
            for m in range(1, tensor):
                total = total + lax.ppermute(parts[m], "tensor", pairs(m))
            total = total.astype(jnp.bfloat16)
            low = [total] + [lax.ppermute(total, "tensor", pairs(m)) for m in range(1, tensor)]
        else:
            low = [lax.psum(parts[0], "tensor").astype(jnp.bfloat16)]
        return attention(firsts, base, starts, keys, values, selected, low, hops, CHUNK, heads)

    def with_more(ups, downs, plan):
        return low_rank(*fetch(usual, more, ups, downs, plan))

    def with_all(ups, downs, plan, usually):
        *parts, selected = low_rank(*fetch(usual, batches, ups, downs, plan))
        return finish(parts, selected)

    *parts, selected = lax.cond(plan[0] > usual * BATCH, with_more, low_rank, ups, downs, plan)
    usually = finish(parts, selected)
    if more == batches:
        return usually
    return lax.cond(
        plan[0] > more * BATCH,
        with_all,
        lambda ups, downs, plan, usually: usually,
        ups,
        downs,
        plan,
        usually,
    )


def solution(mesh):
    return jax.shard_map(
        functools.partial(per_device, dict(mesh.shape)),
        mesh=mesh,
        in_specs=(
            P(("groups", "store"), None),
            P(None, "tensor"),
            P("store", "tensor", None),
            P("store", None, "tensor"),
            P(("groups", "store")),
            P(("groups", "store"), None, None),
            P(("groups", "store")),
        ),
        out_specs=P(("groups", "store"), "tensor"),
        check_vma=False,
    )
```

```python
import functools
import math

import jax
import jax.numpy as jnp
from jax import lax
from jax.experimental import pallas as pl
from jax.experimental.pallas import tpu as pltpu
from jax.sharding import PartitionSpec as P

HEAD_SIZE = 128
GROUP = 8
BLOCK = 128
ADAPTERS = 64
SEGMENTS = 4
SEGMENT_ROWS = 16
BATCH = 2
LAG = BATCH
USUAL = 4
MORE = 1
STRIDE = 2 * BLOCK
CHUNK = 512
MIB = 1 << 20
ANY = pl.BlockSpec(memory_space=pl.ANY)
SMEM = pl.BlockSpec(memory_space=pltpu.SMEM)
VMEM = pl.BlockSpec(memory_space=pltpu.VMEM)


def slot_bound(stores, per_store, blocks):
    load = max(
        min(per_store * (link + 1), blocks * (stores - 1 - link)) for link in range(stores - 1)
    )
    return -(-(load + (stores - 2) * LAG) // BATCH) * BATCH


def plan_kernel(stores, blocks, per_store, slots, *refs):
    index_refs = refs[:stores]
    plan, names, place, listed, far, when = refs[stores:]
    capacity = per_store + 1
    unused = 1 + 2 * slots + blocks
    my_store = lax.axis_index("store")
    zero = jnp.int32(0)
    for shift in range(stores):
        origin = lax.rem(my_store + stores - shift, stores)
        for b in range(blocks):
            names[origin * blocks + b] = index_refs[shift][b]
    for i in range(2 * ADAPTERS):
        place[i] = jnp.int32(-1)
    for i in range(2 * slots):
        plan[1 + i] = zero
    most = zero
    for way in range(2):
        mine = my_store if way == 0 else stores - 1 - my_store
        count = [zero] * stores
        crossing = [[zero] * stores for _ in range(stores)]
        for dest in range(stores - 1, 0, -1):
            real = dest if way == 0 else stores - 1 - dest
            for b in range(blocks):
                name = names[real * blocks + b]
                owner = lax.div(name, jnp.int32(per_store))
                if way == 1:
                    owner = stores - 1 - owner
                held = place[way * ADAPTERS + name]
                new = (owner < dest) & (held < 0)
                at = zero
                for o in range(stores):
                    at = jnp.where(owner == o, count[o], at)
                listed[(way * stores + owner) * capacity + at] = name
                far[(way * stores + owner) * capacity + at] = jnp.int32(dest)
                place[way * ADAPTERS + name] = jnp.where(new, at, held)
                step = new.astype(jnp.int32)
                for o in range(dest):
                    count[o] = count[o] + jnp.where(owner == o, step, 0)
            for o in range(dest):
                crossing[o][dest - 1] = count[o]
        for link in range(stores - 1):
            number = [crossing[o][link] for o in range(link + 1)]

            def fill(carry):
                t, left, *heads = carry
                best, chosen, row = jnp.int32(-1), zero, zero
                for o in range(link, -1, -1):
                    spot = (way * stores + o) * capacity + heads[o]
                    ready = heads[o] < number[o]
                    if o < link:
                        former = ((way * stores + link - 1) * stores + o) * capacity + heads[o]
                        ready = ready & (when[former] + LAG <= t)
                    goes = jnp.where(ready, far[spot], -1)
                    better = goes > best
                    best = jnp.where(better, goes, best)
                    chosen = jnp.where(better, o, chosen)
                    row = jnp.where(better, heads[o], row)
                found = best >= 0
                before = ((way * stores + max(link - 1, 0)) * stores + chosen) * capacity + row
                source = jnp.where(
                    chosen == link,
                    listed[(way * stores + chosen) * capacity + row] - my_store * per_store,
                    per_store + way * slots + when[before],
                )
                plan[jnp.where(found & (mine == link), 1 + way * slots + t, unused)] = source
                now = ((way * stores + link) * stores + chosen) * capacity + row
                when[jnp.where(found, now, when.shape[0] - 1)] = t
                step = found.astype(jnp.int32)
                heads = [heads[o] + jnp.where(chosen == o, step, 0) for o in range(link + 1)]
                return (t + 1, left - step, *heads)

            last, *_ = lax.while_loop(
                lambda carry: carry[1] > 0, fill, (zero, sum(number), *([zero] * (link + 1)))
            )
            most = jnp.maximum(most, last)
    plan[0] = most
    for b in range(blocks):
        name = names[my_store * blocks + b]
        owner = lax.div(name, jnp.int32(per_store))
        source = name - my_store * per_store
        for way in range(2):
            mine = my_store if way == 0 else stores - 1 - my_store
            origin = owner if way == 0 else stores - 1 - owner
            comes = origin < mine
            row = jnp.maximum(place[way * ADAPTERS + name], 0)
            spot = ((way * stores + jnp.maximum(mine - 1, 0)) * stores + origin) * capacity + row
            arrives = per_store + way * slots + when[jnp.where(comes, spot, 0)]
            source = jnp.where(comes, arrives, source)
        plan[1 + 2 * slots + b] = source


def make_plan(indices, stores, blocks, per_store, slots):
    lists = 2 * stores * (per_store + 1)
    return pl.pallas_call(
        functools.partial(plan_kernel, stores, blocks, per_store, slots),
        out_shape=jax.ShapeDtypeStruct((2 + 2 * slots + blocks,), jnp.int32),
        in_specs=[SMEM] * len(indices),
        out_specs=SMEM,
        scratch_shapes=[
            pltpu.SMEM((stores * blocks,), jnp.int32),
            pltpu.SMEM((2 * ADAPTERS,), jnp.int32),
            pltpu.SMEM((lists,), jnp.int32),
            pltpu.SMEM((lists,), jnp.int32),
            pltpu.SMEM((lists * stores + 1,), jnp.int32),
        ],
        name="plan",
    )(*indices)


def adapter_rows(down, up):
    return down.shape[1] * (down.shape[2] // up.shape[2] + 1)


def adapter_moves(down, up, item, sem, into_item):
    rank, width = down.shape
    columns = up.shape[1]
    moves = []
    for c in range(width // columns + 1):
        rows = item.at[pl.ds(c * rank, rank)]
        factor = up if c == width // columns else down.at[:, pl.ds(c * columns, columns)]
        source, target = (factor, rows) if into_item else (rows, factor)
        moves.append(pltpu.make_async_copy(source, target, sem))
    return moves


def pack_kernel(slots, per_store, way, batch, carried, plan, down, up, *refs):
    if carried and batch == 0:
        cache, numbers = refs[:2]
        refs = refs[2:]
    got = refs[:batch]
    out, sems = refs[batch:]
    size = adapter_rows(down, up)
    along = []
    if carried and batch == 0:
        part = carried - SEGMENT_ROWS
        member = lax.rem(lax.axis_index("tensor"), cache.shape[0] // part)
        along = [
            (cache.at[pl.ds(pl.multiple_of(member * part, part), part)], 0, part),
            (numbers, part, SEGMENT_ROWS),
        ]
    elif carried:
        along = [(got[batch - 1].at[pl.ds(BATCH * size, carried)], 0, carried)]
    along = [
        pltpu.make_async_copy(source, out.at[pl.ds(BATCH * size + at, rows)], sems.at[BATCH])
        for source, at, rows in along
    ]

    def copies(i):
        source = plan[1 + way * slots + batch * BATCH + i]
        own = jnp.minimum(source, per_store - 1)
        item = out.at[pl.ds(i * size, size)]
        pairs = [
            (
                source < per_store,
                adapter_moves(down.at[own], up.at[own], item, sems.at[i], True),
            )
        ]
        for j in range(batch * BATCH):
            held = got[j // BATCH].at[pl.ds(j % BATCH * size, size)]
            pairs.append(
                (
                    source == per_store + way * slots + j,
                    [pltpu.make_async_copy(held, item, sems.at[i])],
                )
            )
        return pairs

    for act in ("start", "wait"):
        for i in range(BATCH):
            for chosen, moves in copies(i):

                @pl.when(chosen)
                def _():
                    for move in moves:
                        getattr(move, act)()

        for move in along:
            getattr(move, act)()


def pack(plan, down, up, got, way, slots, carried=0, along=()):
    rows = BATCH * adapter_rows(down, up) + carried
    return pl.pallas_call(
        functools.partial(pack_kernel, slots, down.shape[0], way, len(got), carried),
        out_shape=jax.ShapeDtypeStruct((rows, up.shape[2]), down.dtype),
        in_specs=[SMEM] + [ANY] * (2 + len(along) + len(got)),
        out_specs=VMEM,
        scratch_shapes=[pltpu.SemaphoreType.DMA((BATCH + 1,))],
        compiler_params=pltpu.CompilerParams(vmem_limit_bytes=(16 if got else 60) * MIB),
        cost_estimate=pl.CostEstimate(
            flops=5 * 10**8, bytes_accessed=4 * rows * up.shape[2], transcendentals=0
        ),
        name="pack",
    )(plan, down, up, *along, *got)


def low_rank_kernel(slots, per_store, former, received, tensor, plan, x, down, up, *refs):
    earlier = refs[: tensor + 1] if former is not None else ()
    refs = refs[len(earlier) :]
    number = 2 * received // BATCH
    got = refs[:number]
    outs = refs[number : number + tensor]
    selected, x_rows, factors, sems = refs[number + tensor :]
    blocks, rank, width = factors.shape
    share = blocks // tensor
    member = lax.axis_index("tensor")
    columns = pl.ds(pl.multiple_of(member * width, 128), width)
    if tensor == 1:
        member = 0

    size = adapter_rows(down, up)

    def within(source, number):
        return (source < per_store + number) | (
            (source >= per_store + slots) & (source < per_store + slots + number)
        )

    def due(b):
        source = plan[1 + 2 * slots + b]
        if former is None:
            return within(source, received)
        return jnp.logical_not(within(source, former))

    def copies(b):
        source = plan[1 + 2 * slots + b]
        source = jnp.where(within(source, received), source, 0)
        own = jnp.minimum(source, per_store - 1)
        pairs = [
            (
                source < per_store,
                [
                    pltpu.make_async_copy(down.at[own], factors.at[b], sems.at[b]),
                    pltpu.make_async_copy(up.at[own], selected.at[b], sems.at[b]),
                ],
            )
        ]
        for j in range(2 * received):
            spot = j if j < received else slots + j - received
            item = got[j // BATCH].at[pl.ds(j % BATCH * size, size)]
            pairs.append(
                (
                    source == per_store + spot,
                    adapter_moves(factors.at[b], selected.at[b], item, sems.at[b], False),
                )
            )
        return pairs

    def rows_of(b):
        rows = pl.ds(pl.multiple_of(b * BLOCK, BLOCK), BLOCK)
        return pltpu.make_async_copy(x.at[rows, columns], x_rows.at[b], sems.at[blocks + b])

    if former is not None:
        selected[...] = earlier[tensor][...]
    else:
        selected[...] = jnp.zeros_like(selected)

    def start(b, _):
        @pl.when(due(b))
        def _():
            rows_of(b).start()
            for chosen, moves in copies(b):

                @pl.when(chosen)
                def _():
                    for move in moves:
                        move.start()

        return 0

    lax.fori_loop(0, blocks, start, 0)
    for m in range(tensor):
        for i in range(share):
            b = (member ^ m) * share + i
            wanted = due(b)

            @pl.when(wanted)
            def _():
                pltpu.make_async_copy(down.at[0], factors.at[b], sems.at[b]).wait()
                pltpu.make_async_copy(up.at[0], selected.at[b], sems.at[b]).wait()
                rows_of(b).wait()
                outs[m][i] = lax.dot_general(
                    x_rows[b],
                    factors[b],
                    (((1,), (1,)), ((), ())),
                    preferred_element_type=jnp.float32,
                ).T

            @pl.when(jnp.logical_not(wanted))
            def _():
                if former is not None:
                    outs[m][i] = earlier[m][i]
                else:
                    outs[m][i] = jnp.zeros(outs[m].shape[1:], jnp.float32)


def low_rank_parts(plan, x, down, up, ups, downs, slots, tensor, blocks, former=None, earlier=()):
    per_store, rank, width = down.shape
    share = blocks // tensor
    return pl.pallas_call(
        functools.partial(
            low_rank_kernel, slots, per_store, former, BATCH * len(ups), tensor
        ),
        out_shape=[jax.ShapeDtypeStruct((share, rank, BLOCK), jnp.float32)] * tensor
        + [jax.ShapeDtypeStruct((blocks, rank, up.shape[2]), up.dtype)],
        in_specs=[SMEM] + [ANY] * 3 + [VMEM] * len(earlier) + [ANY] * (2 * len(ups)),
        out_specs=[VMEM] * (tensor + 1),
        scratch_shapes=[
            pltpu.VMEM((blocks, BLOCK, width), x.dtype),
            pltpu.VMEM((blocks, rank, width), down.dtype),
            pltpu.SemaphoreType.DMA((2 * blocks,)),
        ],
        compiler_params=pltpu.CompilerParams(vmem_limit_bytes=50 * MIB),
        cost_estimate=pl.CostEstimate(
            flops=6 * 10**9,
            bytes_accessed=2 * blocks * width * (BLOCK + rank),
            transcendentals=0,
        ),
        name="low_rank",
    )(plan, x, down, up, *earlier, *ups, *downs)


def window_kernel(hops, share, pad, *refs):
    pieces = refs[:share]
    own, segments, keys, values, starts, firsts, buffer, others, sems = refs[share:]
    rows = own.shape[0]
    part = rows // share
    blocks = rows // BLOCK
    member = lax.rem(lax.axis_index("tensor"), share)
    store = lax.axis_index("store")
    moves = [
        pltpu.make_async_copy(own, buffer.at[pl.ds(hops * rows, rows)], sems.at[hops * share])
    ]
    for hop in range(hops):
        for m in range(share):
            at = pl.multiple_of((hops - 1 - hop) * rows + (member ^ m) * part, part)
            moves.append(
                pltpu.make_async_copy(
                    pieces[m].at[hop, pl.ds(0, part)],
                    buffer.at[pl.ds(at, part)],
                    sems.at[hop * share + m],
                )
            )
        moves.append(
            pltpu.make_async_copy(
                pieces[0].at[hop, pl.ds(part, SEGMENT_ROWS)],
                others.at[hop],
                sems.at[hops * share + 1 + hop],
            )
        )
    for move in moves:
        move.start()
    empty = jnp.maximum(hops - store, 0) * rows
    names = segments[...]
    for move in moves:
        move.wait()
    start = jnp.zeros(names.shape, jnp.int32) + empty
    for value in range(1, SEGMENTS):
        before = empty.astype(jnp.float32)
        before = before + jnp.sum((names < value).astype(jnp.float32))
        for hop in range(hops):
            below = (others[hop].astype(jnp.float32) < value).astype(jnp.float32)
            before = before + jnp.where(hop < store, jnp.sum(below), 0.0)
        start = jnp.where(names == value, before.astype(jnp.int32), start)
    starts[...] = start.reshape(starts.shape)
    for j in range(blocks):
        firsts[j] = jnp.min(start[j : j + 1].astype(jnp.float32)).astype(jnp.int32)
    keys[pl.ds(0, pad), :] = jnp.zeros((pad, HEAD_SIZE), keys.dtype)
    values[:, pl.ds(0, pad)] = jnp.zeros((HEAD_SIZE, pad), values.dtype)

    def turn(c, _):
        at = pl.ds(pl.multiple_of(c * 256, 256), 256)
        to = pl.ds(pl.multiple_of(pad + c * 256, 256), 256)
        keys[to, :] = buffer[at, pl.ds(0, HEAD_SIZE)]
        values[:, to] = buffer[at, pl.ds(HEAD_SIZE, HEAD_SIZE)].astype(jnp.float32).T.astype(
            values.dtype
        )
        return 0

    lax.fori_loop(0, (hops + 1) * rows // 256, turn, 0)


def window(pieces, own, segments, hops, share, pad):
    rows = own.shape[0]
    length = pad + (hops + 1) * rows
    return pl.pallas_call(
        functools.partial(window_kernel, hops, share, pad),
        out_shape=[
            jax.ShapeDtypeStruct((length, HEAD_SIZE), own.dtype),
            jax.ShapeDtypeStruct((HEAD_SIZE, length), own.dtype),
            jax.ShapeDtypeStruct((rows // BLOCK, 1, BLOCK), jnp.int32),
            jax.ShapeDtypeStruct((rows // BLOCK,), jnp.int32),
        ],
        in_specs=[ANY] * (len(pieces) + 1) + [VMEM],
        out_specs=[VMEM, VMEM, VMEM, SMEM],
        scratch_shapes=[
            pltpu.VMEM(((hops + 1) * rows, 2 * HEAD_SIZE), own.dtype),
            pltpu.VMEM((hops, SEGMENT_ROWS, own.shape[1]), own.dtype),
            pltpu.SemaphoreType.DMA((hops * share + 1 + hops,)),
        ],
        compiler_params=pltpu.CompilerParams(vmem_limit_bytes=24 * MIB),
        cost_estimate=pl.CostEstimate(
            flops=0, bytes_accessed=8 * length * HEAD_SIZE, transcendentals=0
        ),
        name="window",
    )(*pieces, own, segments)


def base_kernel(x, weight, out, total):
    k = pl.program_id(0)
    product = jnp.dot(x[...], weight[...], preferred_element_type=jnp.float32)

    @pl.when(k == 0)
    def _():
        total[...] = product

    @pl.when(k > 0)
    def _():
        total[...] += product

    @pl.when(k == pl.num_programs(0) - 1)
    def _():
        out[...] = total[...].T


def base_queries(x, weight):
    rows, width = x.shape
    columns = weight.shape[1]
    deep = min(width, 1024)
    return pl.pallas_call(
        base_kernel,
        out_shape=jax.ShapeDtypeStruct((columns, rows), jnp.float32),
        grid=(width // deep,),
        in_specs=[
            pl.BlockSpec((rows, deep), lambda k: (0, k)),
            pl.BlockSpec((deep, columns), lambda k: (k, 0)),
        ],
        out_specs=pl.BlockSpec((columns, rows), lambda k: (0, 0)),
        scratch_shapes=[pltpu.VMEM((rows, columns), jnp.float32)],
        compiler_params=pltpu.CompilerParams(vmem_limit_bytes=60 * MIB),
        cost_estimate=pl.CostEstimate(
            flops=2 * rows * width * columns,
            bytes_accessed=2 * width * (rows + columns),
            transcendentals=0,
        ),
        name="base",
    )(x, weight)


def attention_kernel(
    hops, tensor, pad, heads, firsts, base, starts, keys, values, selected, *refs
):
    ranks = refs[:tensor]
    out, even, odd, even_largest, odd_largest, top, total, summed, queries = refs[tensor:]
    j = pl.program_id(0)
    share = ranks[0].shape[0]
    member = lax.axis_index("tensor") if tensor > 1 else 0
    rows = (keys.shape[0] - pad) // (hops + 1)
    for t in range(STRIDE // BLOCK):
        block = j * (STRIDE // BLOCK) + t
        low = jnp.zeros(ranks[0].shape[1:], jnp.bfloat16)
        for m in range(tensor):
            for i in range(share):
                low = jnp.where(block == (member ^ m) * share + i, ranks[m][i], low)
        term = lax.dot_general(
            selected[t], low, (((0,), (0,)), ((), ())), preferred_element_type=jnp.float32
        )
        turned = (base[:, t * BLOCK : (t + 1) * BLOCK] + term).astype(jnp.bfloat16)
        for h in range(heads):
            queries[:, h * STRIDE + t * BLOCK : h * STRIDE + (t + 1) * BLOCK] = turned[
                h * HEAD_SIZE : (h + 1) * HEAD_SIZE
            ]
    q = queries[...]
    columns = heads * STRIDE
    start = jnp.concatenate([starts[t] for t in range(STRIDE // BLOCK)] * heads, axis=1) + pad
    end = pad + hops * rows + (j + 1) * STRIDE
    steps = lax.div(
        end - pad - firsts[j * (STRIDE // BLOCK)] + CHUNK - 1, jnp.int32(CHUNK)
    )
    scale = HEAD_SIZE**-0.5 * math.log2(math.e)
    key = lax.broadcasted_iota(jnp.int32, (CHUNK, columns), 0)

    def place_of(c):
        return pl.multiple_of(jnp.maximum(end - (c + 1) * CHUNK, 0), BLOCK)

    def score(c, buffer, largest, diagonal):
        at = place_of(c)
        s = jnp.dot(keys[pl.ds(at, CHUNK), :], q, preferred_element_type=jnp.float32)
        allowed = key >= start - at
        if diagonal:
            token = lax.rem(lax.broadcasted_iota(jnp.int32, (1, columns), 1), STRIDE)
            allowed = allowed & (key <= token + (CHUNK - STRIDE))
        s = jnp.where(allowed, s, jnp.float32(-1e30))
        buffer[...] = s
        largest[...] = jnp.max(s.reshape(CHUNK // 8, 8, columns), axis=0)

    def weigh(c, buffer, largest):
        before = top[...]
        now = jnp.maximum(before, jnp.max(largest[...], axis=0, keepdims=True))
        top[...] = now
        fade = jnp.exp2((before - now) * scale)
        w = jnp.exp2((buffer[...] - now) * scale)
        total[...] = total[...] * fade + jnp.sum(w.reshape(CHUNK // 8, 8, columns), axis=0)
        summed[...] = summed[...] * fade + jnp.dot(
            values[:, pl.ds(place_of(c), CHUNK)],
            w.astype(jnp.bfloat16),
            preferred_element_type=jnp.float32,
        )

    top[...] = jnp.full(top.shape, -1e30, jnp.float32)
    total[...] = jnp.zeros(total.shape, jnp.float32)
    summed[...] = jnp.zeros(summed.shape, jnp.float32)
    even, odd = (even, even_largest), (odd, odd_largest)
    score(0, *even, True)

    def two(i, _):
        for c, now, after in ((2 * i, even, odd), (2 * i + 1, odd, even)):

            @pl.when(c + 1 < steps)
            def _():
                score(c + 1, *after, False)
                weigh(c, *now)

            @pl.when(c + 1 == steps)
            def _():
                weigh(c, *now)

        return 0

    lax.fori_loop(0, lax.div(steps + 1, jnp.int32(2)), two, 0)
    attended = summed[...] / jnp.sum(total[...], axis=0, keepdims=True)
    for h in range(heads):
        out[:, h * HEAD_SIZE : (h + 1) * HEAD_SIZE] = (
            attended[:, h * STRIDE : (h + 1) * STRIDE].T.astype(out.dtype)
        )


def attention(firsts, base, starts, keys, values, selected, ranks, hops, pad, heads):
    columns, rows = base.shape
    group = STRIDE // BLOCK
    length = keys.shape[0]
    whole = lambda shape: pl.BlockSpec(shape, lambda j, *_: (0,) * len(shape))
    return pl.pallas_call(
        functools.partial(attention_kernel, hops, len(ranks), pad, heads),
        out_shape=jax.ShapeDtypeStruct((rows, columns), jnp.bfloat16),
        grid_spec=pltpu.PrefetchScalarGridSpec(
            num_scalar_prefetch=1,
            grid=(rows // STRIDE,),
            in_specs=[
                pl.BlockSpec((columns, STRIDE), lambda j, *_: (0, j)),
                pl.BlockSpec((group, 1, BLOCK), lambda j, *_: (j, 0, 0)),
                whole(keys.shape),
                whole(values.shape),
                pl.BlockSpec((group,) + selected.shape[1:], lambda j, *_: (j, 0, 0)),
            ]
            + [whole(r.shape) for r in ranks],
            out_specs=pl.BlockSpec((STRIDE, columns), lambda j, *_: (j, 0)),
            scratch_shapes=[
                pltpu.VMEM((CHUNK, heads * STRIDE), jnp.float32),
                pltpu.VMEM((CHUNK, heads * STRIDE), jnp.float32),
                pltpu.VMEM((8, heads * STRIDE), jnp.float32),
                pltpu.VMEM((8, heads * STRIDE), jnp.float32),
                pltpu.VMEM((1, heads * STRIDE), jnp.float32),
                pltpu.VMEM((8, heads * STRIDE), jnp.float32),
                pltpu.VMEM((HEAD_SIZE, heads * STRIDE), jnp.float32),
                pltpu.VMEM((HEAD_SIZE, heads * STRIDE), jnp.bfloat16),
            ],
        ),
        compiler_params=pltpu.CompilerParams(vmem_limit_bytes=40 * MIB),
        cost_estimate=pl.CostEstimate(
            flops=2 * rows * columns * length,
            bytes_accessed=8 * length * HEAD_SIZE,
            transcendentals=rows * heads * length,
        ),
        name="attention",
    )(firsts, base, starts, keys, values, selected, *ranks)


def per_device(
    mesh_shape,
    normed_input,
    query_weight,
    down_factors,
    up_factors,
    adapter_per_block,
    key_value_cache,
    token_segment,
):
    groups, tensor, stores = (mesh_shape[a] for a in ("groups", "tensor", "store"))
    rows = normed_input.shape[0]
    blocks = adapter_per_block.shape[0]
    heads = query_weight.shape[1] // HEAD_SIZE
    per_store = down_factors.shape[0]
    member = lax.axis_index("tensor")
    slots = slot_bound(stores, per_store, blocks)
    batches = slots // BATCH
    usual = min(batches, USUAL)
    more = min(batches, usual + MORE)
    hops = min(stores - 1, -(-(stores * rows // 2 - 1) // rows))
    share = min(tensor, max(1, GROUP // heads))
    exchange = tensor if blocks % tensor == 0 else 1
    raise_up = [(i, i + 1) for i in range(stores - 1)]
    raise_down = [(i + 1, i) for i in range(stores - 1)]
    pairs = lambda m: [(t, t ^ m) for t in range(tensor)]

    indices = [adapter_per_block] + [
        lax.ppermute(adapter_per_block, "store", [(i, (i + m) % stores) for i in range(stores)])
        for m in range(1, stores)
    ]
    down = jnp.swapaxes(down_factors, 1, 2)

    cache = jnp.swapaxes(key_value_cache, 0, 1)
    cache = lax.dynamic_index_in_dim(cache, member * heads // GROUP, 0, keepdims=False)
    numbers = token_segment.astype(cache.dtype).reshape(-1, cache.shape[1])
    numbers = jnp.pad(
        numbers, ((0, SEGMENT_ROWS - numbers.shape[0]), (0, 0)), constant_values=SEGMENTS
    )
    carried = rows // share + SEGMENT_ROWS
    plan = make_plan(indices, stores, blocks, per_store, slots)

    def fetch(first, last, ups, downs, plan, beside={}):
        ups, downs = list(ups), list(downs)
        for k in range(first, last):
            if k in beside:
                done = beside[k](ups)
                plan, done = lax.optimization_barrier((plan, done))
                found.append(done)
            along = (cache, numbers) if k == 0 else ()
            sent_up = pack(
                plan, down, up_factors, ups[:k], 0, slots, carried if k < hops else 0, along
            )
            plan, sent_up = lax.optimization_barrier((plan, sent_up))
            sent_down = pack(plan, down, up_factors, downs[:k], 1, slots)
            ups.append(lax.ppermute(sent_up, "store", raise_up))
            downs.append(lax.ppermute(sent_down, "store", raise_down))
        return ups, downs, plan

    def exchanged(ups):
        quarters = jnp.stack([up[up.shape[0] - carried :] for up in ups[:hops]])
        shares = [quarters]
        for m in range(1, share):
            bit = m & -m
            shares.append(lax.ppermute(shares[m ^ bit], "tensor", pairs(bit)))
        return shares

    found = []
    beside = {1: lambda ups: base_queries(normed_input, query_weight)}
    early = hops < usual - 1
    if early:
        beside[hops + 1] = exchanged
    ups, downs, plan = fetch(0, usual, [], [], plan, beside)
    base = found[0]
    pieces = found[1] if early else exchanged(ups)
    keys, values, starts, firsts = window(
        pieces, cache, token_segment.reshape(-1, BLOCK), hops, share, CHUNK
    )
    former = usual - 1
    earlier_parts = low_rank_parts(
        plan, normed_input, down, up_factors, ups[:former], downs[:former], slots, exchange, blocks
    )

    plan, *_ = lax.optimization_barrier((plan, keys, values, starts, firsts))

    def low_rank(ups, downs, plan):
        return tuple(
            low_rank_parts(
                plan,
                normed_input,
                down,
                up_factors,
                ups,
                downs,
                slots,
                exchange,
                blocks,
                former * BATCH,
                earlier_parts,
            )
        )

    def finish(parts, selected):
        if exchange > 1:
            total = parts[0]
            for m in range(1, tensor):
                total = total + lax.ppermute(parts[m], "tensor", pairs(m))
            total = total.astype(jnp.bfloat16)
            low = [total] + [lax.ppermute(total, "tensor", pairs(m)) for m in range(1, tensor)]
        else:
            low = [lax.psum(parts[0], "tensor").astype(jnp.bfloat16)]
        return attention(firsts, base, starts, keys, values, selected, low, hops, CHUNK, heads)

    def with_more(ups, downs, plan):
        return low_rank(*fetch(usual, more, ups, downs, plan))

    def with_all(ups, downs, plan, usually):
        *parts, selected = low_rank(*fetch(usual, batches, ups, downs, plan))
        return finish(parts, selected)

    *parts, selected = lax.cond(plan[0] > usual * BATCH, with_more, low_rank, ups, downs, plan)
    usually = finish(parts, selected)
    if more == batches:
        return usually
    return lax.cond(
        plan[0] > more * BATCH,
        with_all,
        lambda ups, downs, plan, usually: usually,
        ups,
        downs,
        plan,
        usually,
    )


def solution(mesh):
    return jax.shard_map(
        functools.partial(per_device, dict(mesh.shape)),
        mesh=mesh,
        in_specs=(
            P(("groups", "store"), None),
            P(None, "tensor"),
            P("store", "tensor", None),
            P("store", None, "tensor"),
            P(("groups", "store")),
            P(("groups", "store"), None, None),
            P(("groups", "store")),
        ),
        out_specs=P(("groups", "store"), "tensor"),
        check_vma=False,
    )
```
